32 devices in a mesh: seq: 8 (over y, x, core), head: 4 (over z).
Axes of the slice: x: 2, y: 2, z: 4, core: 2. Of those that a mesh axis runs over, the one named last changes fastest.
Arguments:
- histories: bfloat16 [9, 4096, 2048], P(None, ('seq', 'head'))
- norm_gains: float32 [4, 2048], replicated, may hold values from 0.1 to 1.9
- mix_in: bfloat16 [2048, 40], replicated, may hold values from -0.125 to 0.125
- mix_out: bfloat16 [40, 36], replicated, may hold values from -0.3125 to 0.3125
- mix_bias: float32 [36], replicated, may hold values from -1.3 to 1.3
- w_query: bfloat16 [2048, 2048], P(None, 'head'), may hold values from -0.125 to 0.125
- w_key: bfloat16 [2048, 2048], P(None, 'head'), may hold values from -0.125 to 0.125
- w_value: bfloat16 [2048, 2048], P(None, 'head'), may hold values from -0.125 to 0.125
- w_out: bfloat16 [2048, 2048], P('head'), may hold values from -0.5 to 0.5
- w_up: bfloat16 [2048, 8192], P(None, 'head'), may hold values from -0.125 to 0.125
- w_down: bfloat16 [8192, 2048], P('head'), may hold values from -0.0625 to 0.0625
- cotangent: bfloat16 [4096, 2048], P(('seq', 'head')), may hold values from -6 to 6
- doc_ids: int32 [4096], replicated, may hold values from 0 to 2, as said below
- positions: int32 [4096], P('seq'), may hold values from 0 to 3583, as said below
Outputs:
- layer_out: bfloat16 [4096, 2048], P(('seq', 'head'))
- grad_histories: bfloat16 [9, 4096, 2048], P(None, ('seq', 'head'))
- grad_norm_gains: float32 [4, 2048], replicated
- grad_mix_in: float32 [2048, 40], replicated
- grad_mix_out: float32 [40, 36], replicated
- grad_mix_bias: float32 [36], replicated
- grad_w_query: float32 [2048, 2048], P(None, 'head')
- grad_w_key: float32 [2048, 2048], P(None, 'head')
- grad_w_value: float32 [2048, 2048], P(None, 'head')
- grad_w_out: float32 [2048, 2048], P('head')
- grad_w_up: float32 [2048, 8192], P(None, 'head')
- grad_w_down: float32 [8192, 2048], P('head')
The draws below stay inside these ranges and needn't reach their ends.
Inputs may be any that keep to these rules, and one draw needn't show every extreme that they name: `doc_ids`: three contiguous documents numbered 0, 1, 2 in order; document 0 has 1 to 511 tokens, document 2 has 512 minus that many, document 1 has 3584 tokens. `positions`: each token's offset from the first token of its document.
All inputs are finite; a program needn't handle non-finite values.
Results may differ from the reference program's by a relative error of at most 0.023.
Values may be sent and summed in bfloat16 or wider, within the bound.
No kernel may reach another device: no remote copies, remote signals or barrier semaphores. Data moves between devices by JAX's collectives and lax.ppermute only.
A program may use at most 256 MiB of HBM per device.

```python
import math
import jax
import jax.numpy as jnp
from jax import lax

D = 2048
FF = 8192
HEADS = 16
HD = 128
ROT = 32
MIX_HIDDEN = 40
HIST = 9
STREAMS = 4
TOK_BLK = 512
TOKENS = 4096


def draw_histories(key, part):
    base_key = jax.random.fold_in(key, 11)
    row_scale = jnp.exp(jax.random.uniform(jax.random.fold_in(base_key, 1), (HIST, TOKENS, 1), minval=math.log(0.3), maxval=math.log(3.0)))
    column_scale = jnp.exp(jax.random.uniform(jax.random.fold_in(base_key, 2), (HIST, 1, D), minval=math.log(0.6), maxval=math.log(1.6)))
    values = jax.random.normal(jax.random.fold_in(base_key, 3), (HIST, TOKENS, D)) * row_scale * column_scale
    return values.astype(jnp.float32).astype(jnp.bfloat16)


def document_layout(key):
    base_key = jax.random.fold_in(key, 29)
    head_length = jax.random.randint(jax.random.fold_in(base_key, 1), (), 1, TOK_BLK)
    tail_length = TOK_BLK - head_length
    token_index = jnp.arange(TOKENS, dtype=jnp.int32)
    tail_start = TOKENS - tail_length
    in_middle = jnp.where(token_index >= head_length, 1, 0)
    in_tail = jnp.where(token_index >= tail_start, 1, 0)
    ids = in_middle + in_tail
    starts = jnp.where(in_tail == 1, tail_start, jnp.where(in_middle == 1, head_length, 0))
    return (ids.astype(jnp.int32), (token_index - starts).astype(jnp.int32))


def draw_doc_ids(key, part):
    return document_layout(key)[0]


def draw_positions(key, part):
    return document_layout(key)[1]


def block_scale(stream_key, dims, pieces, low, largest):
    def one(axis_at, blocks):
        steps = jax.random.uniform(jax.random.fold_in(jax.random.fold_in(stream_key, 6), axis_at), (blocks,), jnp.float32, low / len(pieces), largest / len(pieces))
        return jnp.repeat(jnp.exp(steps), dims[axis_at] // blocks).reshape((-1,) + (1,) * (len(dims) - axis_at - 1))

    loudness = one(*pieces[0])
    for cut in pieces[1:]:
        loudness = loudness * one(*cut)
    return loudness


def gaussian(own_key, shape, deviation, bound, shards=(), held_as=jnp.bfloat16):
    entries = deviation * jax.random.normal(own_key, shape, jnp.float32)
    if shards:
        entries = entries * block_scale(own_key, shape, shards, -0.22, 0.18)
    return jnp.clip(entries, -bound, bound).astype(held_as)


def setup_inputs(seed: int = 0) -> dict:
    seeds = jax.random.split(jax.random.key(seed), 15)
    histories = draw_histories(jax.random.fold_in(seeds[14], 71), 0)
    norm_gains = jnp.clip(1.0 + 0.18 * jax.random.normal(seeds[1], (STREAMS, D), jnp.float32), 0.1, 1.9)
    mix_in = gaussian(seeds[2], (D, MIX_HIDDEN), D ** -0.5, 0.125)
    mix_out = gaussian(seeds[3], (MIX_HIDDEN, STREAMS * HIST), (MIX_HIDDEN * HIST) ** -0.5, 0.3125)
    mix_bias = gaussian(seeds[4], (STREAMS * HIST,), 0.33, 1.3, (), jnp.float32)
    w_query = gaussian(seeds[5], (D, D), D ** -0.5, 0.125, ((1, 4),))
    w_key = gaussian(seeds[6], (D, D), D ** -0.5, 0.125, ((1, 4),))
    w_value = gaussian(seeds[7], (D, D), D ** -0.5, 0.125, ((1, 4),))
    w_out = gaussian(seeds[8], (D, D), (D // 16) ** -0.5, 0.5, ((0, 4),))
    w_up = gaussian(seeds[9], (D, FF), D ** -0.5, 0.125, ((1, 4),))
    w_down = gaussian(seeds[10], (FF, D), FF ** -0.5, 0.0625, ((0, 4),))
    cotangent = gaussian(seeds[11], (TOKENS, D), 1.0, 6.0, ((0, 32),))
    doc_ids = draw_doc_ids(jax.random.fold_in(seeds[14], 71), 0)
    positions = draw_positions(jax.random.fold_in(seeds[14], 71), 0)
    return dict(histories=histories, norm_gains=norm_gains, mix_in=mix_in, mix_out=mix_out, mix_bias=mix_bias, w_query=w_query, w_key=w_key, w_value=w_value, w_out=w_out, w_up=w_up, w_down=w_down, cotangent=cotangent, doc_ids=doc_ids, positions=positions)


@jax.custom_vjp
def low(v):
    return lax.optimization_barrier(v.astype(jnp.bfloat16)).astype(jnp.float32)

@jax.custom_vjp
def low_back(v):
    return v

def low_keep(v):
    return (low(v), None)

def low_pass(kept, grad):
    return (grad,)

def back_keep(v):
    return (v, None)

def back_low(kept, grad):
    return (low(grad),)
low.defvjp(low_keep, low_pass)
low_back.defvjp(back_keep, back_low)
eps_norm = 1e-05
eps_rms = 1e-06
rope_base = 10000.0
hidden_mask = -1e+30

def matmul_hi(left_side, right_side):
    return jnp.dot(left_side, right_side, precision=lax.Precision.HIGHEST)

def layer_norm(values, gain_rows):
    centre = values - lax.optimization_barrier(jnp.mean(values, axis=-1, keepdims=True))
    spread = lax.optimization_barrier(jnp.mean(centre * centre, axis=-1, keepdims=True))
    return centre * lax.rsqrt(spread + eps_norm) * gain_rows

def rope_tables(positions):
    half_rot = ROT // 2
    frequency = rope_base ** (-(jnp.arange(half_rot, dtype=jnp.float32) * 2.0 / ROT))
    angles = positions.astype(jnp.float32)[:, None] * frequency[None, :]
    return (jnp.cos(angles)[:, None, :], jnp.sin(angles)[:, None, :])

def rotate(head_rows, cos_rows, sin_rows):
    half_rot = ROT // 2
    first_half = head_rows[..., :half_rot]
    second = head_rows[..., half_rot:ROT]
    return jnp.concatenate([first_half * cos_rows - second * sin_rows, second * cos_rows + first_half * sin_rows, head_rows[..., ROT:]], axis=-1)

def attention(query_heads, key_heads, value_heads, doc_ids):
    block_rows = min(512, TOKENS)
    score_scale = HD ** (-0.5)
    all_ids = doc_ids.astype(jnp.int32)
    offsets = jnp.arange(block_rows, dtype=jnp.int32)
    key_place = jnp.arange(TOKENS, dtype=jnp.int32)

    def one_block(row_start):
        query_rows = lax.dynamic_slice_in_dim(query_heads, row_start, block_rows, 0)
        query_ids = lax.dynamic_slice_in_dim(all_ids, row_start, block_rows, 0)
        visible = (query_ids[:, None] == all_ids[None, :]) & (key_place[None, :] <= (row_start + offsets)[:, None])
        scores = low_back(jnp.einsum('qhd,khd->hqk', query_rows, key_heads, precision=lax.Precision.HIGHEST) * score_scale)
        scores = jnp.where(visible[None], scores, hidden_mask)
        weights = low(jax.nn.softmax(scores, axis=-1))
        return jnp.einsum('hqk,khd->qhd', weights, value_heads, precision=lax.Precision.HIGHEST)
    starts = jnp.arange(TOKENS // block_rows, dtype=jnp.int32) * block_rows
    mixed_rows = lax.map(jax.checkpoint(one_block), starts)
    return mixed_rows.reshape(TOKENS, HEADS * HD)

def forward(histories, norm_gains, mix_in, mix_out, mix_bias, w_query, w_key, w_value, w_out, w_up, w_down, doc_ids, positions):
    newest = histories[HIST - 1]
    rms_last = newest * lax.rsqrt(lax.optimization_barrier(jnp.mean(newest * newest, axis=-1, keepdims=True)) + eps_rms)
    mix_hidden = low(jax.nn.gelu(matmul_hi(low(rms_last), mix_in), approximate=False))
    coefficient = (matmul_hi(mix_hidden, mix_out) + mix_bias).reshape(TOKENS, STREAMS, HIST)
    streams = jnp.einsum('tcj,jtd->tcd', coefficient, histories, precision=lax.Precision.HIGHEST)
    normed = low(layer_norm(streams, norm_gains[None, :, :]))
    query = matmul_hi(normed[:, 0], w_query)
    key_proj = matmul_hi(normed[:, 1], w_key)
    value_proj = matmul_hi(normed[:, 2], w_value)
    hidden_pre = low_back(matmul_hi(normed[:, 3], w_up))
    cos_rows, sin_rows = rope_tables(positions)
    query_heads = low(rotate(low_back(query).reshape(TOKENS, HEADS, HD), cos_rows, sin_rows))
    key_heads = low(rotate(low_back(key_proj).reshape(TOKENS, HEADS, HD), cos_rows, sin_rows))
    value_heads = low(low_back(value_proj)).reshape(TOKENS, HEADS, HD)
    attended = low(low_back(attention(query_heads, key_heads, value_heads, doc_ids)))
    activated = low(jax.nn.gelu(hidden_pre, approximate=False))
    return streams[:, 3] + matmul_hi(attended, w_out) + matmul_hi(activated, w_down)

def reference(histories, norm_gains, mix_in, mix_out, mix_bias, w_query, w_key, w_value, w_out, w_up, w_down, cotangent, doc_ids, positions):
    floats = tuple((operand.astype(jnp.float32) for operand in (histories, norm_gains, mix_in, mix_out, mix_bias, w_query, w_key, w_value, w_out, w_up, w_down)))

    def layer(*params):
        return forward(*params, doc_ids, positions)
    result, pullback = jax.vjp(layer, *floats)
    gradients = pullback(cotangent.astype(jnp.float32))
    return (result.astype(jnp.bfloat16), gradients[0].astype(jnp.bfloat16), gradients[1], gradients[2], gradients[3], gradients[4], gradients[5], gradients[6], gradients[7], gradients[8], gradients[9], gradients[10])
```

```python
import functools

import jax
import jax.numpy as jnp
from jax import lax
from jax.experimental import pallas as pl
from jax.experimental.pallas import tpu as pltpu
from jax.sharding import PartitionSpec as P

HD = 128
ROT = 32
HALF = ROT // 2
MIB = 1024 * 1024

eps_norm = 1e-05
eps_rms = 1e-06
rope_base = 10000.0
hidden_mask = -1e30
highest = lax.Precision.HIGHEST
f32 = jnp.float32
bf16 = jnp.bfloat16
sqrt_half = 0.7071067811865476
inv_sqrt_2pi = 0.3989422804014327
log2e = 1.4426950408889634


def vmem():
    return pl.BlockSpec(memory_space=pltpu.VMEM)


def params(mib, **more):
    return pltpu.CompilerParams(vmem_limit_bytes=mib * MIB, **more)


def cdf(x):
    return 0.5 * (1.0 + lax.erf(x * sqrt_half))


def pdf(x):
    return jnp.exp(x * x * -0.5) * inv_sqrt_2pi


def dot(a, b):
    return jnp.dot(a, b, preferred_element_type=f32)


def dot_nt(a, b):
    return lax.dot_general(a, b, (((1,), (1,)), ((), ())), preferred_element_type=f32)


def dot_tn(a, b):
    return lax.dot_general(a, b, (((0,), (0,)), ((), ())), preferred_element_type=f32)


def mix_kernel(tile, hist, gains, mix_in, mix_out, mix_bias, n3, nkv, nq, streams, coef, mix_pre):
    hist_count, rows, width = hist.shape
    count = gains.shape[0]
    newest = hist[hist_count - 1].astype(f32)
    scale = lax.rsqrt(jnp.mean(newest * newest, axis=-1, keepdims=True) + eps_rms)
    rms_low = (newest * scale).astype(bf16)
    pre = dot(rms_low, mix_in[...])
    mix_pre[...] = pre
    hidden = (pre * cdf(pre)).astype(bf16)
    coef[...] = dot(hidden, mix_out[...]) + mix_bias[...]
    chunk = 512

    def step(i, carry):
        at = pl.ds(pl.multiple_of(i * tile, tile), tile)
        rows_coef = coef[at, :]
        columns = [
            [rows_coef[:, c * hist_count + j : c * hist_count + j + 1] for j in range(hist_count)]
            for c in range(count)
        ]
        totals = [jnp.zeros((tile, 1), f32) for _ in range(count)]
        for lane in range(0, width, chunk):
            sums = [jnp.zeros((tile, chunk), f32) for _ in range(count)]
            for j in range(hist_count):
                h = hist[j, at, lane : lane + chunk].astype(f32)
                for c in range(count):
                    sums[c] = sums[c] + columns[c][j] * h
            for c in range(count):
                streams[c, at, lane : lane + chunk] = sums[c]
                totals[c] = totals[c] + jnp.sum(sums[c], axis=-1, keepdims=True)
        for c in range(count):
            x = streams[c, at, :]
            centre = x - totals[c] * (1.0 / width)
            spread = jnp.mean(centre * centre, axis=-1, keepdims=True)
            out = (centre * lax.rsqrt(spread + eps_norm) * gains[c : c + 1, :]).astype(bf16)
            if c == 0:
                nq[at, :] = out
            elif c == 3:
                n3[at, :] = out
            else:
                nkv[at, (c - 1) * width : c * width] = out
        return carry

    lax.fori_loop(0, rows // tile, step, 0)


def mix_forward(histories, norm_gains, mix_in, mix_out, mix_bias):
    hist_count, rows, width = histories.shape
    count = norm_gains.shape[0]
    return pl.pallas_call(
        functools.partial(mix_kernel, 16),
        out_shape=(
            jax.ShapeDtypeStruct((rows, width), bf16),
            jax.ShapeDtypeStruct((rows, 2 * width), bf16),
            jax.ShapeDtypeStruct((rows, width), bf16),
            jax.ShapeDtypeStruct((count, rows, width), f32),
            jax.ShapeDtypeStruct((rows, count * hist_count), f32),
            jax.ShapeDtypeStruct((rows, mix_in.shape[1]), f32),
        ),
        in_specs=[vmem()] * 5,
        out_specs=[vmem()] * 6,
        compiler_params=params(48),
        name="mix_forward",
    )(histories, norm_gains, mix_in, mix_out, mix_bias)


def unmix_kernel(
    hist, streams, gn3, gnkv, gnq, cot, coef, mix_pre, gains, mix_in, mix_out, ghist, pack, gs, rms_keep, hid_keep, gc_keep, gmp_keep
):
    hist_count, tile, width = hist.shape
    count = gains.shape[0]
    hidden_units = mix_in.shape[1]
    step = pl.program_id(0)

    @pl.when(step == 0)
    def _():
        pack[...] = jnp.zeros_like(pack)

    for c in range(count):
        x = streams[c]
        centre = x - jnp.mean(x, axis=-1, keepdims=True)
        inv = lax.rsqrt(jnp.mean(centre * centre, axis=-1, keepdims=True) + eps_norm)
        unit = centre * inv
        if c == 0:
            g = gnq[...].astype(f32)
        elif c == 3:
            g = gn3[...].astype(f32)
        else:
            g = gnkv[:, (c - 1) * width : c * width].astype(f32)
        pack[hidden_units + c : hidden_units + c + 1, 0:width] += jnp.sum(g * unit, axis=0, keepdims=True)
        d = g * gains[c : c + 1, :]
        out = inv * (
            d
            - jnp.mean(d, axis=-1, keepdims=True)
            - unit * jnp.mean(d * unit, axis=-1, keepdims=True)
        )
        if c == 3:
            out = out + cot[...].astype(f32)
        gs[c] = out
    lanes = lax.broadcasted_iota(jnp.int32, (tile, count * hist_count), 1)
    gc = jnp.zeros((tile, count * hist_count), f32)
    rows_coef = coef[...]
    for j in range(hist_count):
        h = hist[j].astype(f32)
        for c in range(count):
            k = c * hist_count + j
            gc = jnp.where(lanes == k, jnp.sum(gs[c] * h, axis=-1, keepdims=True), gc)
    for j in range(hist_count):
        total = rows_coef[:, j : j + 1] * gs[0]
        for c in range(1, count):
            k = c * hist_count + j
            total = total + rows_coef[:, k : k + 1] * gs[c]
        if j < hist_count - 1:
            ghist[j] = total.astype(bf16)
    pre = mix_pre[...]
    phi = cdf(pre)
    gmh = lax.dot_general(
        gc, mix_out[...].astype(f32), (((1,), (1,)), ((), ())), precision=highest
    )
    gmp = (phi + pre * pdf(pre)) * gmh
    gmp_low = gmp.astype(bf16)
    grad_rms = dot_nt(gmp_low, mix_in[...])
    newest = hist[hist_count - 1].astype(f32)
    scale = lax.rsqrt(jnp.mean(newest * newest, axis=-1, keepdims=True) + eps_rms)
    inner = jnp.mean(grad_rms * newest, axis=-1, keepdims=True)
    total = total + scale * grad_rms - newest * (scale * scale * scale * inner)
    ghist[hist_count - 1] = total.astype(bf16)
    at = pl.ds(pl.multiple_of(step * tile, tile), tile)
    rms_keep[at, :] = (newest * scale).astype(bf16)
    hid_keep[at, :] = (pre * phi).astype(bf16).astype(f32)
    gc_keep[at, :] = gc
    gmp_keep[at, :] = gmp_low

    @pl.when(step == pl.num_programs(0) - 1)
    def _():
        pack[0:hidden_units, 0:width] = dot_tn(gmp_keep[...], rms_keep[...])
        pack[0:hidden_units, width : width + count * hist_count] = lax.dot_general(
            hid_keep[...], gc_keep[...], (((0,), (0,)), ((), ())), precision=highest
        )
        pack[hidden_units : hidden_units + 1, width : width + count * hist_count] = jnp.sum(
            gc_keep[...], axis=0, keepdims=True
        )


def unmix(histories, streams, gn3, gnkv, gnq, cotangent, coef, mix_pre, norm_gains, mix_in, mix_out):
    hist_count, rows, width = histories.shape
    count = norm_gains.shape[0]
    units = mix_in.shape[1]
    mixes = count * hist_count
    tile = 16
    whole = lambda shape: pl.BlockSpec(shape, lambda i: (0, 0))
    return pl.pallas_call(
        unmix_kernel,
        grid=(rows // tile,),
        out_shape=(
            jax.ShapeDtypeStruct((hist_count, rows, width), bf16),
            jax.ShapeDtypeStruct((units + 8, width + 128), f32),
        ),
        in_specs=[
            pl.BlockSpec((hist_count, tile, width), lambda i: (0, i, 0)),
            pl.BlockSpec((count, tile, width), lambda i: (0, i, 0)),
            pl.BlockSpec((tile, width), lambda i: (i, 0)),
            pl.BlockSpec((tile, 2 * width), lambda i: (i, 0)),
            pl.BlockSpec((tile, width), lambda i: (i, 0)),
            pl.BlockSpec((tile, width), lambda i: (i, 0)),
            pl.BlockSpec((tile, mixes), lambda i: (i, 0)),
            pl.BlockSpec((tile, units), lambda i: (i, 0)),
            whole((count, width)),
            whole((width, units)),
            whole((units, mixes)),
        ],
        out_specs=[
            pl.BlockSpec((hist_count, tile, width), lambda i: (0, i, 0)),
            whole((units + 8, width + 128)),
        ],
        scratch_shapes=[
            pltpu.VMEM((count, tile, width), f32),
            pltpu.VMEM((rows, width), bf16),
            pltpu.VMEM((rows, units), f32),
            pltpu.VMEM((rows, mixes), f32),
            pltpu.VMEM((rows, units), bf16),
        ],
        compiler_params=params(48),
        name="unmix",
    )(histories, streams, gn3, gnkv, gnq, cotangent, coef, mix_pre, norm_gains, mix_in, mix_out)


def ff_kernel(n3, cot, w_up, w_down, ff_out, gn3, gw_up, gw_down, out_acc, gn_acc):
    step = pl.program_id(0)
    last = pl.num_programs(0) - 1
    pre = dot(n3[...], w_up[...])
    phi = cdf(pre)
    act = (pre * phi).astype(bf16)
    slope = phi + pre * pdf(pre)
    grad = (dot_nt(cot[...], w_down[...]) * slope).astype(bf16)
    gw_down[...] = dot_tn(act, cot[...]).astype(bf16)
    gw_up[...] = dot_tn(n3[...], grad).astype(bf16)
    part_out = dot(act, w_down[...])
    part_gn = dot_nt(grad, w_up[...])

    @pl.when(step == 0)
    def _():
        out_acc[...] = part_out
        gn_acc[...] = part_gn

    @pl.when(step > 0)
    def _():
        out_acc[...] += part_out
        gn_acc[...] += part_gn

    @pl.when(step == last)
    def _():
        ff_out[...] = out_acc[...]
        gn3[...] = gn_acc[...].astype(bf16)


def feed_forward(n3, cot, w_up, w_down):
    rows, width = n3.shape
    hidden = w_up.shape[1]
    block = min(512, hidden)
    fixed = pl.BlockSpec((rows, width), lambda i: (0, 0))
    return pl.pallas_call(
        ff_kernel,
        grid=(hidden // block,),
        out_shape=(
            jax.ShapeDtypeStruct((rows, width), f32),
            jax.ShapeDtypeStruct((rows, width), bf16),
            jax.ShapeDtypeStruct((width, hidden), bf16),
            jax.ShapeDtypeStruct((hidden, width), bf16),
        ),
        in_specs=[
            fixed,
            fixed,
            pl.BlockSpec((width, block), lambda i: (0, i)),
            pl.BlockSpec((block, width), lambda i: (i, 0)),
        ],
        out_specs=[
            fixed,
            fixed,
            pl.BlockSpec((width, block), lambda i: (0, i)),
            pl.BlockSpec((block, width), lambda i: (i, 0)),
        ],
        scratch_shapes=[pltpu.VMEM((rows, width), f32), pltpu.VMEM((rows, width), f32)],
        compiler_params=params(60),
        cost_estimate=pl.CostEstimate(
            flops=12 * rows * width * hidden, bytes_accessed=8 * width * hidden, transcendentals=0
        ),
        name="feed_forward",
    )(n3, cot, w_up, w_down)


def turn(x, same, down, up):
    return x * same + pltpu.roll(x, HD - HALF, 1) * down + pltpu.roll(x, HALF, 1) * up


def rotated(x, same, down, up):
    heads = [
        turn(x[:, h : h + HD], same, down, up).astype(bf16) for h in range(0, x.shape[1], HD)
    ]
    return jnp.concatenate(heads, axis=1)


def query_kernel(n, w, same, down, up, out):
    out[...] = rotated(dot(n[...], w[...]), same[...], down[...], up[...])


def key_value_kernel(n, wk, wv, same, down, up, key, value):
    width = wk.shape[0]
    key[...] = rotated(dot(n[:, 0:width], wk[...]), same[...], down[...], up[...])
    value[...] = dot(n[:, width : 2 * width], wv[...]).astype(bf16)


def project(kernel, n, weights, tables, outs, name):
    rows = n.shape[0]
    width, local = weights[0].shape
    block = min(256, rows)
    spec = lambda cols: pl.BlockSpec((block, cols), lambda i: (i, 0))
    return pl.pallas_call(
        kernel,
        grid=(rows // block,),
        out_shape=tuple(jax.ShapeDtypeStruct((rows, local), bf16) for _ in range(outs)),
        in_specs=[spec(n.shape[1])]
        + [pl.BlockSpec((width, local), lambda i: (0, 0))] * len(weights)
        + [spec(HD)] * 3,
        out_specs=tuple(spec(local) for _ in range(outs)),
        compiler_params=params(48),
        cost_estimate=pl.CostEstimate(
            flops=2 * rows * width * local * outs, bytes_accessed=8 * MIB, transcendentals=0
        ),
        name=name,
    )(n, *weights, *tables)


def rope_lanes(positions):
    frequency = rope_base ** (-(jnp.arange(HALF, dtype=f32) * 2.0 / ROT))
    angles = positions.astype(f32)[:, None] * frequency[None, :]
    cos, sin = jnp.cos(angles), jnp.sin(angles)
    rows = positions.shape[0]
    ones = jnp.ones((rows, HD - ROT), f32)
    zeros = jnp.zeros((rows, HD - HALF), f32)
    same = jnp.concatenate([cos, cos, ones], axis=1)
    down = jnp.concatenate([-sin, zeros], axis=1)
    up = jnp.concatenate([zeros[:, :HALF], sin, zeros[:, : HD - ROT]], axis=1)
    return (same, down, up)


def masked(scores, kb, block, first, last_seen):
    place = lax.broadcasted_iota(jnp.int32, scores.shape, 0) + kb * block
    seen = (place >= first) & (place <= last_seen)
    return jnp.where(seen, scores, hidden_mask)


def attend_kernel(scale2, info, kslot, vslot, q, k, v, span, out, lse, peak, total, acc):
    kb = pl.program_id(1)
    rank, reach = info[0], info[1]
    block = k.shape[0]

    @pl.when(kb == 0)
    def _():
        peak[...] = jnp.full_like(peak, hidden_mask)
        total[...] = jnp.zeros_like(total)
        acc[...] = jnp.zeros_like(acc)

    def update(scores):
        old = peak[...]
        new = jnp.maximum(old, jnp.max(scores, axis=0, keepdims=True))
        weights = jnp.exp2(scores - new)
        factor = jnp.exp2(old - new)
        peak[...] = new
        total[...] = total[...] * factor + jnp.sum(weights, axis=0, keepdims=True)
        acc[...] = acc[...] * factor + dot_tn(v[...], weights.astype(bf16))

    needs = (kb == rank) | (reach > kb * block)

    @pl.when((kb <= rank) & jnp.logical_not(needs))
    def _():
        update(dot_nt(k[...], q[...]) * scale2)

    @pl.when((kb <= rank) & needs)
    def _():
        scores = dot_nt(k[...], q[...]) * scale2
        update(masked(scores, kb, block, span[0:1, :], span[1:2, :]))

    @pl.when(kb == pl.num_programs(1) - 1)
    def _():
        out[...] = jnp.transpose(acc[...] / total[...]).astype(bf16)
        lse[...] = (peak[...] + jnp.log2(total[...]))[None]


def attend(q, k_all, v_all, info, kslot, vslot, span, blocks):
    rows, local = q.shape
    heads = local // HD
    block = k_all.shape[0] // blocks
    scale2 = HD ** (-0.5) * log2e
    grid_spec = pltpu.PrefetchScalarGridSpec(
        num_scalar_prefetch=3,
        grid=(heads, blocks),
        in_specs=[
            pl.BlockSpec((rows, HD), lambda h, b, info, ks, vs: (0, h)),
            pl.BlockSpec((block, HD), lambda h, b, info, ks, vs: (ks[jnp.minimum(b, info[0])], h)),
            pl.BlockSpec((block, HD), lambda h, b, info, ks, vs: (vs[jnp.minimum(b, info[0])], h)),
            pl.BlockSpec((8, rows), lambda h, b, info, ks, vs: (0, 0)),
        ],
        out_specs=[
            pl.BlockSpec((rows, HD), lambda h, b, info, ks, vs: (0, h)),
            pl.BlockSpec((1, 1, rows), lambda h, b, info, ks, vs: (h, 0, 0)),
        ],
        scratch_shapes=[
            pltpu.VMEM((1, rows), f32),
            pltpu.VMEM((1, rows), f32),
            pltpu.VMEM((HD, rows), f32),
        ],
    )
    return pl.pallas_call(
        functools.partial(attend_kernel, scale2),
        grid_spec=grid_spec,
        out_shape=(
            jax.ShapeDtypeStruct((rows, local), bf16),
            jax.ShapeDtypeStruct((heads, 1, rows), f32),
        ),
        compiler_params=params(32),
        cost_estimate=pl.CostEstimate(
            flops=8 * rows * block * blocks * local, bytes_accessed=8 * MIB, transcendentals=0
        ),
        name="attend",
    )(info, kslot, vslot, q, k_all, v_all, span)


def attend_back_kernel(
    scale, scale2, info, kslot, vslot, q, k, v, do, o, lse, span, same, down, up, gq, gk, gv, delta, acc
):
    kb = pl.program_id(1)
    rank, reach = info[0], info[1]
    block = k.shape[0]

    @pl.when(kb == 0)
    def _():
        both = do[...].astype(f32) * o[...].astype(f32)
        delta[...] = jnp.sum(jnp.transpose(both), axis=0, keepdims=True)
        acc[...] = jnp.zeros_like(acc)

    def update(scores):
        weights = jnp.exp2(scores - lse[0])
        gv[...] = dot(weights.astype(bf16), do[...]).astype(bf16)
        grad_weights = dot_nt(v[...], do[...])
        grad_scores = (weights * (grad_weights - delta[...])).astype(bf16)
        gk[...] = (dot(grad_scores, q[...]) * scale).astype(bf16)
        acc[...] += dot_tn(k[...], grad_scores)

    needs = (kb == rank) | (reach > kb * block)

    @pl.when((kb <= rank) & jnp.logical_not(needs))
    def _():
        update(dot_nt(k[...], q[...]) * scale2)

    @pl.when((kb <= rank) & needs)
    def _():
        scores = dot_nt(k[...], q[...]) * scale2
        update(masked(scores, kb, block, span[0:1, :], span[1:2, :]))

    @pl.when(kb > rank)
    def _():
        gk[...] = jnp.zeros_like(gk)
        gv[...] = jnp.zeros_like(gv)

    @pl.when(kb == pl.num_programs(1) - 1)
    def _():
        x = jnp.transpose(acc[...]) * scale
        gq[...] = turn(x, same[...], -down[...], -up[...]).astype(bf16)


def attend_back(q, k_all, v_all, do, o, lse, info, kslot, vslot, span, tables, blocks):
    rows, local = q.shape
    heads = local // HD
    block = k_all.shape[0] // blocks
    scale = HD ** (-0.5)
    at_query = pl.BlockSpec((rows, HD), lambda h, b, info, ks, vs: (0, h))
    table = pl.BlockSpec((rows, HD), lambda h, b, info, ks, vs: (0, 0))
    grid_spec = pltpu.PrefetchScalarGridSpec(
        num_scalar_prefetch=3,
        grid=(heads, blocks),
        in_specs=[
            at_query,
            pl.BlockSpec((block, HD), lambda h, b, info, ks, vs: (ks[jnp.minimum(b, info[0])], h)),
            pl.BlockSpec((block, HD), lambda h, b, info, ks, vs: (vs[jnp.minimum(b, info[0])], h)),
            at_query,
            at_query,
            pl.BlockSpec((1, 1, rows), lambda h, b, info, ks, vs: (h, 0, 0)),
            pl.BlockSpec((8, rows), lambda h, b, info, ks, vs: (0, 0)),
            table,
            table,
            table,
        ],
        out_specs=[
            at_query,
            pl.BlockSpec((block, HD), lambda h, b, info, ks, vs: (ks[b], h)),
            pl.BlockSpec((block, HD), lambda h, b, info, ks, vs: (vs[b], h)),
        ],
        scratch_shapes=[pltpu.VMEM((1, rows), f32), pltpu.VMEM((HD, rows), f32)],
    )
    return pl.pallas_call(
        functools.partial(attend_back_kernel, scale, scale * log2e),
        grid_spec=grid_spec,
        out_shape=(
            jax.ShapeDtypeStruct((rows, local), bf16),
            jax.ShapeDtypeStruct(k_all.shape, bf16),
            jax.ShapeDtypeStruct(v_all.shape, bf16),
        ),
        compiler_params=params(32),
        cost_estimate=pl.CostEstimate(
            flops=20 * rows * block * blocks * local, bytes_accessed=20 * MIB, transcendentals=0
        ),
        name="attend_back",
    )(info, kslot, vslot, q, k_all, v_all, do, o, lse, span, *tables)


def flipped(x, axis, bit):
    count = lax.axis_size(axis)
    return lax.ppermute(x, axis, [(i, i ^ bit) for i in range(count)])


def bits_of(count):
    bits = []
    while (1 << len(bits)) < count:
        bits.append(1 << len(bits))
    return bits


def slot_order(bits):
    order = [0]
    for bit in bits:
        order = order + [m | bit for m in order]
    return order


def slots_for(bits, rank, count):
    order = slot_order(bits)
    table = [0] * count
    for slot, m in enumerate(order):
        table[m] = slot
    return jnp.take(jnp.array(table, jnp.int32), jnp.arange(count, dtype=jnp.int32) ^ rank)


def collect(block, bits):
    pieces = [block]
    held = block
    for bit in bits:
        got = flipped(held, "seq", bit)
        pieces.append(got)
        held = jnp.concatenate([held, got], axis=0)
    return held


def summed(a, b):
    return (a.astype(f32) + b.astype(f32)).astype(bf16)


def disperse(parts, bits):
    held = parts
    for at, bit in enumerate(reversed(bits)):
        half = held.shape[0] // 2
        got = flipped(held[half:], "seq", bit)
        if at == len(bits) - 1:
            return held[:half].astype(f32) + got.astype(f32)
        held = summed(held[:half], got)
    return held.astype(f32)


def small_sum(x):
    x = x.astype(bf16)
    for axis in ("seq", "head"):
        for bit in bits_of(lax.axis_size(axis)):
            x = summed(x, flipped(x, axis, bit))
    return x.astype(f32)


def body(
    histories,
    norm_gains,
    mix_in,
    mix_out,
    mix_bias,
    w_query,
    w_key,
    w_value,
    w_out,
    w_up,
    w_down,
    cotangent,
    doc_ids,
    positions,
):
    seq_count = lax.axis_size("seq")
    rank = lax.axis_index("seq")
    block_rows = positions.shape[0]
    hist_count, tok_rows, width = histories.shape
    count = norm_gains.shape[0]
    units = mix_in.shape[1]
    mixes = mix_out.shape[1]

    def gather(x):
        return lax.all_gather(x, "head", axis=0, tiled=True)

    def scatter(x):
        return lax.psum_scatter(x, "head", scatter_dimension=0, tiled=True)

    tables = rope_lanes(positions)
    place = rank * block_rows + jnp.arange(block_rows, dtype=jnp.int32)
    first = place - positions
    span = jnp.concatenate([first[None], place[None], jnp.zeros((6, block_rows), jnp.int32)], axis=0)
    info = jnp.stack([rank.astype(jnp.int32), jnp.max(first)])
    bits = bits_of(seq_count)
    key_bits = bits[1:] + bits[:1]
    value_bits = bits[1:][::-1] + bits[:1]
    key_slots = slots_for(key_bits, rank, seq_count)
    value_slots = slots_for(value_bits, rank, seq_count)

    cot_full = gather(cotangent)
    n3, nkv, nq, streams, coef, mix_pre = mix_forward(
        histories, norm_gains, mix_in, mix_out, mix_bias[None, :]
    )
    n3_full = gather(n3)
    nkv_full = gather(nkv)
    nq_full = gather(nq)
    ff_out, gn3_part, gw_up, gw_down = feed_forward(n3_full, cot_full, w_up, w_down)
    gn3 = scatter(gn3_part)
    key, value = project(key_value_kernel, nkv_full, (w_key, w_value), tables, 2, "project_kv")
    (query,) = project(query_kernel, nq_full, (w_query,), tables, 1, "project_q")
    k_all = collect(key, key_bits)
    v_all = collect(value, value_bits)
    attended, lse = attend(query, k_all, v_all, info, key_slots, value_slots, span, seq_count)
    branch = scatter((ff_out + dot(attended, w_out)).astype(bf16))
    layer_out = (streams[3] + branch.astype(f32)).astype(bf16)
    do = dot_nt(cot_full, w_out).astype(bf16)
    gw_out = dot_tn(attended, cot_full).astype(bf16)
    gq, gk_parts, gv_parts = attend_back(
        query, k_all, v_all, do, attended, lse, info, key_slots, value_slots, span, tables, seq_count
    )
    gnq = scatter(dot_nt(gq, w_query).astype(bf16))
    gk_wide = disperse(gk_parts, key_bits)
    gv = disperse(gv_parts, value_bits).astype(bf16)
    same, down, up = tables
    heads = gk_wide.shape[1] // HD
    gk3 = gk_wide.reshape(block_rows, heads, HD)
    cos, sin = same[:, None, :HALF], -down[:, None, :HALF]
    a, b = gk3[..., :HALF], gk3[..., HALF:ROT]
    gk = (
        jnp.concatenate([a * cos + b * sin, b * cos - a * sin, gk3[..., ROT:]], axis=-1)
        .reshape(gk_wide.shape)
        .astype(bf16)
    )
    gnkv = scatter(jnp.concatenate([dot_nt(gk, w_key), dot_nt(gv, w_value)], axis=1).astype(bf16))
    gw_query = dot_tn(nq_full, gq).astype(bf16)
    gw_key = dot_tn(nkv_full[:, :width], gk).astype(bf16)
    gw_value = dot_tn(nkv_full[:, width:], gv).astype(bf16)
    ghist, pack = unmix(
        histories, streams, gn3, gnkv, gnq, cotangent, coef, mix_pre, norm_gains, mix_in, mix_out
    )
    big = lax.psum((gw_up, gw_down), "seq")
    tied = lax.optimization_barrier((gw_query, gw_key, gw_value, gw_out) + big)
    rest = lax.psum(tied[:4], "seq")
    big = tied[4:]
    pack = small_sum(pack)
    return (
        layer_out,
        ghist,
        pack[units : units + count, :width],
        jnp.transpose(pack[:units, :width]),
        pack[:units, width : width + mixes],
        pack[units, width : width + mixes],
        rest[0].astype(f32),
        rest[1].astype(f32),
        rest[2].astype(f32),
        rest[3].astype(f32),
        big[0].astype(f32),
        big[1].astype(f32),
    )


def solution(mesh):
    return jax.shard_map(
        body,
        mesh=mesh,
        in_specs=(
            P(None, ("seq", "head"), None),
            P(),
            P(),
            P(),
            P(),
            P(None, "head"),
            P(None, "head"),
            P(None, "head"),
            P("head", None),
            P(None, "head"),
            P("head", None),
            P(("seq", "head"), None),
            P(),
            P("seq"),
        ),
        out_specs=(
            P(("seq", "head"), None),
            P(None, ("seq", "head"), None),
            P(),
            P(),
            P(),
            P(),
            P(None, "head"),
            P(None, "head"),
            P(None, "head"),
            P("head", None),
            P(None, "head"),
            P("head", None),
        ),
        check_vma=False,
    )
```

```python
import functools

import jax
import jax.numpy as jnp
from jax import lax
from jax.experimental import pallas as pl
from jax.experimental.pallas import tpu as pltpu
from jax.sharding import PartitionSpec as P

HD = 128
ROT = 32
HALF = ROT // 2
MIB = 1024 * 1024

eps_norm = 1e-05
eps_rms = 1e-06
rope_base = 10000.0
hidden_mask = -1e30
highest = lax.Precision.HIGHEST
f32 = jnp.float32
bf16 = jnp.bfloat16
sqrt_half = 0.7071067811865476
inv_sqrt_2pi = 0.3989422804014327
log2e = 1.4426950408889634
small_cost = pl.CostEstimate(flops=MIB, bytes_accessed=MIB, transcendentals=0)


def vmem():
    return pl.BlockSpec(memory_space=pltpu.VMEM)


def params(mib, **more):
    return pltpu.CompilerParams(vmem_limit_bytes=mib * MIB, **more)


def cdf(x):
    return 0.5 * (1.0 + lax.erf(x * sqrt_half))


def pdf(x):
    return jnp.exp(x * x * -0.5) * inv_sqrt_2pi


def dot(a, b):
    return jnp.dot(a, b, preferred_element_type=f32)


def dot_nt(a, b):
    return lax.dot_general(a, b, (((1,), (1,)), ((), ())), preferred_element_type=f32)


def dot_tn(a, b):
    return lax.dot_general(a, b, (((0,), (0,)), ((), ())), preferred_element_type=f32)


def mix_kernel(tile, hist, gains, mix_in, mix_out, mix_bias, n3, nkv, nq, streams, coef, mix_pre):
    hist_count, rows, width = hist.shape
    count = gains.shape[0]
    newest = hist[hist_count - 1].astype(f32)
    scale = lax.rsqrt(jnp.mean(newest * newest, axis=-1, keepdims=True) + eps_rms)
    rms_low = (newest * scale).astype(bf16)
    pre = dot(rms_low, mix_in[...])
    mix_pre[...] = pre
    hidden = (pre * cdf(pre)).astype(bf16)
    coef[...] = dot(hidden, mix_out[...]) + mix_bias[...]
    chunk = 512

    def step(i, carry):
        at = pl.ds(pl.multiple_of(i * tile, tile), tile)
        rows_coef = coef[at, :]
        columns = [
            [rows_coef[:, c * hist_count + j : c * hist_count + j + 1] for j in range(hist_count)]
            for c in range(count)
        ]
        totals = [jnp.zeros((tile, 1), f32) for _ in range(count)]
        for lane in range(0, width, chunk):
            sums = [jnp.zeros((tile, chunk), f32) for _ in range(count)]
            for j in range(hist_count):
                h = hist[j, at, lane : lane + chunk].astype(f32)
                for c in range(count):
                    sums[c] = sums[c] + columns[c][j] * h
            for c in range(count):
                streams[c, at, lane : lane + chunk] = sums[c]
                totals[c] = totals[c] + jnp.sum(sums[c], axis=-1, keepdims=True)
        for c in range(count):
            x = streams[c, at, :]
            centre = x - totals[c] * (1.0 / width)
            spread = jnp.mean(centre * centre, axis=-1, keepdims=True)
            out = (centre * lax.rsqrt(spread + eps_norm) * gains[c : c + 1, :]).astype(bf16)
            if c == 0:
                nq[at, :] = out
            elif c == 3:
                n3[at, :] = out
            else:
                nkv[at, (c - 1) * width : c * width] = out
        return carry

    lax.fori_loop(0, rows // tile, step, 0)


def mix_forward(histories, norm_gains, mix_in, mix_out, mix_bias):
    hist_count, rows, width = histories.shape
    count = norm_gains.shape[0]
    return pl.pallas_call(
        functools.partial(mix_kernel, 16),
        out_shape=(
            jax.ShapeDtypeStruct((rows, width), bf16),
            jax.ShapeDtypeStruct((rows, 2 * width), bf16),
            jax.ShapeDtypeStruct((rows, width), bf16),
            jax.ShapeDtypeStruct((count, rows, width), f32),
            jax.ShapeDtypeStruct((rows, count * hist_count), f32),
            jax.ShapeDtypeStruct((rows, mix_in.shape[1]), f32),
        ),
        in_specs=[vmem()] * 5,
        out_specs=[vmem()] * 6,
        compiler_params=params(48),
        name="mix_forward",
    )(histories, norm_gains, mix_in, mix_out, mix_bias)


def unmix_kernel(
    hist, streams, gn3, gnkv, gnq, cot, coef, mix_pre, gains, mix_in, mix_out, ghist, pack, gs, rms_keep, hid_keep, gc_keep, gmp_keep
):
    hist_count, tile, width = hist.shape
    count = gains.shape[0]
    hidden_units = mix_in.shape[1]
    step = pl.program_id(0)

    @pl.when(step == 0)
    def _():
        pack[...] = jnp.zeros_like(pack)

    for c in range(count):
        x = streams[c]
        centre = x - jnp.mean(x, axis=-1, keepdims=True)
        inv = lax.rsqrt(jnp.mean(centre * centre, axis=-1, keepdims=True) + eps_norm)
        unit = centre * inv
        if c == 0:
            g = gnq[...].astype(f32)
        elif c == 3:
            g = gn3[...].astype(f32)
        else:
            g = gnkv[:, (c - 1) * width : c * width].astype(f32)
        pack[hidden_units + c : hidden_units + c + 1, 0:width] += jnp.sum(g * unit, axis=0, keepdims=True)
        d = g * gains[c : c + 1, :]
        out = inv * (
            d
            - jnp.mean(d, axis=-1, keepdims=True)
            - unit * jnp.mean(d * unit, axis=-1, keepdims=True)
        )
        if c == 3:
            out = out + cot[...].astype(f32)
        gs[c] = out
    lanes = lax.broadcasted_iota(jnp.int32, (tile, count * hist_count), 1)
    gc = jnp.zeros((tile, count * hist_count), f32)
    rows_coef = coef[...]
    for j in range(hist_count):
        h = hist[j].astype(f32)
        for c in range(count):
            k = c * hist_count + j
            gc = jnp.where(lanes == k, jnp.sum(gs[c] * h, axis=-1, keepdims=True), gc)
    for j in range(hist_count):
        total = rows_coef[:, j : j + 1] * gs[0]
        for c in range(1, count):
            k = c * hist_count + j
            total = total + rows_coef[:, k : k + 1] * gs[c]
        if j < hist_count - 1:
            ghist[j] = total.astype(bf16)
    pre = mix_pre[...]
    phi = cdf(pre)
    gmh = lax.dot_general(
        gc, mix_out[...].astype(f32), (((1,), (1,)), ((), ())), precision=highest
    )
    gmp = (phi + pre * pdf(pre)) * gmh
    gmp_low = gmp.astype(bf16)
    grad_rms = dot_nt(gmp_low, mix_in[...])
    newest = hist[hist_count - 1].astype(f32)
    scale = lax.rsqrt(jnp.mean(newest * newest, axis=-1, keepdims=True) + eps_rms)
    inner = jnp.mean(grad_rms * newest, axis=-1, keepdims=True)
    total = total + scale * grad_rms - newest * (scale * scale * scale * inner)
    ghist[hist_count - 1] = total.astype(bf16)
    at = pl.ds(pl.multiple_of(step * tile, tile), tile)
    rms_keep[at, :] = (newest * scale).astype(bf16)
    hid_keep[at, :] = (pre * phi).astype(bf16).astype(f32)
    gc_keep[at, :] = gc
    gmp_keep[at, :] = gmp_low

    @pl.when(step == pl.num_programs(0) - 1)
    def _():
        pack[0:hidden_units, 0:width] = dot_tn(gmp_keep[...], rms_keep[...])
        pack[0:hidden_units, width : width + count * hist_count] = lax.dot_general(
            hid_keep[...], gc_keep[...], (((0,), (0,)), ((), ())), precision=highest
        )
        pack[hidden_units : hidden_units + 1, width : width + count * hist_count] = jnp.sum(
            gc_keep[...], axis=0, keepdims=True
        )


def unmix(histories, streams, gn3, gnkv, gnq, cotangent, coef, mix_pre, norm_gains, mix_in, mix_out):
    hist_count, rows, width = histories.shape
    count = norm_gains.shape[0]
    units = mix_in.shape[1]
    mixes = count * hist_count
    tile = 16
    whole = lambda shape: pl.BlockSpec(shape, lambda i: (0, 0))
    return pl.pallas_call(
        unmix_kernel,
        grid=(rows // tile,),
        out_shape=(
            jax.ShapeDtypeStruct((hist_count, rows, width), bf16),
            jax.ShapeDtypeStruct((units + 8, width + 128), f32),
        ),
        in_specs=[
            pl.BlockSpec((hist_count, tile, width), lambda i: (0, i, 0)),
            pl.BlockSpec((count, tile, width), lambda i: (0, i, 0)),
            pl.BlockSpec((tile, width), lambda i: (i, 0)),
            pl.BlockSpec((tile, 2 * width), lambda i: (i, 0)),
            pl.BlockSpec((tile, width), lambda i: (i, 0)),
            pl.BlockSpec((tile, width), lambda i: (i, 0)),
            pl.BlockSpec((tile, mixes), lambda i: (i, 0)),
            pl.BlockSpec((tile, units), lambda i: (i, 0)),
            whole((count, width)),
            whole((width, units)),
            whole((units, mixes)),
        ],
        out_specs=[
            pl.BlockSpec((hist_count, tile, width), lambda i: (0, i, 0)),
            whole((units + 8, width + 128)),
        ],
        scratch_shapes=[
            pltpu.VMEM((count, tile, width), f32),
            pltpu.VMEM((rows, width), bf16),
            pltpu.VMEM((rows, units), f32),
            pltpu.VMEM((rows, mixes), f32),
            pltpu.VMEM((rows, units), bf16),
        ],
        compiler_params=params(48),
        name="unmix",
    )(histories, streams, gn3, gnkv, gnq, cotangent, coef, mix_pre, norm_gains, mix_in, mix_out)


def ff_kernel(count, rank_ref, *refs):
    pieces = 2 * count - 1
    sources = (refs[:pieces], refs[pieces : 2 * pieces])
    w_up, w_down, ff_out, gn3, gw_up, gw_down, cot, n3, gn_acc, sems = refs[2 * pieces :]
    step = pl.program_id(0)
    last = pl.num_programs(0) - 1

    @pl.when(step == 0)
    def _():
        rank = rank_ref[0]

        def each(act):
            for which, target in ((0, n3), (1, cot)):
                rows = target.shape[0] // count
                for at in range(pieces):
                    if at == 0:
                        block, there = rank, None
                    elif at < count:
                        block, there = rank - at, rank >= at
                    else:
                        k = at - count + 1
                        block, there = rank + k, rank + k < count

                    def one(block=block, at=at):
                        to = target.at[pl.ds(pl.multiple_of(block * rows, rows), rows), :]
                        act(pltpu.make_async_copy(sources[which][at], to, sems.at[which, at]))

                    if there is None:
                        one()
                    else:
                        pl.when(there)(one)

        each(lambda copy: copy.start())
        each(lambda copy: copy.wait())

    pre = dot(n3[...], w_up[...])
    phi = cdf(pre)
    act = (pre * phi).astype(bf16)
    slope = phi + pre * pdf(pre)
    grad = (dot_nt(cot[...], w_down[...]) * slope).astype(bf16)
    gw_down[...] = dot_tn(act, cot[...]).astype(bf16)
    gw_up[...] = dot_tn(n3[...], grad).astype(bf16)
    part_out = dot(act, w_down[...])
    part_gn = dot_nt(grad, w_up[...])

    @pl.when(step == 0)
    def _():
        ff_out[...] = part_out
        gn_acc[...] = part_gn

    @pl.when(step > 0)
    def _():
        ff_out[...] += part_out
        gn_acc[...] += part_gn

    @pl.when(step == last)
    def _():
        gn3[...] = gn_acc[...].astype(bf16)


def feed_forward(rank, n3_pieces, cot_pieces, w_up, w_down):
    count = (len(n3_pieces) + 1) // 2
    rows, width = n3_pieces[0].shape
    rows = rows * count
    hidden = w_up.shape[1]
    block = min(512, hidden)
    fixed = pl.BlockSpec((rows, width), lambda i, r: (0, 0))
    anywhere = pl.BlockSpec(memory_space=pl.ANY)
    grid_spec = pltpu.PrefetchScalarGridSpec(
        num_scalar_prefetch=1,
        grid=(hidden // block,),
        in_specs=[anywhere] * (2 * len(n3_pieces))
        + [
            pl.BlockSpec((width, block), lambda i, r: (0, i)),
            pl.BlockSpec((block, width), lambda i, r: (i, 0)),
        ],
        out_specs=[
            fixed,
            fixed,
            pl.BlockSpec((width, block), lambda i, r: (0, i)),
            pl.BlockSpec((block, width), lambda i, r: (i, 0)),
            fixed,
        ],
        scratch_shapes=[
            pltpu.VMEM((rows, width), bf16),
            pltpu.VMEM((rows, width), f32),
            pltpu.SemaphoreType.DMA((2, len(n3_pieces))),
        ],
    )
    return pl.pallas_call(
        functools.partial(ff_kernel, count),
        grid_spec=grid_spec,
        out_shape=(
            jax.ShapeDtypeStruct((rows, width), f32),
            jax.ShapeDtypeStruct((rows, width), bf16),
            jax.ShapeDtypeStruct((width, hidden), bf16),
            jax.ShapeDtypeStruct((hidden, width), bf16),
            jax.ShapeDtypeStruct((rows, width), bf16),
        ),
        compiler_params=params(60),
        cost_estimate=small_cost,
        name="feed_forward",
    )(rank, *n3_pieces, *cot_pieces, w_up, w_down)


def turn(x, same, down, up):
    return x * same + pltpu.roll(x, HD - HALF, 1) * down + pltpu.roll(x, HALF, 1) * up


def rotated(x, same, down, up):
    heads = [
        turn(x[:, h : h + HD], same, down, up).astype(bf16) for h in range(0, x.shape[1], HD)
    ]
    return jnp.concatenate(heads, axis=1)


def query_kernel(n, w, same, down, up, out):
    out[...] = rotated(dot(n[...], w[...]), same[...], down[...], up[...])


def key_value_kernel(n, wk, wv, same, down, up, key, value):
    width = wk.shape[0]
    key[...] = rotated(dot(n[:, 0:width], wk[...]), same[...], down[...], up[...])
    value[...] = dot(n[:, width : 2 * width], wv[...]).astype(bf16)


def project(kernel, n, weights, tables, outs, name):
    rows = n.shape[0]
    width, local = weights[0].shape
    block = min(256, rows)
    spec = lambda cols: pl.BlockSpec((block, cols), lambda i: (i, 0))
    return pl.pallas_call(
        kernel,
        grid=(rows // block,),
        out_shape=tuple(jax.ShapeDtypeStruct((rows, local), bf16) for _ in range(outs)),
        in_specs=[spec(n.shape[1])]
        + [pl.BlockSpec((width, local), lambda i: (0, 0))] * len(weights)
        + [spec(HD)] * 3,
        out_specs=tuple(spec(local) for _ in range(outs)),
        compiler_params=params(48),
        cost_estimate=small_cost,
        name=name,
    )(n, *weights, *tables)


def rope_lanes(positions):
    frequency = rope_base ** (-(jnp.arange(HALF, dtype=f32) * 2.0 / ROT))
    angles = positions.astype(f32)[:, None] * frequency[None, :]
    cos, sin = jnp.cos(angles), jnp.sin(angles)
    rows = positions.shape[0]
    ones = jnp.ones((rows, HD - ROT), f32)
    zeros = jnp.zeros((rows, HD - HALF), f32)
    same = jnp.concatenate([cos, cos, ones], axis=1)
    down = jnp.concatenate([-sin, zeros], axis=1)
    up = jnp.concatenate([zeros[:, :HALF], sin, zeros[:, : HD - ROT]], axis=1)
    return (same, down, up)


def hide(kb, block, span, bias):
    place = lax.broadcasted_iota(jnp.int32, bias.shape, 0) + kb * block
    seen = (place >= span[0:1, :]) & (place <= span[1:2, :])
    bias[...] = jnp.where(seen, 0.0, hidden_mask)


def take(step, sources, target):
    for i, source in enumerate(sources):

        @pl.when(step == i)
        def _(source=source):
            target[...] = source[...]


def attend_kernel(scale2, heads, blocks, info, offsets, q, span, *refs):
    keys, values = refs[:blocks], refs[blocks : 2 * blocks]
    out, lse, peak, total, acc, bias, k, v = refs[2 * blocks :]
    step = pl.program_id(0)
    rank, reach = info[0], info[1]
    kb = offsets[step]
    block = k.shape[0]

    @pl.when(step == 0)
    def _():
        peak[...] = jnp.full_like(peak, hidden_mask)
        total[...] = jnp.zeros_like(total)
        acc[...] = jnp.zeros_like(acc)

    def update(extra):
        for h in range(heads):
            lanes = slice(h * HD, (h + 1) * HD)
            one = slice(h, h + 1)
            scores = dot_nt(k[:, lanes], q[:, lanes]) * scale2
            if extra is not None:
                scores = scores + extra[...]
            old = peak[one, :]
            new = jnp.maximum(old, jnp.max(scores, axis=0, keepdims=True))
            weights = jnp.exp2(scores - new)
            factor = jnp.exp2(old - new)
            peak[one, :] = new
            total[one, :] = total[one, :] * factor + jnp.sum(weights, axis=0, keepdims=True)
            acc[lanes, :] = acc[lanes, :] * factor + dot_tn(v[:, lanes], weights.astype(bf16))

    needs = (kb == rank) | (reach > kb * block)

    @pl.when(kb <= rank)
    def _():
        take(step, keys, k)
        take(step, values, v)

    @pl.when((kb <= rank) & jnp.logical_not(needs))
    def _():
        update(None)

    @pl.when((kb <= rank) & needs)
    def _():
        hide(kb, block, span, bias)
        update(bias)

    @pl.when(step == pl.num_programs(0) - 1)
    def _():
        for h in range(heads):
            lanes = slice(h * HD, (h + 1) * HD)
            one = slice(h, h + 1)
            out[:, lanes] = jnp.transpose(acc[lanes, :] / total[one, :]).astype(bf16)
            lse[one, :] = peak[one, :] + jnp.log2(total[one, :])


def attend(q, keys, values, info, offsets, span):
    rows, local = q.shape
    heads = local // HD
    block = keys[0].shape[0]
    blocks = len(keys)
    scale2 = HD ** (-0.5) * log2e
    fixed = lambda shape: pl.BlockSpec(shape, lambda b, info, at: (0, 0))
    grid_spec = pltpu.PrefetchScalarGridSpec(
        num_scalar_prefetch=2,
        grid=(blocks,),
        in_specs=[fixed((rows, local)), fixed((8, rows))] + [fixed((block, local))] * (2 * blocks),
        out_specs=[fixed((rows, local)), fixed((8, rows))],
        scratch_shapes=[
            pltpu.VMEM((8, rows), f32),
            pltpu.VMEM((8, rows), f32),
            pltpu.VMEM((local, rows), f32),
            pltpu.VMEM((block, rows), f32),
            pltpu.VMEM((block, local), bf16),
            pltpu.VMEM((block, local), bf16),
        ],
    )
    return pl.pallas_call(
        functools.partial(attend_kernel, scale2, heads, blocks),
        grid_spec=grid_spec,
        out_shape=(
            jax.ShapeDtypeStruct((rows, local), bf16),
            jax.ShapeDtypeStruct((8, rows), f32),
        ),
        compiler_params=params(56),
        cost_estimate=small_cost,
        name="attend",
    )(info, offsets, q, span, *keys, *values)


def attend_back_kernel(scale, scale2, heads, blocks, *refs):
    info, offsets, _, _ = refs[:4]
    q, do, o, lse, span, same, down, up = refs[4:12]
    keys, values = refs[12 : 12 + blocks], refs[12 + blocks : 12 + 2 * blocks]
    gq, gk_hi, gk_lo, gv_hi, gv_lo, delta, acc, bias, k, v = refs[12 + 2 * blocks :]
    step = pl.program_id(0)
    rank, reach = info[0], info[1]
    kb = offsets[step]
    block = k.shape[0]

    @pl.when(step == 0)
    def _():
        for h in range(heads):
            lanes = slice(h * HD, (h + 1) * HD)
            both = do[:, lanes].astype(f32) * o[:, lanes].astype(f32)
            delta[h : h + 1, :] = jnp.sum(jnp.transpose(both), axis=0, keepdims=True)
        acc[...] = jnp.zeros_like(acc)

    def update(extra, gk, gv):
        for h in range(heads):
            lanes = slice(h * HD, (h + 1) * HD)
            one = slice(h, h + 1)
            scores = dot_nt(k[:, lanes], q[:, lanes]) * scale2
            if extra is not None:
                scores = scores + extra[...]
            weights = jnp.exp2(scores - lse[one, :])
            gv[:, lanes] = dot(weights.astype(bf16), do[:, lanes]).astype(bf16)
            grad_weights = dot_nt(v[:, lanes], do[:, lanes])
            grad_scores = (weights * (grad_weights - delta[one, :])).astype(bf16)
            gk[:, lanes] = (dot(grad_scores, q[:, lanes]) * scale).astype(bf16)
            acc[lanes, :] += dot_tn(k[:, lanes], grad_scores)

    needs = (kb == rank) | (reach > kb * block)

    @pl.when(kb <= rank)
    def _():
        take(step, keys, k)
        take(step, values, v)

    for high, gk, gv in ((True, gk_hi, gv_hi), (False, gk_lo, gv_lo)):
        here = (step < blocks // 2) if high else (step >= blocks // 2)

        @pl.when(here & (kb <= rank) & jnp.logical_not(needs))
        def _(gk=gk, gv=gv):
            update(None, gk, gv)

        @pl.when(here & (kb <= rank) & needs)
        def _(gk=gk, gv=gv):
            hide(kb, block, span, bias)
            update(bias, gk, gv)

        @pl.when(here & (kb > rank))
        def _(gk=gk, gv=gv):
            gk[...] = jnp.zeros_like(gk)
            gv[...] = jnp.zeros_like(gv)

    @pl.when(step == pl.num_programs(0) - 1)
    def _():
        for h in range(heads):
            lanes = slice(h * HD, (h + 1) * HD)
            x = jnp.transpose(acc[lanes, :]) * scale
            gq[:, lanes] = turn(x, same[...], -down[...], -up[...]).astype(bf16)


def attend_back(q, keys, values, do, o, lse, info, offsets, key_at, value_at, span, tables):
    rows, local = q.shape
    heads = local // HD
    block = keys[0].shape[0]
    blocks = len(keys)
    half = blocks // 2
    scale = HD ** (-0.5)
    fixed = lambda shape: pl.BlockSpec(shape, lambda b, info, at, ks, vs: (0, 0))
    high = lambda pick: pl.BlockSpec(
        (block, local), lambda b, info, at, ks, vs: ((ks, vs)[pick][jnp.minimum(b, half - 1)] - half, 0)
    )
    low = lambda pick: pl.BlockSpec(
        (block, local), lambda b, info, at, ks, vs: ((ks, vs)[pick][jnp.maximum(b, half)], 0)
    )
    grid_spec = pltpu.PrefetchScalarGridSpec(
        num_scalar_prefetch=4,
        grid=(blocks,),
        in_specs=[fixed((rows, local))] * 3
        + [fixed((8, rows))] * 2
        + [fixed((rows, HD))] * 3
        + [fixed((block, local))] * (2 * blocks),
        out_specs=[fixed((rows, local)), high(0), low(0), high(1), low(1)],
        scratch_shapes=[
            pltpu.VMEM((8, rows), f32),
            pltpu.VMEM((local, rows), f32),
            pltpu.VMEM((block, rows), f32),
            pltpu.VMEM((block, local), bf16),
            pltpu.VMEM((block, local), bf16),
        ],
    )
    part = jax.ShapeDtypeStruct((half * block, local), bf16)
    return pl.pallas_call(
        functools.partial(attend_back_kernel, scale, scale * log2e, heads, blocks),
        grid_spec=grid_spec,
        out_shape=(jax.ShapeDtypeStruct((rows, local), bf16), part, part, part, part),
        compiler_params=params(60),
        cost_estimate=small_cost,
        name="attend_back",
    )(info, offsets, key_at, value_at, q, do, o, lse, span, *tables, *keys, *values)


def key_value_back_kernel(terms, *refs):
    gk_parts, gv_parts = refs[:terms], refs[terms : 2 * terms]
    wk, wv, same, down, up, gk, gv, gn = refs[2 * terms :]
    width = wk.shape[0]
    add = lambda parts: functools.reduce(lambda a, b: a + b, [p[...].astype(f32) for p in parts])
    gk[...] = rotated(add(gk_parts), same[...], -down[...], -up[...])
    gv[...] = add(gv_parts).astype(bf16)
    gn[:, 0:width] = dot_nt(gk[...], wk[...]).astype(bf16)
    gn[:, width : 2 * width] = dot_nt(gv[...], wv[...]).astype(bf16)


def key_value_back(gk_parts, gv_parts, wk, wv, tables):
    rows = tables[0].shape[0]
    local = gk_parts[0].shape[1]
    width = wk.shape[0]
    block = min(256, rows)
    spec = lambda cols: pl.BlockSpec((block, cols), lambda i: (i, 0))
    whole = pl.BlockSpec((width, local), lambda i: (0, 0))
    return pl.pallas_call(
        functools.partial(key_value_back_kernel, len(gk_parts)),
        grid=(rows // block,),
        out_shape=(
            jax.ShapeDtypeStruct((rows, local), bf16),
            jax.ShapeDtypeStruct((rows, local), bf16),
            jax.ShapeDtypeStruct((rows, 2 * width), bf16),
        ),
        in_specs=[spec(local)] * (2 * len(gk_parts)) + [whole] * 2 + [spec(HD)] * 3,
        out_specs=[spec(local), spec(local), spec(2 * width)],
        compiler_params=params(48),
        cost_estimate=small_cost,
        name="key_value_back",
    )(*gk_parts, *gv_parts, wk, wv, *tables)


def weight_grad_kernel(half, core, nq, nk, nv, cot, gq, gk, gv, att, send_a, own_a, send_b, own_b):
    step = pl.program_id(0)
    local = gq.shape[1]

    def fill(a, b):
        a[:, 0:local] = dot_tn(nq[...], gq[...]).astype(bf16)
        a[:, local : 2 * local] = dot_tn(nk[...], gk[...]).astype(bf16)
        b[:, 0:local] = dot_tn(nv[...], gv[...]).astype(bf16)
        b[:, local : 2 * local] = dot_tn(cot[...], att[...]).astype(bf16)

    @pl.when(step < half)
    def _():
        fill(send_a, send_b)

    @pl.when(step >= half)
    def _():
        fill(own_a, own_b)


def weight_grads(core, nq, nkv, cot, gq, gk, gv, att):
    rows, width = nq.shape
    local = gq.shape[1]
    block = 256
    steps = width // block
    half = steps // 2
    column = lambda i, core: jnp.where(i < half, (1 - core[0]) * half + i, core[0] * half + i - half)
    lhs = lambda shift: pl.BlockSpec((rows, block), lambda i, core: (0, column(i, core) + shift))
    rhs = pl.BlockSpec((rows, local), lambda i, core: (0, 0))
    out = jax.ShapeDtypeStruct((width // 2, 2 * local), bf16)
    first = pl.BlockSpec((block, 2 * local), lambda i, core: (jnp.minimum(i, half - 1), 0))
    second = pl.BlockSpec((block, 2 * local), lambda i, core: (jnp.maximum(i - half, 0), 0))
    grid_spec = pltpu.PrefetchScalarGridSpec(
        num_scalar_prefetch=1,
        grid=(steps,),
        in_specs=[lhs(0), lhs(0), lhs(steps), lhs(0)] + [rhs] * 4,
        out_specs=[first, second, first, second],
    )
    return pl.pallas_call(
        functools.partial(weight_grad_kernel, half),
        grid_spec=grid_spec,
        out_shape=(out, out, out, out),
        compiler_params=params(48),
        cost_estimate=small_cost,
        name="weight_grads",
    )(core, nq, nkv, nkv, cot, gq, gk, gv, att)


def assemble_kernel(half, local, a_slot, b_slot, a_lo, a_hi, b_lo, b_hi, gwq, gwk, gwv, gwo):
    r = pl.program_id(0)

    @pl.when(a_slot[r] < half)
    def _():
        gwq[...] = a_lo[:, 0:local].astype(f32)
        gwk[...] = a_lo[:, local : 2 * local].astype(f32)

    @pl.when(a_slot[r] >= half)
    def _():
        gwq[...] = a_hi[:, 0:local].astype(f32)
        gwk[...] = a_hi[:, local : 2 * local].astype(f32)

    @pl.when(b_slot[r] < half)
    def _():
        gwv[...] = b_lo[:, 0:local].astype(f32)
        gwo[...] = jnp.transpose(b_lo[:, local : 2 * local].astype(f32))

    @pl.when(b_slot[r] >= half)
    def _():
        gwv[...] = b_hi[:, 0:local].astype(f32)
        gwo[...] = jnp.transpose(b_hi[:, local : 2 * local].astype(f32))


def assemble(a_slot, b_slot, a_lo, a_hi, b_lo, b_hi, pieces):
    half = pieces // 2
    piece = a_lo.shape[0] // half
    local = a_lo.shape[1] // 2
    width = pieces * piece
    low = lambda pick: pl.BlockSpec(
        (piece, 2 * local), lambda i, a, b: (jnp.minimum((a, b)[pick][i], half - 1), 0)
    )
    high = lambda pick: pl.BlockSpec(
        (piece, 2 * local), lambda i, a, b: (jnp.maximum((a, b)[pick][i] - half, 0), 0)
    )
    rowed = pl.BlockSpec((piece, local), lambda i, a, b: (i, 0))
    tall = jax.ShapeDtypeStruct((width, local), f32)
    grid_spec = pltpu.PrefetchScalarGridSpec(
        num_scalar_prefetch=2,
        grid=(pieces,),
        in_specs=[low(0), high(0), low(1), high(1)],
        out_specs=[rowed, rowed, rowed, pl.BlockSpec((local, piece), lambda i, a, b: (0, i))],
    )
    return pl.pallas_call(
        functools.partial(assemble_kernel, half, local),
        grid_spec=grid_spec,
        out_shape=(tall, tall, tall, jax.ShapeDtypeStruct((local, width), f32)),
        compiler_params=params(32),
        name="assemble",
    )(a_slot, b_slot, a_lo, a_hi, b_lo, b_hi)


def flipped(x, axis, bit, sender=None):
    count = lax.axis_size(axis)
    sends = [i for i in range(count) if sender is None or bool(i & bit) == sender]
    return lax.ppermute(x, axis, [(i, i ^ bit) for i in sends])


def top(bit):
    return 2 * bit == lax.axis_size("seq")


def bits_of(count):
    bits = []
    while (1 << len(bits)) < count:
        bits.append(1 << len(bits))
    return bits


def slot_order(bits):
    order = [0]
    for bit in bits:
        order = order + [m | bit for m in order]
    return order


def collect(block, bits):
    held = {0: block}
    for bit in bits:
        sender = False if top(bit) else None
        held.update({m | bit: flipped(x, "seq", bit, sender) for m, x in held.items()})
    return held


def summed(a, b):
    return (a.astype(f32) + b.astype(f32)).astype(bf16)


def disperse(low, high, bits):
    terms = [low, flipped(high, "seq", bits[-1], True if top(bits[-1]) else None)]
    half = low.shape[0] // 2
    for bit in reversed(bits[:-1]):
        total = functools.reduce(lambda a, b: a + b, [t[half : 2 * half].astype(f32) for t in terms])
        terms.append(flipped(total.astype(bf16), "seq", bit, True if top(bit) else None))
        half = half // 2
    return terms


def reduced(own, got, bits, rank):
    for bit in bits:
        half = own.shape[0] // 2
        side = (rank & bit) // bit
        cut = lambda x, at: lax.dynamic_slice_in_dim(x, at * half, half)
        send = summed(cut(own, 1 - side), cut(got, 1 - side))
        own = summed(cut(own, side), cut(got, side))
        got = flipped(send, "seq", bit)
    return summed(own, got)


def spread(piece, bits):
    held = piece
    for bit in bits[:-1]:
        held = jnp.concatenate([held, flipped(held, "seq", bit)], axis=0)
    return held, flipped(held, "seq", bits[-1])


def piece_slots(bits, rank, count):
    order = slot_order(bits[::-1])
    table = [0] * count
    for slot, m in enumerate(order):
        table[m] = slot
    owners = []
    for r in range(count):
        owner = 0
        for at, bit in enumerate(bits):
            if (r >> (len(bits) - 1 - at)) & 1:
                owner |= bit
        owners.append(owner)
    return jnp.take(jnp.array(table, jnp.int32), jnp.array(owners, jnp.int32) ^ rank)


def ring(x, axis):
    count = lax.axis_size(axis)
    from_below, from_above = [], []
    up = down = x
    for k in range(1, count):
        up = lax.ppermute(up, axis, [(i, i + 1) for i in range(k - 1, count - 1)])
        down = lax.ppermute(down, axis, [(i, i - 1) for i in range(1, count - k + 1)])
        from_below.append(up)
        from_above.append(down)
    return from_below + from_above


def after(x, *earlier):
    anywhere = pl.BlockSpec(memory_space=pl.ANY)
    return pl.pallas_call(
        lambda *refs: None,
        out_shape=jax.ShapeDtypeStruct(x.shape, x.dtype),
        in_specs=[anywhere] * (1 + len(earlier)),
        out_specs=anywhere,
        input_output_aliases={0: 0},
        name="after",
    )(x, *earlier)


def small_sum(x):
    x = x.astype(bf16)
    for axis in ("seq", "head"):
        for bit in bits_of(lax.axis_size(axis)):
            x = summed(x, flipped(x, axis, bit))
    return x.astype(f32)


def body(
    histories,
    norm_gains,
    mix_in,
    mix_out,
    mix_bias,
    w_query,
    w_key,
    w_value,
    w_out,
    w_up,
    w_down,
    cotangent,
    doc_ids,
    positions,
):
    seq_count = lax.axis_size("seq")
    rank = lax.axis_index("seq")
    block_rows = positions.shape[0]
    hist_count, tok_rows, width = histories.shape
    count = norm_gains.shape[0]
    units = mix_in.shape[1]
    mixes = mix_out.shape[1]

    def gather(x):
        return lax.all_gather(x, "head", axis=0, tiled=True)

    def scatter(x):
        return lax.psum_scatter(x, "head", scatter_dimension=0, tiled=True)

    tables = rope_lanes(positions)
    place = rank * block_rows + jnp.arange(block_rows, dtype=jnp.int32)
    first = place - positions
    span = jnp.concatenate([first[None], place[None], jnp.zeros((6, block_rows), jnp.int32)], axis=0)
    info = jnp.stack([rank.astype(jnp.int32), jnp.max(first)])
    bits = bits_of(seq_count)
    key_bits = bits[1:] + bits[:1]
    value_bits = bits[1:][::-1] + bits[:1]
    key_order = slot_order(key_bits)
    value_order = slot_order(value_bits)
    half = seq_count // 2
    order = key_order[half:] + key_order[:half]
    offsets = jnp.array(order, jnp.int32) ^ rank
    key_at = jnp.array([key_order.index(m) for m in order], jnp.int32)
    value_at = jnp.array([value_order.index(m) for m in order], jnp.int32)
    same, down, up = tables
    core = (rank & 1)[None].astype(jnp.int32)
    cot_pieces = [cotangent] + ring(cotangent, "head")
    n3, nkv, nq, streams, coef, mix_pre = mix_forward(
        histories, norm_gains, mix_in, mix_out, mix_bias[None, :]
    )
    n3_pieces = [n3] + ring(n3, "head")
    nkv_full = gather(after(nkv, *n3_pieces[1:], *cot_pieces[1:]))
    nq_full = gather(nq)
    ff_out, gn3_part, gw_up, gw_down, cot_full = feed_forward(
        lax.axis_index("head")[None], n3_pieces, cot_pieces, w_up, w_down
    )
    gn3 = scatter(gn3_part)
    gw_up, gw_down = lax.psum((gw_up, gw_down), "seq")
    key, value = project(
        key_value_kernel, nkv_full, (w_key, w_value), (after(same, gn3_part), down, up), 2, "project_kv"
    )
    (query,) = project(query_kernel, nq_full, (w_query,), tables, 1, "project_q")
    keys = collect(key, key_bits)
    values = collect(value, value_bits)
    keys, values = [keys[m] for m in order], [values[m] for m in order]
    attended, lse = attend(query, keys, values, info, offsets, span)
    branch = scatter((ff_out + dot(attended, w_out)).astype(bf16))
    layer_out = (streams[3] + branch.astype(f32)).astype(bf16)
    do = dot_nt(cot_full, w_out).astype(bf16)
    gq, gk_hi, gk_lo, gv_hi, gv_lo = attend_back(
        query,
        keys,
        values,
        do,
        attended,
        lse,
        info,
        offsets,
        key_at,
        value_at,
        span,
        tables,
    )
    gnq = scatter(dot_nt(gq, w_query).astype(bf16))
    gk, gv, gnkv_part = key_value_back(
        disperse(gk_lo, gk_hi, key_bits),
        disperse(gv_lo, gv_hi, value_bits),
        w_key,
        w_value,
        tables,
    )
    gnkv = scatter(gnkv_part)
    gw_up, gw_down = gw_up.astype(f32), gw_down.astype(f32)
    send_a, own_a, send_b, own_b = weight_grads(
        core, nq_full, nkv_full, cot_full, gq, gk, gv, attended
    )
    got_a = flipped(send_a, "seq", 1)
    got_b = flipped(send_b, "seq", 1)
    a_bits = bits[1:]
    b_bits = bits[1:][::-1]
    a_lo, a_hi = spread(reduced(own_a, got_a, a_bits, rank), a_bits[::-1] + bits[:1])
    b_lo, b_hi = spread(reduced(own_b, got_b, b_bits, rank), b_bits[::-1] + bits[:1])
    gwq, gwk, gwv, gwo = assemble(
        piece_slots(bits[:1] + a_bits, rank, seq_count),
        piece_slots(bits[:1] + b_bits, rank, seq_count),
        a_lo,
        a_hi,
        b_lo,
        b_hi,
        seq_count,
    )
    coef = after(coef, gw_up, gw_down)
    ghist, pack = unmix(
        histories, streams, gn3, gnkv, gnq, cotangent, coef, mix_pre, norm_gains, mix_in, mix_out
    )
    pack = small_sum(pack)
    return (
        layer_out,
        ghist,
        pack[units : units + count, :width],
        jnp.transpose(pack[:units, :width]),
        pack[:units, width : width + mixes],
        pack[units, width : width + mixes],
        gwq,
        gwk,
        gwv,
        gwo,
        gw_up,
        gw_down,
    )


def solution(mesh):
    return jax.shard_map(
        body,
        mesh=mesh,
        in_specs=(
            P(None, ("seq", "head"), None),
            P(),
            P(),
            P(),
            P(),
            P(None, "head"),
            P(None, "head"),
            P(None, "head"),
            P("head", None),
            P(None, "head"),
            P("head", None),
            P(("seq", "head"), None),
            P(),
            P("seq"),
        ),
        out_specs=(
            P(("seq", "head"), None),
            P(None, ("seq", "head"), None),
            P(),
            P(),
            P(),
            P(),
            P(None, "head"),
            P(None, "head"),
            P(None, "head"),
            P("head", None),
            P(None, "head"),
            P("head", None),
        ),
        check_vma=False,
    )
```

```python
import functools

import jax
import jax.numpy as jnp
from jax import lax
from jax.experimental import pallas as pl
from jax.experimental.pallas import tpu as pltpu
from jax.sharding import PartitionSpec as P

HD = 128
ROT = 32
HALF = ROT // 2
MIB = 1024 * 1024

eps_norm = 1e-05
eps_rms = 1e-06
rope_base = 10000.0
hidden_mask = -1e30
highest = lax.Precision.HIGHEST
f32 = jnp.float32
bf16 = jnp.bfloat16
sqrt_half = 0.7071067811865476
inv_sqrt_2pi = 0.3989422804014327
log2e = 1.4426950408889634
small_cost = pl.CostEstimate(flops=MIB, bytes_accessed=MIB, transcendentals=0)


def vmem():
    return pl.BlockSpec(memory_space=pltpu.VMEM)


def params(mib, **more):
    return pltpu.CompilerParams(vmem_limit_bytes=mib * MIB, **more)


def cdf(x):
    return 0.5 * (1.0 + lax.erf(x * sqrt_half))


def pdf(x):
    return jnp.exp(x * x * -0.5) * inv_sqrt_2pi


def dot(a, b):
    return jnp.dot(a, b, preferred_element_type=f32)


def dot_nt(a, b):
    return lax.dot_general(a, b, (((1,), (1,)), ((), ())), preferred_element_type=f32)


def dot_tn(a, b):
    return lax.dot_general(a, b, (((0,), (0,)), ((), ())), preferred_element_type=f32)


def mix_kernel(tile, hist, gains, mix_in, mix_out, mix_bias, n3, nkv, nq, streams, coef, mix_pre):
    hist_count, rows, width = hist.shape
    count = gains.shape[0]
    newest = hist[hist_count - 1].astype(f32)
    scale = lax.rsqrt(jnp.mean(newest * newest, axis=-1, keepdims=True) + eps_rms)
    rms_low = (newest * scale).astype(bf16)
    pre = dot(rms_low, mix_in[...])
    mix_pre[...] = pre
    hidden = (pre * cdf(pre)).astype(bf16)
    coef[...] = dot(hidden, mix_out[...]) + mix_bias[...]
    chunk = 512

    def step(i, carry):
        at = pl.ds(pl.multiple_of(i * tile, tile), tile)
        rows_coef = coef[at, :]
        columns = [
            [rows_coef[:, c * hist_count + j : c * hist_count + j + 1] for j in range(hist_count)]
            for c in range(count)
        ]
        totals = [jnp.zeros((tile, 1), f32) for _ in range(count)]
        for lane in range(0, width, chunk):
            sums = [jnp.zeros((tile, chunk), f32) for _ in range(count)]
            for j in range(hist_count):
                h = hist[j, at, lane : lane + chunk].astype(f32)
                for c in range(count):
                    sums[c] = sums[c] + columns[c][j] * h
            for c in range(count):
                streams[c, at, lane : lane + chunk] = sums[c]
                totals[c] = totals[c] + jnp.sum(sums[c], axis=-1, keepdims=True)
        for c in range(count):
            x = streams[c, at, :]
            centre = x - totals[c] * (1.0 / width)
            spread = jnp.mean(centre * centre, axis=-1, keepdims=True)
            out = (centre * lax.rsqrt(spread + eps_norm) * gains[c : c + 1, :]).astype(bf16)
            if c == 0:
                nq[at, :] = out
            elif c == 3:
                n3[at, :] = out
            else:
                nkv[at, (c - 1) * width : c * width] = out
        return carry

    lax.fori_loop(0, rows // tile, step, 0)


def mix_forward(histories, norm_gains, mix_in, mix_out, mix_bias):
    hist_count, rows, width = histories.shape
    count = norm_gains.shape[0]
    return pl.pallas_call(
        functools.partial(mix_kernel, 16),
        out_shape=(
            jax.ShapeDtypeStruct((rows, width), bf16),
            jax.ShapeDtypeStruct((rows, 2 * width), bf16),
            jax.ShapeDtypeStruct((rows, width), bf16),
            jax.ShapeDtypeStruct((count, rows, width), f32),
            jax.ShapeDtypeStruct((rows, count * hist_count), f32),
            jax.ShapeDtypeStruct((rows, mix_in.shape[1]), f32),
        ),
        in_specs=[vmem()] * 5,
        out_specs=[vmem()] * 6,
        compiler_params=params(48),
        name="mix_forward",
    )(histories, norm_gains, mix_in, mix_out, mix_bias)


def unmix_kernel(
    hist, streams, gn3, gnkv, gnq, cot, coef, mix_pre, gains, mix_in, mix_out, ghist, pack, gs, rms_keep, hid_keep, gc_keep, gmp_keep
):
    hist_count, tile, width = hist.shape
    count = gains.shape[0]
    hidden_units = mix_in.shape[1]
    step = pl.program_id(0)

    @pl.when(step == 0)
    def _():
        pack[...] = jnp.zeros_like(pack)

    for c in range(count):
        x = streams[c]
        centre = x - jnp.mean(x, axis=-1, keepdims=True)
        inv = lax.rsqrt(jnp.mean(centre * centre, axis=-1, keepdims=True) + eps_norm)
        unit = centre * inv
        if c == 0:
            g = gnq[...].astype(f32)
        elif c == 3:
            g = gn3[...].astype(f32)
        else:
            g = gnkv[:, (c - 1) * width : c * width].astype(f32)
        pack[hidden_units + c : hidden_units + c + 1, 0:width] += jnp.sum(g * unit, axis=0, keepdims=True)
        d = g * gains[c : c + 1, :]
        out = inv * (
            d
            - jnp.mean(d, axis=-1, keepdims=True)
            - unit * jnp.mean(d * unit, axis=-1, keepdims=True)
        )
        if c == 3:
            out = out + cot[...].astype(f32)
        gs[c] = out
    lanes = lax.broadcasted_iota(jnp.int32, (tile, count * hist_count), 1)
    gc = jnp.zeros((tile, count * hist_count), f32)
    rows_coef = coef[...]
    for j in range(hist_count):
        h = hist[j].astype(f32)
        for c in range(count):
            k = c * hist_count + j
            gc = jnp.where(lanes == k, jnp.sum(gs[c] * h, axis=-1, keepdims=True), gc)
    for j in range(hist_count):
        total = rows_coef[:, j : j + 1] * gs[0]
        for c in range(1, count):
            k = c * hist_count + j
            total = total + rows_coef[:, k : k + 1] * gs[c]
        if j < hist_count - 1:
            ghist[j] = total.astype(bf16)
    pre = mix_pre[...]
    phi = cdf(pre)
    gmh = lax.dot_general(
        gc, mix_out[...].astype(f32), (((1,), (1,)), ((), ())), precision=highest
    )
    gmp = (phi + pre * pdf(pre)) * gmh
    gmp_low = gmp.astype(bf16)
    grad_rms = dot_nt(gmp_low, mix_in[...])
    newest = hist[hist_count - 1].astype(f32)
    scale = lax.rsqrt(jnp.mean(newest * newest, axis=-1, keepdims=True) + eps_rms)
    inner = jnp.mean(grad_rms * newest, axis=-1, keepdims=True)
    total = total + scale * grad_rms - newest * (scale * scale * scale * inner)
    ghist[hist_count - 1] = total.astype(bf16)
    at = pl.ds(pl.multiple_of(step * tile, tile), tile)
    rms_keep[at, :] = (newest * scale).astype(bf16)
    hid_keep[at, :] = (pre * phi).astype(bf16).astype(f32)
    gc_keep[at, :] = gc
    gmp_keep[at, :] = gmp_low

    @pl.when(step == pl.num_programs(0) - 1)
    def _():
        pack[0:hidden_units, 0:width] = dot_tn(gmp_keep[...], rms_keep[...])
        pack[0:hidden_units, width : width + count * hist_count] = lax.dot_general(
            hid_keep[...], gc_keep[...], (((0,), (0,)), ((), ())), precision=highest
        )
        pack[hidden_units : hidden_units + 1, width : width + count * hist_count] = jnp.sum(
            gc_keep[...], axis=0, keepdims=True
        )


def unmix(histories, streams, gn3, gnkv, gnq, cotangent, coef, mix_pre, norm_gains, mix_in, mix_out):
    hist_count, rows, width = histories.shape
    count = norm_gains.shape[0]
    units = mix_in.shape[1]
    mixes = count * hist_count
    tile = 16
    whole = lambda shape: pl.BlockSpec(shape, lambda i: (0, 0))
    return pl.pallas_call(
        unmix_kernel,
        grid=(rows // tile,),
        out_shape=(
            jax.ShapeDtypeStruct((hist_count, rows, width), bf16),
            jax.ShapeDtypeStruct((units + 8, width + 128), f32),
        ),
        in_specs=[
            pl.BlockSpec((hist_count, tile, width), lambda i: (0, i, 0)),
            pl.BlockSpec((count, tile, width), lambda i: (0, i, 0)),
            pl.BlockSpec((tile, width), lambda i: (i, 0)),
            pl.BlockSpec((tile, 2 * width), lambda i: (i, 0)),
            pl.BlockSpec((tile, width), lambda i: (i, 0)),
            pl.BlockSpec((tile, width), lambda i: (i, 0)),
            pl.BlockSpec((tile, mixes), lambda i: (i, 0)),
            pl.BlockSpec((tile, units), lambda i: (i, 0)),
            whole((count, width)),
            whole((width, units)),
            whole((units, mixes)),
        ],
        out_specs=[
            pl.BlockSpec((hist_count, tile, width), lambda i: (0, i, 0)),
            whole((units + 8, width + 128)),
        ],
        scratch_shapes=[
            pltpu.VMEM((count, tile, width), f32),
            pltpu.VMEM((rows, width), bf16),
            pltpu.VMEM((rows, units), f32),
            pltpu.VMEM((rows, mixes), f32),
            pltpu.VMEM((rows, units), bf16),
        ],
        compiler_params=params(48),
        name="unmix",
    )(histories, streams, gn3, gnkv, gnq, cotangent, coef, mix_pre, norm_gains, mix_in, mix_out)


def ff_kernel(count, rank_ref, *refs):
    pieces = 2 * count - 1
    sources = (refs[:pieces], refs[pieces : 2 * pieces])
    w_up, w_down, ff_out, gn3, gw_up, gw_down, cot, n3, gn_acc, sems = refs[2 * pieces :]
    step = pl.program_id(0)
    last = pl.num_programs(0) - 1

    @pl.when(step == 0)
    def _():
        rank = rank_ref[0]

        def each(act):
            for which, target in ((0, n3), (1, cot)):
                rows = target.shape[0] // count
                for at in range(pieces):
                    if at == 0:
                        block, there = rank, None
                    elif at < count:
                        block, there = rank - at, rank >= at
                    else:
                        k = at - count + 1
                        block, there = rank + k, rank + k < count

                    def one(block=block, at=at):
                        to = target.at[pl.ds(pl.multiple_of(block * rows, rows), rows), :]
                        act(pltpu.make_async_copy(sources[which][at], to, sems.at[which, at]))

                    if there is None:
                        one()
                    else:
                        pl.when(there)(one)

        each(lambda copy: copy.start())
        each(lambda copy: copy.wait())

    pre = dot(n3[...], w_up[...])
    phi = cdf(pre)
    act = (pre * phi).astype(bf16)
    slope = phi + pre * pdf(pre)
    grad = (dot_nt(cot[...], w_down[...]) * slope).astype(bf16)
    gw_down[...] = dot_tn(act, cot[...]).astype(bf16)
    gw_up[...] = dot_tn(n3[...], grad).astype(bf16)
    part_out = dot(act, w_down[...])
    part_gn = dot_nt(grad, w_up[...])

    @pl.when(step == 0)
    def _():
        ff_out[...] = part_out
        gn_acc[...] = part_gn

    @pl.when(step > 0)
    def _():
        ff_out[...] += part_out
        gn_acc[...] += part_gn

    @pl.when(step == last)
    def _():
        gn3[...] = gn_acc[...].astype(bf16)


def feed_forward(rank, n3_pieces, cot_pieces, w_up, w_down):
    count = (len(n3_pieces) + 1) // 2
    rows, width = n3_pieces[0].shape
    rows = rows * count
    hidden = w_up.shape[1]
    block = min(512, hidden)
    fixed = pl.BlockSpec((rows, width), lambda i, r: (0, 0))
    anywhere = pl.BlockSpec(memory_space=pl.ANY)
    grid_spec = pltpu.PrefetchScalarGridSpec(
        num_scalar_prefetch=1,
        grid=(hidden // block,),
        in_specs=[anywhere] * (2 * len(n3_pieces))
        + [
            pl.BlockSpec((width, block), lambda i, r: (0, i)),
            pl.BlockSpec((block, width), lambda i, r: (i, 0)),
        ],
        out_specs=[
            fixed,
            fixed,
            pl.BlockSpec((width, block), lambda i, r: (0, i)),
            pl.BlockSpec((block, width), lambda i, r: (i, 0)),
            fixed,
        ],
        scratch_shapes=[
            pltpu.VMEM((rows, width), bf16),
            pltpu.VMEM((rows, width), f32),
            pltpu.SemaphoreType.DMA((2, len(n3_pieces))),
        ],
    )
    return pl.pallas_call(
        functools.partial(ff_kernel, count),
        grid_spec=grid_spec,
        out_shape=(
            jax.ShapeDtypeStruct((rows, width), f32),
            jax.ShapeDtypeStruct((rows, width), bf16),
            jax.ShapeDtypeStruct((width, hidden), bf16),
            jax.ShapeDtypeStruct((hidden, width), bf16),
            jax.ShapeDtypeStruct((rows, width), bf16),
        ),
        compiler_params=params(60),
        cost_estimate=small_cost,
        name="feed_forward",
    )(rank, *n3_pieces, *cot_pieces, w_up, w_down)


def turn(x, same, down, up):
    return x * same + pltpu.roll(x, HD - HALF, 1) * down + pltpu.roll(x, HALF, 1) * up


def rotated(x, same, down, up):
    heads = [
        turn(x[:, h : h + HD], same, down, up).astype(bf16) for h in range(0, x.shape[1], HD)
    ]
    return jnp.concatenate(heads, axis=1)


def query_kernel(n, w, same, down, up, out):
    out[...] = rotated(dot(n[...], w[...]), same[...], down[...], up[...])


def key_value_kernel(n, wk, wv, same, down, up, key, value):
    width = wk.shape[0]
    key[...] = rotated(dot(n[:, 0:width], wk[...]), same[...], down[...], up[...])
    value[...] = dot(n[:, width : 2 * width], wv[...]).astype(bf16)


def project(kernel, n, weights, tables, outs, name):
    rows = n.shape[0]
    width, local = weights[0].shape
    block = min(256, rows)
    spec = lambda cols: pl.BlockSpec((block, cols), lambda i: (i, 0))
    return pl.pallas_call(
        kernel,
        grid=(rows // block,),
        out_shape=tuple(jax.ShapeDtypeStruct((rows, local), bf16) for _ in range(outs)),
        in_specs=[spec(n.shape[1])]
        + [pl.BlockSpec((width, local), lambda i: (0, 0))] * len(weights)
        + [spec(HD)] * 3,
        out_specs=tuple(spec(local) for _ in range(outs)),
        compiler_params=params(48),
        cost_estimate=small_cost,
        name=name,
    )(n, *weights, *tables)


def rope_lanes(positions):
    frequency = rope_base ** (-(jnp.arange(HALF, dtype=f32) * 2.0 / ROT))
    angles = positions.astype(f32)[:, None] * frequency[None, :]
    cos, sin = jnp.cos(angles), jnp.sin(angles)
    rows = positions.shape[0]
    ones = jnp.ones((rows, HD - ROT), f32)
    zeros = jnp.zeros((rows, HD - HALF), f32)
    same = jnp.concatenate([cos, cos, ones], axis=1)
    down = jnp.concatenate([-sin, zeros], axis=1)
    up = jnp.concatenate([zeros[:, :HALF], sin, zeros[:, : HD - ROT]], axis=1)
    return (same, down, up)


def hide(kb, block, span, bias):
    place = lax.broadcasted_iota(jnp.int32, bias.shape, 0) + kb * block
    seen = (place >= span[0:1, :]) & (place <= span[1:2, :])
    bias[...] = jnp.where(seen, 0.0, hidden_mask)


def take(step, sources, target):
    for i, source in enumerate(sources):

        @pl.when(step == i)
        def _(source=source):
            target[...] = source[...]


def attend_kernel(scale2, heads, blocks, info, offsets, q, span, *refs):
    keys, values = refs[:blocks], refs[blocks : 2 * blocks]
    out, lse, peak, total, acc, bias, k, v = refs[2 * blocks :]
    step = pl.program_id(0)
    rank, reach = info[0], info[1]
    kb = offsets[step]
    block = k.shape[0]

    @pl.when(step == 0)
    def _():
        peak[...] = jnp.full_like(peak, hidden_mask)
        total[...] = jnp.zeros_like(total)
        acc[...] = jnp.zeros_like(acc)

    def update(extra):
        for h in range(heads):
            lanes = slice(h * HD, (h + 1) * HD)
            one = slice(h, h + 1)
            scores = dot_nt(k[:, lanes], q[:, lanes]) * scale2
            if extra is not None:
                scores = scores + extra[...]
            old = peak[one, :]
            new = jnp.maximum(old, jnp.max(scores, axis=0, keepdims=True))
            weights = jnp.exp2(scores - new)
            factor = jnp.exp2(old - new)
            peak[one, :] = new
            total[one, :] = total[one, :] * factor + jnp.sum(weights, axis=0, keepdims=True)
            acc[lanes, :] = acc[lanes, :] * factor + dot_tn(v[:, lanes], weights.astype(bf16))

    needs = (kb == rank) | (reach > kb * block)

    @pl.when(kb <= rank)
    def _():
        take(step, keys, k)
        take(step, values, v)

    @pl.when((kb <= rank) & jnp.logical_not(needs))
    def _():
        update(None)

    @pl.when((kb <= rank) & needs)
    def _():
        hide(kb, block, span, bias)
        update(bias)

    @pl.when(step == pl.num_programs(0) - 1)
    def _():
        for h in range(heads):
            lanes = slice(h * HD, (h + 1) * HD)
            one = slice(h, h + 1)
            out[:, lanes] = jnp.transpose(acc[lanes, :] / total[one, :]).astype(bf16)
            lse[one, :] = peak[one, :] + jnp.log2(total[one, :])


def attend(q, keys, values, info, offsets, span):
    rows, local = q.shape
    heads = local // HD
    block = keys[0].shape[0]
    blocks = len(keys)
    scale2 = HD ** (-0.5) * log2e
    fixed = lambda shape: pl.BlockSpec(shape, lambda b, info, at: (0, 0))
    grid_spec = pltpu.PrefetchScalarGridSpec(
        num_scalar_prefetch=2,
        grid=(blocks,),
        in_specs=[fixed((rows, local)), fixed((8, rows))] + [fixed((block, local))] * (2 * blocks),
        out_specs=[fixed((rows, local)), fixed((8, rows))],
        scratch_shapes=[
            pltpu.VMEM((8, rows), f32),
            pltpu.VMEM((8, rows), f32),
            pltpu.VMEM((local, rows), f32),
            pltpu.VMEM((block, rows), f32),
            pltpu.VMEM((block, local), bf16),
            pltpu.VMEM((block, local), bf16),
        ],
    )
    return pl.pallas_call(
        functools.partial(attend_kernel, scale2, heads, blocks),
        grid_spec=grid_spec,
        out_shape=(
            jax.ShapeDtypeStruct((rows, local), bf16),
            jax.ShapeDtypeStruct((8, rows), f32),
        ),
        compiler_params=params(56),
        cost_estimate=small_cost,
        name="attend",
    )(info, offsets, q, span, *keys, *values)


def attend_back_kernel(scale, scale2, heads, blocks, *refs):
    info, offsets, _, _ = refs[:4]
    q, do, o, lse, span, same, down, up = refs[4:12]
    keys, values = refs[12 : 12 + blocks], refs[12 + blocks : 12 + 2 * blocks]
    gq, gk_hi, gk_lo, gv_hi, gv_lo, delta, acc, bias, k, v = refs[12 + 2 * blocks :]
    step = pl.program_id(0)
    rank, reach = info[0], info[1]
    kb = offsets[step]
    block = k.shape[0]

    @pl.when(step == 0)
    def _():
        for h in range(heads):
            lanes = slice(h * HD, (h + 1) * HD)
            both = do[:, lanes].astype(f32) * o[:, lanes].astype(f32)
            delta[h : h + 1, :] = jnp.sum(jnp.transpose(both), axis=0, keepdims=True)
        acc[...] = jnp.zeros_like(acc)

    def update(extra, gk, gv):
        for h in range(heads):
            lanes = slice(h * HD, (h + 1) * HD)
            one = slice(h, h + 1)
            scores = dot_nt(k[:, lanes], q[:, lanes]) * scale2
            if extra is not None:
                scores = scores + extra[...]
            weights = jnp.exp2(scores - lse[one, :])
            gv[:, lanes] = dot(weights.astype(bf16), do[:, lanes]).astype(bf16)
            grad_weights = dot_nt(v[:, lanes], do[:, lanes])
            grad_scores = (weights * (grad_weights - delta[one, :])).astype(bf16)
            gk[:, lanes] = (dot(grad_scores, q[:, lanes]) * scale).astype(bf16)
            acc[lanes, :] += dot_tn(k[:, lanes], grad_scores)

    needs = (kb == rank) | (reach > kb * block)

    @pl.when(kb <= rank)
    def _():
        take(step, keys, k)
        take(step, values, v)

    for high, gk, gv in ((True, gk_hi, gv_hi), (False, gk_lo, gv_lo)):
        here = (step < blocks // 2) if high else (step >= blocks // 2)

        @pl.when(here & (kb <= rank) & jnp.logical_not(needs))
        def _(gk=gk, gv=gv):
            update(None, gk, gv)

        @pl.when(here & (kb <= rank) & needs)
        def _(gk=gk, gv=gv):
            hide(kb, block, span, bias)
            update(bias, gk, gv)

        @pl.when(here & (kb > rank))
        def _(gk=gk, gv=gv):
            gk[...] = jnp.zeros_like(gk)
            gv[...] = jnp.zeros_like(gv)

    @pl.when(step == pl.num_programs(0) - 1)
    def _():
        for h in range(heads):
            lanes = slice(h * HD, (h + 1) * HD)
            x = jnp.transpose(acc[lanes, :]) * scale
            gq[:, lanes] = turn(x, same[...], -down[...], -up[...]).astype(bf16)


def attend_back(q, keys, values, do, o, lse, info, offsets, key_at, value_at, span, tables):
    rows, local = q.shape
    heads = local // HD
    block = keys[0].shape[0]
    blocks = len(keys)
    half = blocks // 2
    scale = HD ** (-0.5)
    fixed = lambda shape: pl.BlockSpec(shape, lambda b, info, at, ks, vs: (0, 0))
    high = lambda pick: pl.BlockSpec(
        (block, local), lambda b, info, at, ks, vs: ((ks, vs)[pick][jnp.minimum(b, half - 1)] - half, 0)
    )
    low = lambda pick: pl.BlockSpec(
        (block, local), lambda b, info, at, ks, vs: ((ks, vs)[pick][jnp.maximum(b, half)], 0)
    )
    grid_spec = pltpu.PrefetchScalarGridSpec(
        num_scalar_prefetch=4,
        grid=(blocks,),
        in_specs=[fixed((rows, local))] * 3
        + [fixed((8, rows))] * 2
        + [fixed((rows, HD))] * 3
        + [fixed((block, local))] * (2 * blocks),
        out_specs=[fixed((rows, local)), high(0), low(0), high(1), low(1)],
        scratch_shapes=[
            pltpu.VMEM((8, rows), f32),
            pltpu.VMEM((local, rows), f32),
            pltpu.VMEM((block, rows), f32),
            pltpu.VMEM((block, local), bf16),
            pltpu.VMEM((block, local), bf16),
        ],
    )
    part = jax.ShapeDtypeStruct((half * block, local), bf16)
    return pl.pallas_call(
        functools.partial(attend_back_kernel, scale, scale * log2e, heads, blocks),
        grid_spec=grid_spec,
        out_shape=(jax.ShapeDtypeStruct((rows, local), bf16), part, part, part, part),
        compiler_params=params(60),
        cost_estimate=small_cost,
        name="attend_back",
    )(info, offsets, key_at, value_at, q, do, o, lse, span, *tables, *keys, *values)


def key_value_back_kernel(terms, *refs):
    gk_parts, gv_parts = refs[:terms], refs[terms : 2 * terms]
    wk, wv, same, down, up, gk, gv, gn = refs[2 * terms :]
    width = wk.shape[0]
    add = lambda parts: functools.reduce(lambda a, b: a + b, [p[...].astype(f32) for p in parts])
    gk[...] = rotated(add(gk_parts), same[...], -down[...], -up[...])
    gv[...] = add(gv_parts).astype(bf16)
    gn[:, 0:width] = dot_nt(gk[...], wk[...]).astype(bf16)
    gn[:, width : 2 * width] = dot_nt(gv[...], wv[...]).astype(bf16)


def key_value_back(gk_parts, gv_parts, wk, wv, tables):
    rows = tables[0].shape[0]
    local = gk_parts[0].shape[1]
    width = wk.shape[0]
    block = min(256, rows)
    spec = lambda cols: pl.BlockSpec((block, cols), lambda i: (i, 0))
    whole = pl.BlockSpec((width, local), lambda i: (0, 0))
    return pl.pallas_call(
        functools.partial(key_value_back_kernel, len(gk_parts)),
        grid=(rows // block,),
        out_shape=(
            jax.ShapeDtypeStruct((rows, local), bf16),
            jax.ShapeDtypeStruct((rows, local), bf16),
            jax.ShapeDtypeStruct((rows, 2 * width), bf16),
        ),
        in_specs=[spec(local)] * (2 * len(gk_parts)) + [whole] * 2 + [spec(HD)] * 3,
        out_specs=[spec(local), spec(local), spec(2 * width)],
        compiler_params=params(48),
        cost_estimate=small_cost,
        name="key_value_back",
    )(*gk_parts, *gv_parts, wk, wv, *tables)


def weight_grad_kernel(half, core, nq, nk, nv, cot, gq, gk, gv, att, send_a, own_a, send_b, own_b):
    step = pl.program_id(0)
    local = gq.shape[1]

    def fill(a, b):
        a[:, 0:local] = dot_tn(nq[...], gq[...]).astype(bf16)
        a[:, local : 2 * local] = dot_tn(nk[...], gk[...]).astype(bf16)
        b[:, 0:local] = dot_tn(nv[...], gv[...]).astype(bf16)
        b[:, local : 2 * local] = dot_tn(cot[...], att[...]).astype(bf16)

    @pl.when(step < half)
    def _():
        fill(send_a, send_b)

    @pl.when(step >= half)
    def _():
        fill(own_a, own_b)


def weight_grads(core, nq, nkv, cot, gq, gk, gv, att):
    rows, width = nq.shape
    local = gq.shape[1]
    block = 256
    steps = width // block
    half = steps // 2
    column = lambda i, core: jnp.where(i < half, (1 - core[0]) * half + i, core[0] * half + i - half)
    lhs = lambda shift: pl.BlockSpec((rows, block), lambda i, core: (0, column(i, core) + shift))
    rhs = pl.BlockSpec((rows, local), lambda i, core: (0, 0))
    out = jax.ShapeDtypeStruct((width // 2, 2 * local), bf16)
    first = pl.BlockSpec((block, 2 * local), lambda i, core: (jnp.minimum(i, half - 1), 0))
    second = pl.BlockSpec((block, 2 * local), lambda i, core: (jnp.maximum(i - half, 0), 0))
    grid_spec = pltpu.PrefetchScalarGridSpec(
        num_scalar_prefetch=1,
        grid=(steps,),
        in_specs=[lhs(0), lhs(0), lhs(steps), lhs(0)] + [rhs] * 4,
        out_specs=[first, second, first, second],
    )
    return pl.pallas_call(
        functools.partial(weight_grad_kernel, half),
        grid_spec=grid_spec,
        out_shape=(out, out, out, out),
        compiler_params=params(48),
        cost_estimate=small_cost,
        name="weight_grads",
    )(core, nq, nkv, nkv, cot, gq, gk, gv, att)


def assemble_kernel(half, local, a_slot, b_slot, a_lo, a_hi, b_lo, b_hi, gwq, gwk, gwv, gwo):
    r = pl.program_id(0)

    @pl.when(a_slot[r] < half)
    def _():
        gwq[...] = a_lo[:, 0:local].astype(f32)
        gwk[...] = a_lo[:, local : 2 * local].astype(f32)

    @pl.when(a_slot[r] >= half)
    def _():
        gwq[...] = a_hi[:, 0:local].astype(f32)
        gwk[...] = a_hi[:, local : 2 * local].astype(f32)

    @pl.when(b_slot[r] < half)
    def _():
        gwv[...] = b_lo[:, 0:local].astype(f32)
        gwo[...] = jnp.transpose(b_lo[:, local : 2 * local].astype(f32))

    @pl.when(b_slot[r] >= half)
    def _():
        gwv[...] = b_hi[:, 0:local].astype(f32)
        gwo[...] = jnp.transpose(b_hi[:, local : 2 * local].astype(f32))


def assemble(a_slot, b_slot, a_lo, a_hi, b_lo, b_hi, pieces):
    half = pieces // 2
    piece = a_lo.shape[0] // half
    local = a_lo.shape[1] // 2
    width = pieces * piece
    low = lambda pick: pl.BlockSpec(
        (piece, 2 * local), lambda i, a, b: (jnp.minimum((a, b)[pick][i], half - 1), 0)
    )
    high = lambda pick: pl.BlockSpec(
        (piece, 2 * local), lambda i, a, b: (jnp.maximum((a, b)[pick][i] - half, 0), 0)
    )
    rowed = pl.BlockSpec((piece, local), lambda i, a, b: (i, 0))
    tall = jax.ShapeDtypeStruct((width, local), f32)
    grid_spec = pltpu.PrefetchScalarGridSpec(
        num_scalar_prefetch=2,
        grid=(pieces,),
        in_specs=[low(0), high(0), low(1), high(1)],
        out_specs=[rowed, rowed, rowed, pl.BlockSpec((local, piece), lambda i, a, b: (0, i))],
    )
    return pl.pallas_call(
        functools.partial(assemble_kernel, half, local),
        grid_spec=grid_spec,
        out_shape=(tall, tall, tall, jax.ShapeDtypeStruct((local, width), f32)),
        compiler_params=params(32),
        name="assemble",
    )(a_slot, b_slot, a_lo, a_hi, b_lo, b_hi)


def flipped(x, axis, bit, sender=None):
    count = lax.axis_size(axis)
    sends = [i for i in range(count) if sender is None or bool(i & bit) == sender]
    return lax.ppermute(x, axis, [(i, i ^ bit) for i in sends])


def top(bit):
    return 2 * bit == lax.axis_size("seq")


def bits_of(count):
    bits = []
    while (1 << len(bits)) < count:
        bits.append(1 << len(bits))
    return bits


def slot_order(bits):
    order = [0]
    for bit in bits:
        order = order + [m | bit for m in order]
    return order


def collect(block, bits):
    held = {0: block}
    for bit in bits:
        sender = False if top(bit) else None
        held.update({m | bit: flipped(x, "seq", bit, sender) for m, x in held.items()})
    return held


def summed(a, b):
    return (a.astype(f32) + b.astype(f32)).astype(bf16)


def disperse(low, high, bits):
    terms = [low, flipped(high, "seq", bits[-1], True if top(bits[-1]) else None)]
    half = low.shape[0] // 2
    for bit in reversed(bits[:-1]):
        total = functools.reduce(lambda a, b: a + b, [t[half : 2 * half].astype(f32) for t in terms])
        terms.append(flipped(total.astype(bf16), "seq", bit, True if top(bit) else None))
        half = half // 2
    return terms


def reduced(own, got, bits, rank, midway):
    for at, bit in enumerate(bits):
        half = own.shape[0] // 2
        side = (rank & bit) // bit
        cut = lambda x, at: lax.dynamic_slice_in_dim(x, at * half, half)
        send = summed(cut(own, 1 - side), cut(got, 1 - side))
        if at == len(bits) - 1:
            send = after(send, midway)
        own = summed(cut(own, side), cut(got, side))
        got = flipped(send, "seq", bit)
    return summed(own, got)


def spread(piece, bits):
    held = piece
    for bit in bits[:-1]:
        held = jnp.concatenate([held, flipped(held, "seq", bit)], axis=0)
    return held, flipped(held, "seq", bits[-1])


def piece_slots(bits, rank, count):
    order = slot_order(bits[::-1])
    table = [0] * count
    for slot, m in enumerate(order):
        table[m] = slot
    owners = []
    for r in range(count):
        owner = 0
        for at, bit in enumerate(bits):
            if (r >> (len(bits) - 1 - at)) & 1:
                owner |= bit
        owners.append(owner)
    return jnp.take(jnp.array(table, jnp.int32), jnp.array(owners, jnp.int32) ^ rank)


def ring(x, axis):
    count = lax.axis_size(axis)
    from_below, from_above = [], []
    up = down = x
    for k in range(1, count):
        up = lax.ppermute(up, axis, [(i, i + 1) for i in range(k - 1, count - 1)])
        down = lax.ppermute(down, axis, [(i, i - 1) for i in range(1, count - k + 1)])
        from_below.append(up)
        from_above.append(down)
    return from_below + from_above


def after(x, *earlier):
    anywhere = pl.BlockSpec(memory_space=pl.ANY)
    return pl.pallas_call(
        lambda *refs: None,
        out_shape=jax.ShapeDtypeStruct(x.shape, x.dtype),
        in_specs=[anywhere] * (1 + len(earlier)),
        out_specs=anywhere,
        input_output_aliases={0: 0},
        name="after",
    )(x, *earlier)


def small_sum(x):
    x = x.astype(bf16)
    for axis in ("head", "seq"):
        for bit in bits_of(lax.axis_size(axis)):
            x = summed(x, flipped(x, axis, bit))
    return x.astype(f32)


def body(
    histories,
    norm_gains,
    mix_in,
    mix_out,
    mix_bias,
    w_query,
    w_key,
    w_value,
    w_out,
    w_up,
    w_down,
    cotangent,
    doc_ids,
    positions,
):
    seq_count = lax.axis_size("seq")
    rank = lax.axis_index("seq")
    block_rows = positions.shape[0]
    hist_count, tok_rows, width = histories.shape
    count = norm_gains.shape[0]
    units = mix_in.shape[1]
    mixes = mix_out.shape[1]

    def gather(x):
        return lax.all_gather(x, "head", axis=0, tiled=True)

    def scatter(x):
        return lax.psum_scatter(x, "head", scatter_dimension=0, tiled=True)

    tables = rope_lanes(positions)
    place = rank * block_rows + jnp.arange(block_rows, dtype=jnp.int32)
    first = place - positions
    span = jnp.concatenate([first[None], place[None], jnp.zeros((6, block_rows), jnp.int32)], axis=0)
    info = jnp.stack([rank.astype(jnp.int32), jnp.max(first)])
    bits = bits_of(seq_count)
    key_bits = bits[1:] + bits[:1]
    value_bits = bits[1:][::-1] + bits[:1]
    key_order = slot_order(key_bits)
    value_order = slot_order(value_bits)
    half = seq_count // 2
    order = key_order[half:] + key_order[:half]
    offsets = jnp.array(order, jnp.int32) ^ rank
    key_at = jnp.array([key_order.index(m) for m in order], jnp.int32)
    value_at = jnp.array([value_order.index(m) for m in order], jnp.int32)
    same, down, up = tables
    core = (rank & 1)[None].astype(jnp.int32)
    cot_pieces = [cotangent] + ring(cotangent, "head")
    n3, nkv, nq, streams, coef, mix_pre = mix_forward(
        histories, norm_gains, mix_in, mix_out, mix_bias[None, :]
    )
    n3_pieces = [n3] + ring(n3, "head")
    nkv_full = gather(after(nkv, *n3_pieces[1:], *cot_pieces[1:]))
    nq_full = gather(nq)
    ff_out, gn3_part, gw_up, gw_down, cot_full = feed_forward(
        lax.axis_index("head")[None], n3_pieces, cot_pieces, w_up, w_down
    )
    gn3 = scatter(gn3_part)
    gw_up, gw_down = lax.psum((gw_up, gw_down), "seq")
    key, value = project(
        key_value_kernel, nkv_full, (w_key, w_value), (after(same, gn3_part), down, up), 2, "project_kv"
    )
    (query,) = project(query_kernel, nq_full, (w_query,), tables, 1, "project_q")
    keys = collect(key, key_bits)
    values = collect(value, value_bits)
    keys, values = [keys[m] for m in order], [values[m] for m in order]
    attended, lse = attend(query, keys, values, info, offsets, span)
    branch = scatter((ff_out + dot(attended, w_out)).astype(bf16))
    layer_out = (streams[3] + branch.astype(f32)).astype(bf16)
    do = dot_nt(cot_full, w_out).astype(bf16)
    gq, gk_hi, gk_lo, gv_hi, gv_lo = attend_back(
        query,
        keys,
        values,
        do,
        attended,
        lse,
        info,
        offsets,
        key_at,
        value_at,
        span,
        tables,
    )
    gnq = scatter(dot_nt(gq, w_query).astype(bf16))
    gk, gv, gnkv_part = key_value_back(
        disperse(gk_lo, gk_hi, key_bits),
        disperse(gv_lo, gv_hi, value_bits),
        w_key,
        w_value,
        (after(same, gn3), down, up),
    )
    gnkv = scatter(gnkv_part)
    send_a, own_a, send_b, own_b = weight_grads(
        core, nq_full, nkv_full, cot_full, gq, gk, after(gv, gw_up, gw_down), attended
    )
    got_a = flipped(send_a, "seq", 1)
    got_b = flipped(send_b, "seq", 1)
    a_bits = bits[1:]
    b_bits = bits[1:][::-1]
    gw_up, gw_down = gw_up.astype(f32), gw_down.astype(f32)
    piece_a = reduced(own_a, got_a, a_bits, rank, gw_up)
    piece_b = after(reduced(own_b, got_b, b_bits, rank, gw_up), gw_down)
    a_lo, a_hi = spread(piece_a, a_bits[::-1] + bits[:1])
    b_lo, b_hi = spread(piece_b, b_bits[::-1] + bits[:1])
    gwq, gwk, gwv, gwo = assemble(
        piece_slots(bits[:1] + a_bits, rank, seq_count),
        piece_slots(bits[:1] + b_bits, rank, seq_count),
        a_lo,
        a_hi,
        b_lo,
        b_hi,
        seq_count,
    )
    coef = after(coef, layer_out)
    ghist, pack = unmix(
        histories, streams, gn3, gnkv, gnq, cotangent, coef, mix_pre, norm_gains, mix_in, mix_out
    )
    pack = small_sum(pack)
    return (
        layer_out,
        ghist,
        pack[units : units + count, :width],
        jnp.transpose(pack[:units, :width]),
        pack[:units, width : width + mixes],
        pack[units, width : width + mixes],
        gwq,
        gwk,
        gwv,
        gwo,
        gw_up,
        gw_down,
    )


def solution(mesh):
    return jax.shard_map(
        body,
        mesh=mesh,
        in_specs=(
            P(None, ("seq", "head"), None),
            P(),
            P(),
            P(),
            P(),
            P(None, "head"),
            P(None, "head"),
            P(None, "head"),
            P("head", None),
            P(None, "head"),
            P("head", None),
            P(("seq", "head"), None),
            P(),
            P("seq"),
        ),
        out_specs=(
            P(("seq", "head"), None),
            P(None, ("seq", "head"), None),
            P(),
            P(),
            P(),
            P(),
            P(None, "head"),
            P(None, "head"),
            P(None, "head"),
            P("head", None),
            P(None, "head"),
            P("head", None),
        ),
        check_vma=False,
    )
```

```python
import functools

import jax
import jax.numpy as jnp
from jax import lax
from jax.experimental import pallas as pl
from jax.experimental.pallas import tpu as pltpu
from jax.sharding import PartitionSpec as P

HD = 128
ROT = 32
HALF = ROT // 2
MIB = 1024 * 1024

eps_norm = 1e-05
eps_rms = 1e-06
rope_base = 10000.0
hidden_mask = -1e30
highest = lax.Precision.HIGHEST
f32 = jnp.float32
bf16 = jnp.bfloat16
sqrt_half = 0.7071067811865476
inv_sqrt_2pi = 0.3989422804014327
log2e = 1.4426950408889634
small_cost = pl.CostEstimate(flops=MIB, bytes_accessed=MIB, transcendentals=0)


def vmem():
    return pl.BlockSpec(memory_space=pltpu.VMEM)


def params(mib, **more):
    return pltpu.CompilerParams(vmem_limit_bytes=60 * MIB, **more)


def cdf(x):
    return 0.5 * (1.0 + lax.erf(x * sqrt_half))


def pdf(x):
    return jnp.exp(x * x * -0.5) * inv_sqrt_2pi


def dot(a, b):
    return jnp.dot(a, b, preferred_element_type=f32)


def dot_nt(a, b):
    return lax.dot_general(a, b, (((1,), (1,)), ((), ())), preferred_element_type=f32)


def dot_tn(a, b):
    return lax.dot_general(a, b, (((0,), (0,)), ((), ())), preferred_element_type=f32)


def mix_kernel(tile, hist, gains, mix_in, mix_out, mix_bias, n3, nkv, nq, streams, coef, mix_pre):
    hist_count, rows, width = hist.shape
    count = gains.shape[0]
    newest = hist[hist_count - 1].astype(f32)
    scale = lax.rsqrt(jnp.mean(newest * newest, axis=-1, keepdims=True) + eps_rms)
    rms_low = (newest * scale).astype(bf16)
    pre = dot(rms_low, mix_in[...])
    mix_pre[...] = pre
    hidden = (pre * cdf(pre)).astype(bf16)
    coef[...] = dot(hidden, mix_out[...]) + mix_bias[...]
    chunk = 512

    def step(i, carry):
        at = pl.ds(pl.multiple_of(i * tile, tile), tile)
        rows_coef = coef[at, :]
        columns = [
            [rows_coef[:, c * hist_count + j : c * hist_count + j + 1] for j in range(hist_count)]
            for c in range(count)
        ]
        totals = [jnp.zeros((tile, 1), f32) for _ in range(count)]
        for lane in range(0, width, chunk):
            sums = [jnp.zeros((tile, chunk), f32) for _ in range(count)]
            for j in range(hist_count):
                h = hist[j, at, lane : lane + chunk].astype(f32)
                for c in range(count):
                    sums[c] = sums[c] + columns[c][j] * h
            for c in range(count):
                streams[c, at, lane : lane + chunk] = sums[c]
                totals[c] = totals[c] + jnp.sum(sums[c], axis=-1, keepdims=True)
        for c in range(count):
            x = streams[c, at, :]
            centre = x - totals[c] * (1.0 / width)
            spread = jnp.mean(centre * centre, axis=-1, keepdims=True)
            out = (centre * lax.rsqrt(spread + eps_norm) * gains[c : c + 1, :]).astype(bf16)
            if c == 0:
                nq[at, :] = out
            elif c == 3:
                n3[at, :] = out
            else:
                nkv[at, (c - 1) * width : c * width] = out
        return carry

    lax.fori_loop(0, rows // tile, step, 0)


def mix_forward(histories, norm_gains, mix_in, mix_out, mix_bias):
    hist_count, rows, width = histories.shape
    count = norm_gains.shape[0]
    return pl.pallas_call(
        functools.partial(mix_kernel, 16),
        out_shape=(
            jax.ShapeDtypeStruct((rows, width), bf16),
            jax.ShapeDtypeStruct((rows, 2 * width), bf16),
            jax.ShapeDtypeStruct((rows, width), bf16),
            jax.ShapeDtypeStruct((count, rows, width), f32),
            jax.ShapeDtypeStruct((rows, count * hist_count), f32),
            jax.ShapeDtypeStruct((rows, mix_in.shape[1]), f32),
        ),
        in_specs=[vmem()] * 5,
        out_specs=[vmem()] * 6,
        compiler_params=params(48),
        name="mix_forward",
    )(histories, norm_gains, mix_in, mix_out, mix_bias)


def unmix_kernel(
    hist, streams, gn3, gnkv, gnq, cot, coef, mix_pre, gains, mix_in, mix_out, ghist, pack, gs, rms_keep, hid_keep, gc_keep, gmp_keep
):
    hist_count, tile, width = hist.shape
    count = gains.shape[0]
    hidden_units = mix_in.shape[1]
    step = pl.program_id(0)

    @pl.when(step == 0)
    def _():
        pack[...] = jnp.zeros_like(pack)

    for c in range(count):
        x = streams[c]
        centre = x - jnp.mean(x, axis=-1, keepdims=True)
        inv = lax.rsqrt(jnp.mean(centre * centre, axis=-1, keepdims=True) + eps_norm)
        unit = centre * inv
        if c == 0:
            g = gnq[...].astype(f32)
        elif c == 3:
            g = gn3[...].astype(f32)
        else:
            g = gnkv[:, (c - 1) * width : c * width].astype(f32)
        pack[hidden_units + c : hidden_units + c + 1, 0:width] += jnp.sum(g * unit, axis=0, keepdims=True)
        d = g * gains[c : c + 1, :]
        out = inv * (
            d
            - jnp.mean(d, axis=-1, keepdims=True)
            - unit * jnp.mean(d * unit, axis=-1, keepdims=True)
        )
        if c == 3:
            out = out + cot[...].astype(f32)
        gs[c] = out
    lanes = lax.broadcasted_iota(jnp.int32, (tile, count * hist_count), 1)
    gc = jnp.zeros((tile, count * hist_count), f32)
    rows_coef = coef[...]
    for j in range(hist_count):
        h = hist[j].astype(f32)
        for c in range(count):
            k = c * hist_count + j
            gc = jnp.where(lanes == k, jnp.sum(gs[c] * h, axis=-1, keepdims=True), gc)
    for j in range(hist_count):
        total = rows_coef[:, j : j + 1] * gs[0]
        for c in range(1, count):
            k = c * hist_count + j
            total = total + rows_coef[:, k : k + 1] * gs[c]
        if j < hist_count - 1:
            ghist[j] = total.astype(bf16)
    pre = mix_pre[...]
    phi = cdf(pre)
    gmh = lax.dot_general(
        gc, mix_out[...].astype(f32), (((1,), (1,)), ((), ())), precision=highest
    )
    gmp = (phi + pre * pdf(pre)) * gmh
    gmp_low = gmp.astype(bf16)
    grad_rms = dot_nt(gmp_low, mix_in[...])
    newest = hist[hist_count - 1].astype(f32)
    scale = lax.rsqrt(jnp.mean(newest * newest, axis=-1, keepdims=True) + eps_rms)
    inner = jnp.mean(grad_rms * newest, axis=-1, keepdims=True)
    total = total + scale * grad_rms - newest * (scale * scale * scale * inner)
    ghist[hist_count - 1] = total.astype(bf16)
    at = pl.ds(pl.multiple_of(step * tile, tile), tile)
    rms_keep[at, :] = (newest * scale).astype(bf16)
    hid_keep[at, :] = (pre * phi).astype(bf16).astype(f32)
    gc_keep[at, :] = gc
    gmp_keep[at, :] = gmp_low

    @pl.when(step == pl.num_programs(0) - 1)
    def _():
        pack[0:hidden_units, 0:width] = dot_tn(gmp_keep[...], rms_keep[...])
        pack[0:hidden_units, width : width + count * hist_count] = lax.dot_general(
            hid_keep[...], gc_keep[...], (((0,), (0,)), ((), ())), precision=highest
        )
        pack[hidden_units : hidden_units + 1, width : width + count * hist_count] = jnp.sum(
            gc_keep[...], axis=0, keepdims=True
        )


def unmix(histories, streams, gn3, gnkv, gnq, cotangent, coef, mix_pre, norm_gains, mix_in, mix_out):
    hist_count, rows, width = histories.shape
    count = norm_gains.shape[0]
    units = mix_in.shape[1]
    mixes = count * hist_count
    tile = 32
    whole = lambda shape: pl.BlockSpec(shape, lambda i: (0, 0))
    return pl.pallas_call(
        unmix_kernel,
        grid=(rows // tile,),
        out_shape=(
            jax.ShapeDtypeStruct((hist_count, rows, width), bf16),
            jax.ShapeDtypeStruct((units + 8, width + 128), f32),
        ),
        in_specs=[
            pl.BlockSpec((hist_count, tile, width), lambda i: (0, i, 0)),
            pl.BlockSpec((count, tile, width), lambda i: (0, i, 0)),
            pl.BlockSpec((tile, width), lambda i: (i, 0)),
            pl.BlockSpec((tile, 2 * width), lambda i: (i, 0)),
            pl.BlockSpec((tile, width), lambda i: (i, 0)),
            pl.BlockSpec((tile, width), lambda i: (i, 0)),
            pl.BlockSpec((tile, mixes), lambda i: (i, 0)),
            pl.BlockSpec((tile, units), lambda i: (i, 0)),
            whole((count, width)),
            whole((width, units)),
            whole((units, mixes)),
        ],
        out_specs=[
            pl.BlockSpec((hist_count, tile, width), lambda i: (0, i, 0)),
            whole((units + 8, width + 128)),
        ],
        scratch_shapes=[
            pltpu.VMEM((count, tile, width), f32),
            pltpu.VMEM((rows, width), bf16),
            pltpu.VMEM((rows, units), f32),
            pltpu.VMEM((rows, mixes), f32),
            pltpu.VMEM((rows, units), bf16),
        ],
        compiler_params=params(48),
        name="unmix",
    )(histories, streams, gn3, gnkv, gnq, cotangent, coef, mix_pre, norm_gains, mix_in, mix_out)


def ff_kernel(count, rank_ref, *refs):
    pieces = 2 * count - 1
    sources = (refs[:pieces], refs[pieces : 2 * pieces])
    w_up, w_down, act, grad, gw_up, gw_down, cot, n3, sems = refs[2 * pieces :]
    step = pl.program_id(0)

    @pl.when(step == 0)
    def _():
        rank = rank_ref[0]

        def each(act):
            for which, target in ((0, n3), (1, cot)):
                rows = target.shape[0] // count
                for at in range(pieces):
                    if at == 0:
                        block, there = rank, None
                    elif at < count:
                        block, there = rank - at, rank >= at
                    else:
                        k = at - count + 1
                        block, there = rank + k, rank + k < count

                    def one(block=block, at=at):
                        to = target.at[pl.ds(pl.multiple_of(block * rows, rows), rows), :]
                        act(pltpu.make_async_copy(sources[which][at], to, sems.at[which, at]))

                    if there is None:
                        one()
                    else:
                        pl.when(there)(one)

        each(lambda copy: copy.start())
        each(lambda copy: copy.wait())

    pre = dot(n3[...], w_up[...])
    phi = cdf(pre)
    act[...] = (pre * phi).astype(bf16)
    slope = phi + pre * pdf(pre)
    grad[...] = (dot_nt(cot[...], w_down[...]) * slope).astype(bf16)
    gw_down[...] = dot_tn(act[...], cot[...]).astype(bf16)
    gw_up[...] = dot_tn(n3[...], grad[...]).astype(bf16)


def feed_forward(rank, n3_pieces, cot_pieces, w_up, w_down):
    count = (len(n3_pieces) + 1) // 2
    rows, width = n3_pieces[0].shape
    rows = rows * count
    hidden = w_up.shape[1]
    block = min(512, hidden)
    fixed = pl.BlockSpec((rows, width), lambda i, r: (0, 0))
    anywhere = pl.BlockSpec(memory_space=pl.ANY)
    grid_spec = pltpu.PrefetchScalarGridSpec(
        num_scalar_prefetch=1,
        grid=(hidden // block,),
        in_specs=[anywhere] * (2 * len(n3_pieces))
        + [
            pl.BlockSpec((width, block), lambda i, r: (0, i)),
            pl.BlockSpec((block, width), lambda i, r: (i, 0)),
        ],
        out_specs=[
            pl.BlockSpec((rows, block), lambda i, r: (0, i)),
            pl.BlockSpec((rows, block), lambda i, r: (0, i)),
            pl.BlockSpec((width, block), lambda i, r: (0, i)),
            pl.BlockSpec((block, width), lambda i, r: (i, 0)),
            fixed,
        ],
        scratch_shapes=[
            pltpu.VMEM((rows, width), bf16),
            pltpu.SemaphoreType.DMA((2, len(n3_pieces))),
        ],
    )
    return pl.pallas_call(
        functools.partial(ff_kernel, count),
        grid_spec=grid_spec,
        out_shape=(
            jax.ShapeDtypeStruct((rows, hidden), bf16),
            jax.ShapeDtypeStruct((rows, hidden), bf16),
            jax.ShapeDtypeStruct((width, hidden), bf16),
            jax.ShapeDtypeStruct((hidden, width), bf16),
            jax.ShapeDtypeStruct((rows, width), bf16),
        ),
        compiler_params=params(60),
        cost_estimate=small_cost,
        name="feed_forward",
    )(rank, *n3_pieces, *cot_pieces, w_up, w_down)


def ff_sums_kernel(act, grad, w_up, w_down, ff_out, gn3):
    ff_out[...] = dot(act[...], w_down[...])
    gn3[...] = dot_nt(grad[...], w_up[...]).astype(bf16)


def feed_forward_sums(act, grad, w_up, w_down):
    rows, hidden = act.shape
    width = w_up.shape[0]
    block = min(512, width)
    fixed = pl.BlockSpec((rows, hidden), lambda i: (0, 0))
    out = pl.BlockSpec((rows, block), lambda i: (0, i))
    return pl.pallas_call(
        ff_sums_kernel,
        grid=(width // block,),
        out_shape=(
            jax.ShapeDtypeStruct((rows, width), f32),
            jax.ShapeDtypeStruct((rows, width), bf16),
        ),
        in_specs=[
            fixed,
            fixed,
            pl.BlockSpec((block, hidden), lambda i: (i, 0)),
            pl.BlockSpec((hidden, block), lambda i: (0, i)),
        ],
        out_specs=[out, out],
        compiler_params=params(56),
        cost_estimate=small_cost,
        name="feed_forward_sums",
    )(act, grad, w_up, w_down)


def turn(x, same, down, up):
    return x * same + pltpu.roll(x, HD - HALF, 1) * down + pltpu.roll(x, HALF, 1) * up


def rotated(x, same, down, up):
    heads = [
        turn(x[:, h : h + HD], same, down, up).astype(bf16) for h in range(0, x.shape[1], HD)
    ]
    return jnp.concatenate(heads, axis=1)


def query_kernel(n, w, same, down, up, out):
    out[...] = rotated(dot(n[...], w[...]), same[...], down[...], up[...])


def key_value_kernel(n, wk, wv, same, down, up, key, value):
    width = wk.shape[0]
    key[...] = rotated(dot(n[:, 0:width], wk[...]), same[...], down[...], up[...])
    value[...] = dot(n[:, width : 2 * width], wv[...]).astype(bf16)


def project(kernel, n, weights, tables, outs, name):
    rows = n.shape[0]
    width, local = weights[0].shape
    block = min(256, rows)
    spec = lambda cols: pl.BlockSpec((block, cols), lambda i: (i, 0))
    return pl.pallas_call(
        kernel,
        grid=(rows // block,),
        out_shape=tuple(jax.ShapeDtypeStruct((rows, local), bf16) for _ in range(outs)),
        in_specs=[spec(n.shape[1])]
        + [pl.BlockSpec((width, local), lambda i: (0, 0))] * len(weights)
        + [spec(HD)] * 3,
        out_specs=tuple(spec(local) for _ in range(outs)),
        compiler_params=params(48),
        cost_estimate=small_cost,
        name=name,
    )(n, *weights, *tables)


def rope_lanes(positions):
    frequency = rope_base ** (-(jnp.arange(HALF, dtype=f32) * 2.0 / ROT))
    angles = positions.astype(f32)[:, None] * frequency[None, :]
    cos, sin = jnp.cos(angles), jnp.sin(angles)
    rows = positions.shape[0]
    ones = jnp.ones((rows, HD - ROT), f32)
    zeros = jnp.zeros((rows, HD - HALF), f32)
    same = jnp.concatenate([cos, cos, ones], axis=1)
    down = jnp.concatenate([-sin, zeros], axis=1)
    up = jnp.concatenate([zeros[:, :HALF], sin, zeros[:, : HD - ROT]], axis=1)
    return (same, down, up)


def hide(kb, block, span, bias):
    place = lax.broadcasted_iota(jnp.int32, bias.shape, 0) + kb * block
    seen = (place >= span[0:1, :]) & (place <= span[1:2, :])
    bias[...] = jnp.where(seen, 0.0, hidden_mask)


def take(step, sources, target):
    for i, source in enumerate(sources):

        @pl.when(step == i)
        def _(source=source):
            target[...] = source[...]


def attend_kernel(scale2, heads, blocks, info, offsets, q, span, *refs):
    keys, values = refs[:blocks], refs[blocks : 2 * blocks]
    out, lse, peak, total, acc, bias, k, v = refs[2 * blocks :]
    step = pl.program_id(0)
    rank, reach = info[0], info[1]
    kb = offsets[step]
    block = k.shape[0]

    @pl.when(step == 0)
    def _():
        peak[...] = jnp.full_like(peak, hidden_mask)
        total[...] = jnp.zeros_like(total)
        acc[...] = jnp.zeros_like(acc)

    def update(extra):
        for h in range(heads):
            lanes = slice(h * HD, (h + 1) * HD)
            one = slice(h, h + 1)
            scores = dot_nt(k[:, lanes], q[:, lanes]) * scale2
            if extra is not None:
                scores = scores + extra[...]
            old = peak[one, :]
            new = jnp.maximum(old, jnp.max(scores, axis=0, keepdims=True))
            weights = jnp.exp2(scores - new)
            factor = jnp.exp2(old - new)
            peak[one, :] = new
            total[one, :] = total[one, :] * factor + jnp.sum(weights, axis=0, keepdims=True)
            acc[lanes, :] = acc[lanes, :] * factor + dot_tn(v[:, lanes], weights.astype(bf16))

    needs = (kb == rank) | (reach > kb * block)

    @pl.when(kb <= rank)
    def _():
        take(step, keys, k)
        take(step, values, v)

    @pl.when((kb <= rank) & jnp.logical_not(needs))
    def _():
        update(None)

    @pl.when((kb <= rank) & needs)
    def _():
        hide(kb, block, span, bias)
        update(bias)

    @pl.when(step == pl.num_programs(0) - 1)
    def _():
        for h in range(heads):
            lanes = slice(h * HD, (h + 1) * HD)
            one = slice(h, h + 1)
            out[:, lanes] = jnp.transpose(acc[lanes, :] / total[one, :]).astype(bf16)
            lse[one, :] = peak[one, :] + jnp.log2(total[one, :])


def attend(q, keys, values, info, offsets, span):
    rows, local = q.shape
    heads = local // HD
    block = keys[0].shape[0]
    blocks = len(keys)
    scale2 = HD ** (-0.5) * log2e
    fixed = lambda shape: pl.BlockSpec(shape, lambda b, info, at: (0, 0))
    grid_spec = pltpu.PrefetchScalarGridSpec(
        num_scalar_prefetch=2,
        grid=(blocks,),
        in_specs=[fixed((rows, local)), fixed((8, rows))] + [fixed((block, local))] * (2 * blocks),
        out_specs=[fixed((rows, local)), fixed((8, rows))],
        scratch_shapes=[
            pltpu.VMEM((8, rows), f32),
            pltpu.VMEM((8, rows), f32),
            pltpu.VMEM((local, rows), f32),
            pltpu.VMEM((block, rows), f32),
            pltpu.VMEM((block, local), bf16),
            pltpu.VMEM((block, local), bf16),
        ],
    )
    return pl.pallas_call(
        functools.partial(attend_kernel, scale2, heads, blocks),
        grid_spec=grid_spec,
        out_shape=(
            jax.ShapeDtypeStruct((rows, local), bf16),
            jax.ShapeDtypeStruct((8, rows), f32),
        ),
        compiler_params=params(56),
        cost_estimate=small_cost,
        name="attend",
    )(info, offsets, q, span, *keys, *values)


def attend_back_kernel(scale, scale2, heads, blocks, *refs):
    info, offsets, _, _ = refs[:4]
    q, do, o, lse, span, same, down, up = refs[4:12]
    keys, values = refs[12 : 12 + blocks], refs[12 + blocks : 12 + 2 * blocks]
    gq, gk_hi, gk_lo, gv_hi, gv_lo, delta, acc, bias, k, v = refs[12 + 2 * blocks :]
    step = pl.program_id(0)
    rank, reach = info[0], info[1]
    kb = offsets[step]
    block = k.shape[0]

    @pl.when(step == 0)
    def _():
        for h in range(heads):
            lanes = slice(h * HD, (h + 1) * HD)
            both = do[:, lanes].astype(f32) * o[:, lanes].astype(f32)
            delta[h : h + 1, :] = jnp.sum(jnp.transpose(both), axis=0, keepdims=True)
        acc[...] = jnp.zeros_like(acc)

    def update(extra, gk, gv):
        for h in range(heads):
            lanes = slice(h * HD, (h + 1) * HD)
            one = slice(h, h + 1)
            scores = dot_nt(k[:, lanes], q[:, lanes]) * scale2
            if extra is not None:
                scores = scores + extra[...]
            weights = jnp.exp2(scores - lse[one, :])
            gv[:, lanes] = dot(weights.astype(bf16), do[:, lanes]).astype(bf16)
            grad_weights = dot_nt(v[:, lanes], do[:, lanes])
            grad_scores = (weights * (grad_weights - delta[one, :])).astype(bf16)
            gk[:, lanes] = (dot(grad_scores, q[:, lanes]) * scale).astype(bf16)
            acc[lanes, :] += dot_tn(k[:, lanes], grad_scores)

    needs = (kb == rank) | (reach > kb * block)

    @pl.when(kb <= rank)
    def _():
        take(step, keys, k)
        take(step, values, v)

    for high, gk, gv in ((True, gk_hi, gv_hi), (False, gk_lo, gv_lo)):
        here = (step < blocks // 2) if high else (step >= blocks // 2)

        @pl.when(here & (kb <= rank) & jnp.logical_not(needs))
        def _(gk=gk, gv=gv):
            update(None, gk, gv)

        @pl.when(here & (kb <= rank) & needs)
        def _(gk=gk, gv=gv):
            hide(kb, block, span, bias)
            update(bias, gk, gv)

        @pl.when(here & (kb > rank))
        def _(gk=gk, gv=gv):
            gk[...] = jnp.zeros_like(gk)
            gv[...] = jnp.zeros_like(gv)

    @pl.when(step == pl.num_programs(0) - 1)
    def _():
        for h in range(heads):
            lanes = slice(h * HD, (h + 1) * HD)
            x = jnp.transpose(acc[lanes, :]) * scale
            gq[:, lanes] = turn(x, same[...], -down[...], -up[...]).astype(bf16)


def attend_back(q, keys, values, do, o, lse, info, offsets, key_at, value_at, span, tables):
    rows, local = q.shape
    heads = local // HD
    block = keys[0].shape[0]
    blocks = len(keys)
    half = blocks // 2
    scale = HD ** (-0.5)
    fixed = lambda shape: pl.BlockSpec(shape, lambda b, info, at, ks, vs: (0, 0))
    high = lambda pick: pl.BlockSpec(
        (block, local), lambda b, info, at, ks, vs: ((ks, vs)[pick][jnp.minimum(b, half - 1)] - half, 0)
    )
    low = lambda pick: pl.BlockSpec(
        (block, local), lambda b, info, at, ks, vs: ((ks, vs)[pick][jnp.maximum(b, half)], 0)
    )
    grid_spec = pltpu.PrefetchScalarGridSpec(
        num_scalar_prefetch=4,
        grid=(blocks,),
        in_specs=[fixed((rows, local))] * 3
        + [fixed((8, rows))] * 2
        + [fixed((rows, HD))] * 3
        + [fixed((block, local))] * (2 * blocks),
        out_specs=[fixed((rows, local)), high(0), low(0), high(1), low(1)],
        scratch_shapes=[
            pltpu.VMEM((8, rows), f32),
            pltpu.VMEM((local, rows), f32),
            pltpu.VMEM((block, rows), f32),
            pltpu.VMEM((block, local), bf16),
            pltpu.VMEM((block, local), bf16),
        ],
    )
    part = jax.ShapeDtypeStruct((half * block, local), bf16)
    return pl.pallas_call(
        functools.partial(attend_back_kernel, scale, scale * log2e, heads, blocks),
        grid_spec=grid_spec,
        out_shape=(jax.ShapeDtypeStruct((rows, local), bf16), part, part, part, part),
        compiler_params=params(60),
        cost_estimate=small_cost,
        name="attend_back",
    )(info, offsets, key_at, value_at, q, do, o, lse, span, *tables, *keys, *values)


def key_value_back_kernel(terms, *refs):
    gk_parts, gv_parts = refs[:terms], refs[terms : 2 * terms]
    wk, wv, same, down, up, gk, gv, gn = refs[2 * terms :]
    width = wk.shape[0]
    add = lambda parts: functools.reduce(lambda a, b: a + b, [p[...].astype(f32) for p in parts])
    gk[...] = rotated(add(gk_parts), same[...], -down[...], -up[...])
    gv[...] = add(gv_parts).astype(bf16)
    gn[:, 0:width] = dot_nt(gk[...], wk[...]).astype(bf16)
    gn[:, width : 2 * width] = dot_nt(gv[...], wv[...]).astype(bf16)


def key_value_back(gk_parts, gv_parts, wk, wv, tables):
    rows = tables[0].shape[0]
    local = gk_parts[0].shape[1]
    width = wk.shape[0]
    block = min(256, rows)
    spec = lambda cols: pl.BlockSpec((block, cols), lambda i: (i, 0))
    whole = pl.BlockSpec((width, local), lambda i: (0, 0))
    return pl.pallas_call(
        functools.partial(key_value_back_kernel, len(gk_parts)),
        grid=(rows // block,),
        out_shape=(
            jax.ShapeDtypeStruct((rows, local), bf16),
            jax.ShapeDtypeStruct((rows, local), bf16),
            jax.ShapeDtypeStruct((rows, 2 * width), bf16),
        ),
        in_specs=[spec(local)] * (2 * len(gk_parts)) + [whole] * 2 + [spec(HD)] * 3,
        out_specs=[spec(local), spec(local), spec(2 * width)],
        compiler_params=params(48),
        cost_estimate=small_cost,
        name="key_value_back",
    )(*gk_parts, *gv_parts, wk, wv, *tables)


def weight_grad_kernel(half, core, nq, nk, nv, cot, gq, gk, gv, att, send_a, own_a, send_b, own_b):
    step = pl.program_id(0)
    local = gq.shape[1]

    def fill(a, b):
        a[:, 0:local] = dot_tn(nq[...], gq[...]).astype(bf16)
        a[:, local : 2 * local] = dot_tn(nk[...], gk[...]).astype(bf16)
        b[:, 0:local] = dot_tn(nv[...], gv[...]).astype(bf16)
        b[:, local : 2 * local] = dot_tn(cot[...], att[...]).astype(bf16)

    @pl.when(step < half)
    def _():
        fill(send_a, send_b)

    @pl.when(step >= half)
    def _():
        fill(own_a, own_b)


def weight_grads(core, nq, nkv, cot, gq, gk, gv, att):
    rows, width = nq.shape
    local = gq.shape[1]
    block = 256
    steps = width // block
    half = steps // 2
    column = lambda i, core: jnp.where(i < half, (1 - core[0]) * half + i, core[0] * half + i - half)
    lhs = lambda shift: pl.BlockSpec((rows, block), lambda i, core: (0, column(i, core) + shift))
    rhs = pl.BlockSpec((rows, local), lambda i, core: (0, 0))
    out = jax.ShapeDtypeStruct((width // 2, 2 * local), bf16)
    first = pl.BlockSpec((block, 2 * local), lambda i, core: (jnp.minimum(i, half - 1), 0))
    second = pl.BlockSpec((block, 2 * local), lambda i, core: (jnp.maximum(i - half, 0), 0))
    grid_spec = pltpu.PrefetchScalarGridSpec(
        num_scalar_prefetch=1,
        grid=(steps,),
        in_specs=[lhs(0), lhs(0), lhs(steps), lhs(0)] + [rhs] * 4,
        out_specs=[first, second, first, second],
    )
    return pl.pallas_call(
        functools.partial(weight_grad_kernel, half),
        grid_spec=grid_spec,
        out_shape=(out, out, out, out),
        compiler_params=params(48),
        cost_estimate=small_cost,
        name="weight_grads",
    )(core, nq, nkv, nkv, cot, gq, gk, gv, att)


def assemble_kernel(half, local, a_slot, b_slot, a_lo, a_hi, b_lo, b_hi, gwq, gwk, gwv, gwo):
    r = pl.program_id(0)

    @pl.when(a_slot[r] < half)
    def _():
        gwq[...] = a_lo[:, 0:local].astype(f32)
        gwk[...] = a_lo[:, local : 2 * local].astype(f32)

    @pl.when(a_slot[r] >= half)
    def _():
        gwq[...] = a_hi[:, 0:local].astype(f32)
        gwk[...] = a_hi[:, local : 2 * local].astype(f32)

    @pl.when(b_slot[r] < half)
    def _():
        gwv[...] = b_lo[:, 0:local].astype(f32)
        gwo[...] = jnp.transpose(b_lo[:, local : 2 * local].astype(f32))

    @pl.when(b_slot[r] >= half)
    def _():
        gwv[...] = b_hi[:, 0:local].astype(f32)
        gwo[...] = jnp.transpose(b_hi[:, local : 2 * local].astype(f32))


def assemble(a_slot, b_slot, a_lo, a_hi, b_lo, b_hi, pieces):
    half = pieces // 2
    piece = a_lo.shape[0] // half
    local = a_lo.shape[1] // 2
    width = pieces * piece
    low = lambda pick: pl.BlockSpec(
        (piece, 2 * local), lambda i, a, b: (jnp.minimum((a, b)[pick][i], half - 1), 0)
    )
    high = lambda pick: pl.BlockSpec(
        (piece, 2 * local), lambda i, a, b: (jnp.maximum((a, b)[pick][i] - half, 0), 0)
    )
    rowed = pl.BlockSpec((piece, local), lambda i, a, b: (i, 0))
    tall = jax.ShapeDtypeStruct((width, local), f32)
    grid_spec = pltpu.PrefetchScalarGridSpec(
        num_scalar_prefetch=2,
        grid=(pieces,),
        in_specs=[low(0), high(0), low(1), high(1)],
        out_specs=[rowed, rowed, rowed, pl.BlockSpec((local, piece), lambda i, a, b: (0, i))],
    )
    return pl.pallas_call(
        functools.partial(assemble_kernel, half, local),
        grid_spec=grid_spec,
        out_shape=(tall, tall, tall, jax.ShapeDtypeStruct((local, width), f32)),
        compiler_params=params(32),
        name="assemble",
    )(a_slot, b_slot, a_lo, a_hi, b_lo, b_hi)


def flipped(x, axis, bit, sender=None):
    count = lax.axis_size(axis)
    sends = [i for i in range(count) if sender is None or bool(i & bit) == sender]
    return lax.ppermute(x, axis, [(i, i ^ bit) for i in sends])


def top(bit):
    return 2 * bit == lax.axis_size("seq")


def bits_of(count):
    bits = []
    while (1 << len(bits)) < count:
        bits.append(1 << len(bits))
    return bits


def slot_order(bits):
    order = [0]
    for bit in bits:
        order = order + [m | bit for m in order]
    return order


def collect(block, bits):
    held = {0: block}
    for bit in bits:
        sender = False if top(bit) else None
        held.update({m | bit: flipped(x, "seq", bit, sender) for m, x in held.items()})
    return held


def summed(a, b):
    return (a.astype(f32) + b.astype(f32)).astype(bf16)


def disperse(low, high, bits):
    terms = [low, flipped(high, "seq", bits[-1], True if top(bits[-1]) else None)]
    half = low.shape[0] // 2
    for bit in reversed(bits[:-1]):
        total = functools.reduce(lambda a, b: a + b, [t[half : 2 * half].astype(f32) for t in terms])
        terms.append(flipped(total.astype(bf16), "seq", bit, True if top(bit) else None))
        half = half // 2
    return terms


def merge_kernel(count, blocks, sides, *refs):
    step = pl.program_id(0)
    ins, outs = refs[: 2 * count], refs[2 * count :]

    @pl.when(step < blocks)
    def _():
        for i in range(count):
            outs[2 * i][...] = summed(ins[2 * i][...], ins[2 * i + 1][...])

    @pl.when(step >= blocks)
    def _():
        for i in range(count):
            outs[2 * i + 1][...] = summed(ins[2 * i][...], ins[2 * i + 1][...])


def reduce_level(pairs, bits, rank, midway=None):
    sides = jnp.stack([(rank & bit) // bit for bit in bits]).astype(jnp.int32)
    blocks = 2
    in_specs, out_specs, out_shape = [], [], []
    for at, (own, _) in enumerate(pairs):
        half, cols = own.shape[0] // 2, own.shape[1]
        block = half // blocks

        def pick(i, sides, at=at):
            side = sides[at]
            return (jnp.where(i < blocks, (1 - side) * blocks + i, side * blocks + i - blocks), 0)

        in_specs += [pl.BlockSpec((block, cols), pick)] * 2
        out_specs.append(pl.BlockSpec((block, cols), lambda i, sides: (jnp.minimum(i, blocks - 1), 0)))
        out_specs.append(pl.BlockSpec((block, cols), lambda i, sides: (jnp.maximum(i - blocks, 0), 0)))
        out_shape += [jax.ShapeDtypeStruct((half, cols), bf16)] * 2
    outs = pl.pallas_call(
        functools.partial(merge_kernel, len(pairs), blocks),
        grid_spec=pltpu.PrefetchScalarGridSpec(
            num_scalar_prefetch=1, grid=(2 * blocks,), in_specs=in_specs, out_specs=out_specs
        ),
        out_shape=out_shape,
        compiler_params=params(32),
        cost_estimate=small_cost,
        name="merge",
    )(sides, *[x for pair in pairs for x in pair])
    pairs = []
    for i, bit in enumerate(bits):
        send = outs[2 * i] if midway is None else after(outs[2 * i], midway)
        pairs.append((outs[2 * i + 1], flipped(send, "seq", bit)))
    return pairs


def widen_kernel(x, out):
    out[...] = x[...].astype(f32)


def widened(x):
    rows, cols = x.shape
    spec = pl.BlockSpec((min(512, rows), cols), lambda i: (i, 0))
    return pl.pallas_call(
        widen_kernel,
        grid=(rows // min(512, rows),),
        out_shape=jax.ShapeDtypeStruct(x.shape, f32),
        in_specs=[spec],
        out_specs=spec,
        compiler_params=params(48),
        name="widen",
    )(x)


def spread(piece, bits):
    held = piece
    for bit in bits[:-1]:
        held = jnp.concatenate([held, flipped(held, "seq", bit)], axis=0)
    return held, flipped(held, "seq", bits[-1])


def piece_slots(bits, rank, count):
    order = slot_order(bits[::-1])
    table = [0] * count
    for slot, m in enumerate(order):
        table[m] = slot
    owners = []
    for r in range(count):
        owner = 0
        for at, bit in enumerate(bits):
            if (r >> (len(bits) - 1 - at)) & 1:
                owner |= bit
        owners.append(owner)
    return jnp.take(jnp.array(table, jnp.int32), jnp.array(owners, jnp.int32) ^ rank)


def ring(x, axis):
    count = lax.axis_size(axis)
    from_below, from_above = [], []
    up = down = x
    for k in range(1, count):
        up = lax.ppermute(up, axis, [(i, i + 1) for i in range(k - 1, count - 1)])
        down = lax.ppermute(down, axis, [(i, i - 1) for i in range(1, count - k + 1)])
        from_below.append(up)
        from_above.append(down)
    return from_below + from_above


def after(x, *earlier):
    anywhere = pl.BlockSpec(memory_space=pl.ANY)
    return pl.pallas_call(
        lambda *refs: None,
        out_shape=jax.ShapeDtypeStruct(x.shape, x.dtype),
        in_specs=[anywhere] * (1 + len(earlier)),
        out_specs=anywhere,
        input_output_aliases={0: 0},
        name="after",
    )(x, *earlier)


def small_sum(x, midway):
    x = x.astype(bf16)
    for axis in ("seq", "head"):
        if axis == "head":
            x = after(x, midway)
        for bit in bits_of(lax.axis_size(axis)):
            x = summed(x, flipped(x, axis, bit))
    return x.astype(f32)


def body(
    histories,
    norm_gains,
    mix_in,
    mix_out,
    mix_bias,
    w_query,
    w_key,
    w_value,
    w_out,
    w_up,
    w_down,
    cotangent,
    doc_ids,
    positions,
):
    seq_count = lax.axis_size("seq")
    rank = lax.axis_index("seq")
    block_rows = positions.shape[0]
    hist_count, tok_rows, width = histories.shape
    count = norm_gains.shape[0]
    units = mix_in.shape[1]
    mixes = mix_out.shape[1]

    def gather(x):
        return lax.all_gather(x, "head", axis=0, tiled=True)

    def scatter(x):
        return lax.psum_scatter(x, "head", scatter_dimension=0, tiled=True)

    tables = rope_lanes(positions)
    place = rank * block_rows + jnp.arange(block_rows, dtype=jnp.int32)
    first = place - positions
    span = jnp.concatenate([first[None], place[None], jnp.zeros((6, block_rows), jnp.int32)], axis=0)
    info = jnp.stack([rank.astype(jnp.int32), jnp.max(first)])
    bits = bits_of(seq_count)
    key_bits = bits[1:] + bits[:1]
    value_bits = bits[1:][::-1] + bits[:1]
    key_order = slot_order(key_bits)
    value_order = slot_order(value_bits)
    half = seq_count // 2
    order = key_order[half:] + key_order[:half]
    offsets = jnp.array(order, jnp.int32) ^ rank
    key_at = jnp.array([key_order.index(m) for m in order], jnp.int32)
    value_at = jnp.array([value_order.index(m) for m in order], jnp.int32)
    same, down, up = tables
    core = (rank & 1)[None].astype(jnp.int32)
    cot_pieces = [cotangent] + ring(cotangent, "head")
    n3, nkv, nq, streams, coef, mix_pre = mix_forward(
        histories, norm_gains, mix_in, mix_out, mix_bias[None, :]
    )
    n3_pieces = [n3] + ring(n3, "head")
    nkv_full = gather(after(nkv, *n3_pieces[1:], *cot_pieces[1:]))
    nq_full = gather(nq)
    act, ff_grad, gw_up, gw_down, cot_full = feed_forward(
        lax.axis_index("head")[None], n3_pieces, cot_pieces, w_up, w_down
    )
    gw_up, gw_down = lax.psum((gw_up, gw_down), "seq")
    key, value = project(
        key_value_kernel, nkv_full, (w_key, w_value), (after(same, act), down, up), 2, "project_kv"
    )
    (query,) = project(query_kernel, nq_full, (w_query,), tables, 1, "project_q")
    keys = collect(key, key_bits)
    values = collect(value, value_bits)
    keys, values = [keys[m] for m in order], [values[m] for m in order]
    do = dot_nt(cot_full, w_out).astype(bf16)
    attended, lse = attend(query, keys, values, info, offsets, after(span, do))
    gq, gk_hi, gk_lo, gv_hi, gv_lo = attend_back(
        query,
        keys,
        values,
        do,
        attended,
        lse,
        info,
        offsets,
        key_at,
        value_at,
        span,
        tables,
    )
    gnq = scatter(dot_nt(gq, w_query).astype(bf16))
    ff_out, gn3_part = feed_forward_sums(after(act, gq), ff_grad, w_up, w_down)
    gn3 = scatter(gn3_part)
    branch_part = (ff_out + dot(attended, w_out)).astype(bf16)
    branch = scatter(branch_part)
    layer_out = (streams[3] + branch.astype(f32)).astype(bf16)
    gk, gv, gnkv_part = key_value_back(
        disperse(gk_lo, gk_hi, key_bits),
        disperse(gv_lo, gv_hi, value_bits),
        w_key,
        w_value,
        (after(same, gn3_part, branch_part), down, up),
    )
    gnkv = scatter(gnkv_part)
    send_a, own_a, send_b, own_b = weight_grads(
        core, nq_full, nkv_full, cot_full, gq, gk, after(gv, gw_up, gw_down), attended
    )
    pairs = [(own_a, flipped(send_a, "seq", 1)), (own_b, flipped(send_b, "seq", 1))]
    a_bits = bits[1:]
    b_bits = bits[1:][::-1]
    gw_up, gw_down = widened(gw_up), widened(gw_down)
    for level in range(len(a_bits)):
        last = level == len(a_bits) - 1
        pairs = reduce_level(pairs, (a_bits[level], b_bits[level]), rank, gw_up if last else None)
    piece_a, piece_b = summed(*pairs[0]), summed(*pairs[1])
    a_lo, a_hi = spread(piece_a, a_bits[::-1] + bits[:1])
    b_lo, b_hi = spread(piece_b, b_bits[::-1] + bits[:1])
    gwq, gwk, gwv, gwo = assemble(
        piece_slots(bits[:1] + a_bits, rank, seq_count),
        piece_slots(bits[:1] + b_bits, rank, seq_count),
        a_lo,
        a_hi,
        b_lo,
        b_hi,
        seq_count,
    )
    ghist, pack = unmix(
        histories, streams, gn3, gnkv, gnq, cotangent, coef, mix_pre, norm_gains, mix_in, mix_out
    )
    pack = small_sum(pack, gw_down)
    return (
        layer_out,
        ghist,
        pack[units : units + count, :width],
        jnp.transpose(pack[:units, :width]),
        pack[:units, width : width + mixes],
        pack[units, width : width + mixes],
        gwq,
        gwk,
        gwv,
        gwo,
        gw_up,
        gw_down,
    )


def solution(mesh):
    return jax.shard_map(
        body,
        mesh=mesh,
        in_specs=(
            P(None, ("seq", "head"), None),
            P(),
            P(),
            P(),
            P(),
            P(None, "head"),
            P(None, "head"),
            P(None, "head"),
            P("head", None),
            P(None, "head"),
            P("head", None),
            P(("seq", "head"), None),
            P(),
            P("seq"),
        ),
        out_specs=(
            P(("seq", "head"), None),
            P(None, ("seq", "head"), None),
            P(),
            P(),
            P(),
            P(),
            P(None, "head"),
            P(None, "head"),
            P(None, "head"),
            P("head", None),
            P(None, "head"),
            P("head", None),
        ),
        check_vma=False,
    )
```

```python
import functools

import jax
import jax.numpy as jnp
from jax import lax
from jax.experimental import pallas as pl
from jax.experimental.pallas import tpu as pltpu
from jax.sharding import PartitionSpec as P

HD = 128
ROT = 32
HALF = ROT // 2
MIB = 1024 * 1024

eps_norm = 1e-05
eps_rms = 1e-06
rope_base = 10000.0
hidden_mask = -1e30
highest = lax.Precision.HIGHEST
f32 = jnp.float32
bf16 = jnp.bfloat16
sqrt_half = 0.7071067811865476
inv_sqrt_2pi = 0.3989422804014327
log2e = 1.4426950408889634
small_cost = pl.CostEstimate(flops=MIB, bytes_accessed=MIB, transcendentals=0)


def vmem():
    return pl.BlockSpec(memory_space=pltpu.VMEM)


def params(mib, **more):
    return pltpu.CompilerParams(vmem_limit_bytes=60 * MIB, **more)


def cdf(x):
    return 0.5 * (1.0 + lax.erf(x * sqrt_half))


def pdf(x):
    return jnp.exp(x * x * -0.5) * inv_sqrt_2pi


def dot(a, b):
    return jnp.dot(a, b, preferred_element_type=f32)


def dot_nt(a, b):
    return lax.dot_general(a, b, (((1,), (1,)), ((), ())), preferred_element_type=f32)


def dot_tn(a, b):
    return lax.dot_general(a, b, (((0,), (0,)), ((), ())), preferred_element_type=f32)


def mix_kernel(tile, hist, gains, mix_in, mix_out, mix_bias, n3, nkv, nq, streams, coef, mix_pre):
    hist_count, rows, width = hist.shape
    count = gains.shape[0]
    newest = hist[hist_count - 1].astype(f32)
    scale = lax.rsqrt(jnp.mean(newest * newest, axis=-1, keepdims=True) + eps_rms)
    rms_low = (newest * scale).astype(bf16)
    pre = dot(rms_low, mix_in[...])
    mix_pre[...] = pre
    hidden = (pre * cdf(pre)).astype(bf16)
    coef[...] = dot(hidden, mix_out[...]) + mix_bias[...]
    chunk = 512

    def step(i, carry):
        at = pl.ds(pl.multiple_of(i * tile, tile), tile)
        rows_coef = coef[at, :]
        columns = [
            [rows_coef[:, c * hist_count + j : c * hist_count + j + 1] for j in range(hist_count)]
            for c in range(count)
        ]
        totals = [jnp.zeros((tile, 1), f32) for _ in range(count)]
        for lane in range(0, width, chunk):
            sums = [jnp.zeros((tile, chunk), f32) for _ in range(count)]
            for j in range(hist_count):
                h = hist[j, at, lane : lane + chunk].astype(f32)
                for c in range(count):
                    sums[c] = sums[c] + columns[c][j] * h
            for c in range(count):
                streams[c, at, lane : lane + chunk] = sums[c]
                totals[c] = totals[c] + jnp.sum(sums[c], axis=-1, keepdims=True)
        for c in range(count):
            x = streams[c, at, :]
            centre = x - totals[c] * (1.0 / width)
            spread = jnp.mean(centre * centre, axis=-1, keepdims=True)
            out = (centre * lax.rsqrt(spread + eps_norm) * gains[c : c + 1, :]).astype(bf16)
            if c == 0:
                nq[at, :] = out
            elif c == 3:
                n3[at, :] = out
            else:
                nkv[at, (c - 1) * width : c * width] = out
        return carry

    lax.fori_loop(0, rows // tile, step, 0)


def mix_forward(histories, norm_gains, mix_in, mix_out, mix_bias):
    hist_count, rows, width = histories.shape
    count = norm_gains.shape[0]
    return pl.pallas_call(
        functools.partial(mix_kernel, min(32, rows)),
        out_shape=(
            jax.ShapeDtypeStruct((rows, width), bf16),
            jax.ShapeDtypeStruct((rows, 2 * width), bf16),
            jax.ShapeDtypeStruct((rows, width), bf16),
            jax.ShapeDtypeStruct((count, rows, width), f32),
            jax.ShapeDtypeStruct((rows, count * hist_count), f32),
            jax.ShapeDtypeStruct((rows, mix_in.shape[1]), f32),
        ),
        in_specs=[vmem()] * 5,
        out_specs=[vmem()] * 6,
        compiler_params=params(48),
        name="mix_forward",
    )(histories, norm_gains, mix_in, mix_out, mix_bias)


def unmix_kernel(
    hist, streams, gn3, gnkv, gnq, cot, coef, mix_pre, gains, mix_in, mix_out, ghist, pack, gs, rms_keep, hid_keep, gc_keep, gmp_keep
):
    hist_count, tile, width = hist.shape
    count = gains.shape[0]
    hidden_units = mix_in.shape[1]
    step = pl.program_id(0)

    @pl.when(step == 0)
    def _():
        pack[...] = jnp.zeros_like(pack)

    for c in range(count):
        x = streams[c]
        centre = x - jnp.mean(x, axis=-1, keepdims=True)
        inv = lax.rsqrt(jnp.mean(centre * centre, axis=-1, keepdims=True) + eps_norm)
        unit = centre * inv
        if c == 0:
            g = gnq[...].astype(f32)
        elif c == 3:
            g = gn3[...].astype(f32)
        else:
            g = gnkv[:, (c - 1) * width : c * width].astype(f32)
        pack[hidden_units + c : hidden_units + c + 1, 0:width] += jnp.sum(g * unit, axis=0, keepdims=True)
        d = g * gains[c : c + 1, :]
        out = inv * (
            d
            - jnp.mean(d, axis=-1, keepdims=True)
            - unit * jnp.mean(d * unit, axis=-1, keepdims=True)
        )
        if c == 3:
            out = out + cot[...].astype(f32)
        gs[c] = out
    lanes = lax.broadcasted_iota(jnp.int32, (tile, count * hist_count), 1)
    gc = jnp.zeros((tile, count * hist_count), f32)
    rows_coef = coef[...]
    for j in range(hist_count):
        h = hist[j].astype(f32)
        for c in range(count):
            k = c * hist_count + j
            gc = jnp.where(lanes == k, jnp.sum(gs[c] * h, axis=-1, keepdims=True), gc)
    for j in range(hist_count):
        total = rows_coef[:, j : j + 1] * gs[0]
        for c in range(1, count):
            k = c * hist_count + j
            total = total + rows_coef[:, k : k + 1] * gs[c]
        if j < hist_count - 1:
            ghist[j] = total.astype(bf16)
    pre = mix_pre[...]
    phi = cdf(pre)
    gmh = lax.dot_general(
        gc, mix_out[...].astype(f32), (((1,), (1,)), ((), ())), precision=highest
    )
    gmp = (phi + pre * pdf(pre)) * gmh
    gmp_low = gmp.astype(bf16)
    grad_rms = dot_nt(gmp_low, mix_in[...])
    newest = hist[hist_count - 1].astype(f32)
    scale = lax.rsqrt(jnp.mean(newest * newest, axis=-1, keepdims=True) + eps_rms)
    inner = jnp.mean(grad_rms * newest, axis=-1, keepdims=True)
    total = total + scale * grad_rms - newest * (scale * scale * scale * inner)
    ghist[hist_count - 1] = total.astype(bf16)
    at = pl.ds(pl.multiple_of(step * tile, tile), tile)
    rms_keep[at, :] = (newest * scale).astype(bf16)
    hid_keep[at, :] = (pre * phi).astype(bf16).astype(f32)
    gc_keep[at, :] = gc
    gmp_keep[at, :] = gmp_low

    @pl.when(step == pl.num_programs(0) - 1)
    def _():
        pack[0:hidden_units, 0:width] = dot_tn(gmp_keep[...], rms_keep[...])
        pack[0:hidden_units, width : width + count * hist_count] = lax.dot_general(
            hid_keep[...], gc_keep[...], (((0,), (0,)), ((), ())), precision=highest
        )
        pack[hidden_units : hidden_units + 1, width : width + count * hist_count] = jnp.sum(
            gc_keep[...], axis=0, keepdims=True
        )


def unmix(histories, streams, gn3, gnkv, gnq, cotangent, coef, mix_pre, norm_gains, mix_in, mix_out):
    hist_count, rows, width = histories.shape
    count = norm_gains.shape[0]
    units = mix_in.shape[1]
    mixes = count * hist_count
    tile = 32
    whole = lambda shape: pl.BlockSpec(shape, lambda i: (0, 0))
    return pl.pallas_call(
        unmix_kernel,
        grid=(rows // tile,),
        out_shape=(
            jax.ShapeDtypeStruct((hist_count, rows, width), bf16),
            jax.ShapeDtypeStruct((units + 8, width + 128), f32),
        ),
        in_specs=[
            pl.BlockSpec((hist_count, tile, width), lambda i: (0, i, 0)),
            pl.BlockSpec((count, tile, width), lambda i: (0, i, 0)),
            pl.BlockSpec((tile, width), lambda i: (i, 0)),
            pl.BlockSpec((tile, 2 * width), lambda i: (i, 0)),
            pl.BlockSpec((tile, width), lambda i: (i, 0)),
            pl.BlockSpec((tile, width), lambda i: (i, 0)),
            pl.BlockSpec((tile, mixes), lambda i: (i, 0)),
            pl.BlockSpec((tile, units), lambda i: (i, 0)),
            whole((count, width)),
            whole((width, units)),
            whole((units, mixes)),
        ],
        out_specs=[
            pl.BlockSpec((hist_count, tile, width), lambda i: (0, i, 0)),
            whole((units + 8, width + 128)),
        ],
        scratch_shapes=[
            pltpu.VMEM((count, tile, width), f32),
            pltpu.VMEM((rows, width), bf16),
            pltpu.VMEM((rows, units), f32),
            pltpu.VMEM((rows, mixes), f32),
            pltpu.VMEM((rows, units), bf16),
        ],
        compiler_params=params(48),
        name="unmix",
    )(histories, streams, gn3, gnkv, gnq, cotangent, coef, mix_pre, norm_gains, mix_in, mix_out)


def ff_kernel(count, rank_ref, *refs):
    pieces = 2 * count - 1
    sources = (refs[:pieces], refs[pieces : 2 * pieces])
    w_up, w_down, act, grad, gw_up, gw_down, cot, n3, sems = refs[2 * pieces :]
    step = pl.program_id(0)

    @pl.when(step == 0)
    def _():
        rank = rank_ref[0]

        def each(act):
            for which, target in ((0, n3), (1, cot)):
                rows = target.shape[0] // count
                for at in range(pieces):
                    if at == 0:
                        block, there = rank, None
                    elif at < count:
                        block, there = rank - at, rank >= at
                    else:
                        k = at - count + 1
                        block, there = rank + k, rank + k < count

                    def one(block=block, at=at):
                        to = target.at[pl.ds(pl.multiple_of(block * rows, rows), rows), :]
                        act(pltpu.make_async_copy(sources[which][at], to, sems.at[which, at]))

                    if there is None:
                        one()
                    else:
                        pl.when(there)(one)

        each(lambda copy: copy.start())
        each(lambda copy: copy.wait())

    pre = dot(n3[...], w_up[...])
    phi = cdf(pre)
    act[...] = (pre * phi).astype(bf16)
    slope = phi + pre * pdf(pre)
    grad[...] = (dot_nt(cot[...], w_down[...]) * slope).astype(bf16)
    gw_down[...] = dot_tn(act[...], cot[...]).astype(bf16)
    gw_up[...] = dot_tn(n3[...], grad[...]).astype(bf16)


def feed_forward(rank, n3_pieces, cot_pieces, w_up, w_down):
    count = (len(n3_pieces) + 1) // 2
    rows, width = n3_pieces[0].shape
    rows = rows * count
    hidden = w_up.shape[1]
    block = min(512, hidden)
    fixed = pl.BlockSpec((rows, width), lambda i, r: (0, 0))
    anywhere = pl.BlockSpec(memory_space=pl.ANY)
    grid_spec = pltpu.PrefetchScalarGridSpec(
        num_scalar_prefetch=1,
        grid=(hidden // block,),
        in_specs=[anywhere] * (2 * len(n3_pieces))
        + [
            pl.BlockSpec((width, block), lambda i, r: (0, i)),
            pl.BlockSpec((block, width), lambda i, r: (i, 0)),
        ],
        out_specs=[
            pl.BlockSpec((rows, block), lambda i, r: (0, i)),
            pl.BlockSpec((rows, block), lambda i, r: (0, i)),
            pl.BlockSpec((width, block), lambda i, r: (0, i)),
            pl.BlockSpec((block, width), lambda i, r: (i, 0)),
            fixed,
        ],
        scratch_shapes=[
            pltpu.VMEM((rows, width), bf16),
            pltpu.SemaphoreType.DMA((2, len(n3_pieces))),
        ],
    )
    return pl.pallas_call(
        functools.partial(ff_kernel, count),
        grid_spec=grid_spec,
        out_shape=(
            jax.ShapeDtypeStruct((rows, hidden), bf16),
            jax.ShapeDtypeStruct((rows, hidden), bf16),
            jax.ShapeDtypeStruct((width, hidden), bf16),
            jax.ShapeDtypeStruct((hidden, width), bf16),
            jax.ShapeDtypeStruct((rows, width), bf16),
        ),
        compiler_params=params(60),
        cost_estimate=small_cost,
        name="feed_forward",
    )(rank, *n3_pieces, *cot_pieces, w_up, w_down)


def ff_sums_kernel(act, grad, w_up, w_down, ff_out, gn3):
    ff_out[...] = dot(act[...], w_down[...])
    gn3[...] = dot_nt(grad[...], w_up[...]).astype(bf16)


def feed_forward_sums(act, grad, w_up, w_down):
    rows, hidden = act.shape
    width = w_up.shape[0]
    block = min(512, width)
    fixed = pl.BlockSpec((rows, hidden), lambda i: (0, 0))
    out = pl.BlockSpec((rows, block), lambda i: (0, i))
    return pl.pallas_call(
        ff_sums_kernel,
        grid=(width // block,),
        out_shape=(
            jax.ShapeDtypeStruct((rows, width), f32),
            jax.ShapeDtypeStruct((rows, width), bf16),
        ),
        in_specs=[
            fixed,
            fixed,
            pl.BlockSpec((block, hidden), lambda i: (i, 0)),
            pl.BlockSpec((hidden, block), lambda i: (0, i)),
        ],
        out_specs=[out, out],
        compiler_params=params(56),
        cost_estimate=small_cost,
        name="feed_forward_sums",
    )(act, grad, w_up, w_down)


def turn(x, same, down, up):
    return x * same + pltpu.roll(x, HD - HALF, 1) * down + pltpu.roll(x, HALF, 1) * up


def rotated(x, same, down, up):
    heads = [
        turn(x[:, h : h + HD], same, down, up).astype(bf16) for h in range(0, x.shape[1], HD)
    ]
    return jnp.concatenate(heads, axis=1)


def query_kernel(n, w, same, down, up, out):
    out[...] = rotated(dot(n[...], w[...]), same[...], down[...], up[...])


def key_value_kernel(n, wk, wv, same, down, up, key, value):
    width = wk.shape[0]
    key[...] = rotated(dot(n[:, 0:width], wk[...]), same[...], down[...], up[...])
    value[...] = dot(n[:, width : 2 * width], wv[...]).astype(bf16)


def project(kernel, n, weights, tables, outs, name):
    rows = n.shape[0]
    width, local = weights[0].shape
    block = min(256, rows)
    spec = lambda cols: pl.BlockSpec((block, cols), lambda i: (i, 0))
    return pl.pallas_call(
        kernel,
        grid=(rows // block,),
        out_shape=tuple(jax.ShapeDtypeStruct((rows, local), bf16) for _ in range(outs)),
        in_specs=[spec(n.shape[1])]
        + [pl.BlockSpec((width, local), lambda i: (0, 0))] * len(weights)
        + [spec(HD)] * 3,
        out_specs=tuple(spec(local) for _ in range(outs)),
        compiler_params=params(48),
        cost_estimate=small_cost,
        name=name,
    )(n, *weights, *tables)


def rope_lanes(positions):
    frequency = rope_base ** (-(jnp.arange(HALF, dtype=f32) * 2.0 / ROT))
    angles = positions.astype(f32)[:, None] * frequency[None, :]
    cos, sin = jnp.cos(angles), jnp.sin(angles)
    rows = positions.shape[0]
    ones = jnp.ones((rows, HD - ROT), f32)
    zeros = jnp.zeros((rows, HD - HALF), f32)
    same = jnp.concatenate([cos, cos, ones], axis=1)
    down = jnp.concatenate([-sin, zeros], axis=1)
    up = jnp.concatenate([zeros[:, :HALF], sin, zeros[:, : HD - ROT]], axis=1)
    return (same, down, up)


def hide(kb, block, span, bias):
    place = lax.broadcasted_iota(jnp.int32, bias.shape, 0) + kb * block
    seen = (place >= span[0:1, :]) & (place <= span[1:2, :])
    bias[...] = jnp.where(seen, 0.0, hidden_mask)


def take(step, sources, target):
    for i, source in enumerate(sources):

        @pl.when(step == i)
        def _(source=source):
            target[...] = source[...]


def attend_kernel(scale2, heads, blocks, info, offsets, q, span, *refs):
    keys, values = refs[:blocks], refs[blocks : 2 * blocks]
    out, lse, peak, total, acc, bias, k, v = refs[2 * blocks :]
    step = pl.program_id(0)
    rank, reach = info[0], info[1]
    kb = offsets[step]
    block = k.shape[0]

    @pl.when(step == 0)
    def _():
        peak[...] = jnp.full_like(peak, hidden_mask)
        total[...] = jnp.zeros_like(total)
        acc[...] = jnp.zeros_like(acc)

    def update(extra):
        for h in range(heads):
            lanes = slice(h * HD, (h + 1) * HD)
            one = slice(h, h + 1)
            scores = dot_nt(k[:, lanes], q[:, lanes]) * scale2
            if extra is not None:
                scores = scores + extra[...]
            old = peak[one, :]
            new = jnp.maximum(old, jnp.max(scores, axis=0, keepdims=True))
            weights = jnp.exp2(scores - new)
            factor = jnp.exp2(old - new)
            peak[one, :] = new
            total[one, :] = total[one, :] * factor + jnp.sum(weights, axis=0, keepdims=True)
            acc[lanes, :] = acc[lanes, :] * factor + dot_tn(v[:, lanes], weights.astype(bf16))

    needs = (kb == rank) | (reach > kb * block)

    @pl.when(kb <= rank)
    def _():
        take(step, keys, k)
        take(step, values, v)

    @pl.when((kb <= rank) & jnp.logical_not(needs))
    def _():
        update(None)

    @pl.when((kb <= rank) & needs)
    def _():
        hide(kb, block, span, bias)
        update(bias)

    @pl.when(step == pl.num_programs(0) - 1)
    def _():
        for h in range(heads):
            lanes = slice(h * HD, (h + 1) * HD)
            one = slice(h, h + 1)
            out[:, lanes] = jnp.transpose(acc[lanes, :] / total[one, :]).astype(bf16)
            lse[one, :] = peak[one, :] + jnp.log2(total[one, :])


def attend(q, keys, values, info, offsets, span):
    rows, local = q.shape
    heads = local // HD
    block = keys[0].shape[0]
    blocks = len(keys)
    scale2 = HD ** (-0.5) * log2e
    fixed = lambda shape: pl.BlockSpec(shape, lambda b, info, at: (0, 0))
    grid_spec = pltpu.PrefetchScalarGridSpec(
        num_scalar_prefetch=2,
        grid=(blocks,),
        in_specs=[fixed((rows, local)), fixed((8, rows))] + [fixed((block, local))] * (2 * blocks),
        out_specs=[fixed((rows, local)), fixed((8, rows))],
        scratch_shapes=[
            pltpu.VMEM((8, rows), f32),
            pltpu.VMEM((8, rows), f32),
            pltpu.VMEM((local, rows), f32),
            pltpu.VMEM((block, rows), f32),
            pltpu.VMEM((block, local), bf16),
            pltpu.VMEM((block, local), bf16),
        ],
    )
    return pl.pallas_call(
        functools.partial(attend_kernel, scale2, heads, blocks),
        grid_spec=grid_spec,
        out_shape=(
            jax.ShapeDtypeStruct((rows, local), bf16),
            jax.ShapeDtypeStruct((8, rows), f32),
        ),
        compiler_params=params(56),
        cost_estimate=small_cost,
        name="attend",
    )(info, offsets, q, span, *keys, *values)


def attend_back_kernel(scale, scale2, heads, blocks, *refs):
    info, offsets, _, _ = refs[:4]
    q, do, o, lse, span, same, down, up = refs[4:12]
    keys, values = refs[12 : 12 + blocks], refs[12 + blocks : 12 + 2 * blocks]
    gq, gk_hi, gk_lo, gv_hi, gv_lo, delta, acc, bias, k, v = refs[12 + 2 * blocks :]
    step = pl.program_id(0)
    rank, reach = info[0], info[1]
    kb = offsets[step]
    block = k.shape[0]

    @pl.when(step == 0)
    def _():
        for h in range(heads):
            lanes = slice(h * HD, (h + 1) * HD)
            both = do[:, lanes].astype(f32) * o[:, lanes].astype(f32)
            delta[h : h + 1, :] = jnp.sum(jnp.transpose(both), axis=0, keepdims=True)
        acc[...] = jnp.zeros_like(acc)

    def update(extra, gk, gv):
        for h in range(heads):
            lanes = slice(h * HD, (h + 1) * HD)
            one = slice(h, h + 1)
            scores = dot_nt(k[:, lanes], q[:, lanes]) * scale2
            if extra is not None:
                scores = scores + extra[...]
            weights = jnp.exp2(scores - lse[one, :])
            gv[:, lanes] = dot(weights.astype(bf16), do[:, lanes]).astype(bf16)
            grad_weights = dot_nt(v[:, lanes], do[:, lanes])
            grad_scores = (weights * (grad_weights - delta[one, :])).astype(bf16)
            gk[:, lanes] = (dot(grad_scores, q[:, lanes]) * scale).astype(bf16)
            acc[lanes, :] += dot_tn(k[:, lanes], grad_scores)

    needs = (kb == rank) | (reach > kb * block)

    @pl.when(kb <= rank)
    def _():
        take(step, keys, k)
        take(step, values, v)

    for high, gk, gv in ((True, gk_hi, gv_hi), (False, gk_lo, gv_lo)):
        here = (step < blocks // 2) if high else (step >= blocks // 2)

        @pl.when(here & (kb <= rank) & jnp.logical_not(needs))
        def _(gk=gk, gv=gv):
            update(None, gk, gv)

        @pl.when(here & (kb <= rank) & needs)
        def _(gk=gk, gv=gv):
            hide(kb, block, span, bias)
            update(bias, gk, gv)

        @pl.when(here & (kb > rank))
        def _(gk=gk, gv=gv):
            gk[...] = jnp.zeros_like(gk)
            gv[...] = jnp.zeros_like(gv)

    @pl.when(step == pl.num_programs(0) - 1)
    def _():
        for h in range(heads):
            lanes = slice(h * HD, (h + 1) * HD)
            x = jnp.transpose(acc[lanes, :]) * scale
            gq[:, lanes] = turn(x, same[...], -down[...], -up[...]).astype(bf16)


def attend_back(q, keys, values, do, o, lse, info, offsets, key_at, value_at, span, tables):
    rows, local = q.shape
    heads = local // HD
    block = keys[0].shape[0]
    blocks = len(keys)
    half = blocks // 2
    scale = HD ** (-0.5)
    fixed = lambda shape: pl.BlockSpec(shape, lambda b, info, at, ks, vs: (0, 0))
    high = lambda pick: pl.BlockSpec(
        (block, local), lambda b, info, at, ks, vs: ((ks, vs)[pick][jnp.minimum(b, half - 1)] - half, 0)
    )
    low = lambda pick: pl.BlockSpec(
        (block, local), lambda b, info, at, ks, vs: ((ks, vs)[pick][jnp.maximum(b, half)], 0)
    )
    grid_spec = pltpu.PrefetchScalarGridSpec(
        num_scalar_prefetch=4,
        grid=(blocks,),
        in_specs=[fixed((rows, local))] * 3
        + [fixed((8, rows))] * 2
        + [fixed((rows, HD))] * 3
        + [fixed((block, local))] * (2 * blocks),
        out_specs=[fixed((rows, local)), high(0), low(0), high(1), low(1)],
        scratch_shapes=[
            pltpu.VMEM((8, rows), f32),
            pltpu.VMEM((local, rows), f32),
            pltpu.VMEM((block, rows), f32),
            pltpu.VMEM((block, local), bf16),
            pltpu.VMEM((block, local), bf16),
        ],
    )
    part = jax.ShapeDtypeStruct((half * block, local), bf16)
    return pl.pallas_call(
        functools.partial(attend_back_kernel, scale, scale * log2e, heads, blocks),
        grid_spec=grid_spec,
        out_shape=(jax.ShapeDtypeStruct((rows, local), bf16), part, part, part, part),
        compiler_params=params(60),
        cost_estimate=small_cost,
        name="attend_back",
    )(info, offsets, key_at, value_at, q, do, o, lse, span, *tables, *keys, *values)


def key_value_back_kernel(terms, *refs):
    gk_parts, gv_parts = refs[:terms], refs[terms : 2 * terms]
    wk, wv, same, down, up, gk, gv, gn = refs[2 * terms :]
    width = wk.shape[0]
    add = lambda parts: functools.reduce(lambda a, b: a + b, [p[...].astype(f32) for p in parts])
    gk[...] = rotated(add(gk_parts), same[...], -down[...], -up[...])
    gv[...] = add(gv_parts).astype(bf16)
    gn[:, 0:width] = dot_nt(gk[...], wk[...]).astype(bf16)
    gn[:, width : 2 * width] = dot_nt(gv[...], wv[...]).astype(bf16)


def key_value_back(gk_parts, gv_parts, wk, wv, tables):
    rows = tables[0].shape[0]
    local = gk_parts[0].shape[1]
    width = wk.shape[0]
    block = min(256, rows)
    spec = lambda cols: pl.BlockSpec((block, cols), lambda i: (i, 0))
    whole = pl.BlockSpec((width, local), lambda i: (0, 0))
    return pl.pallas_call(
        functools.partial(key_value_back_kernel, len(gk_parts)),
        grid=(rows // block,),
        out_shape=(
            jax.ShapeDtypeStruct((rows, local), bf16),
            jax.ShapeDtypeStruct((rows, local), bf16),
            jax.ShapeDtypeStruct((rows, 2 * width), bf16),
        ),
        in_specs=[spec(local)] * (2 * len(gk_parts)) + [whole] * 2 + [spec(HD)] * 3,
        out_specs=[spec(local), spec(local), spec(2 * width)],
        compiler_params=params(48),
        cost_estimate=small_cost,
        name="key_value_back",
    )(*gk_parts, *gv_parts, wk, wv, *tables)


def weight_grad_kernel(half, core, nq, nk, nv, cot, gq, gk, gv, att, send_a, own_a, send_b, own_b):
    step = pl.program_id(0)
    local = gq.shape[1]

    def fill(a, b):
        a[:, 0:local] = dot_tn(nq[...], gq[...]).astype(bf16)
        a[:, local : 2 * local] = dot_tn(nk[...], gk[...]).astype(bf16)
        b[:, 0:local] = dot_tn(nv[...], gv[...]).astype(bf16)
        b[:, local : 2 * local] = dot_tn(cot[...], att[...]).astype(bf16)

    @pl.when(step < half)
    def _():
        fill(send_a, send_b)

    @pl.when(step >= half)
    def _():
        fill(own_a, own_b)


def weight_grads(core, nq, nkv, cot, gq, gk, gv, att):
    rows, width = nq.shape
    local = gq.shape[1]
    block = 256
    steps = width // block
    half = steps // 2
    column = lambda i, core: jnp.where(i < half, (1 - core[0]) * half + i, core[0] * half + i - half)
    lhs = lambda shift: pl.BlockSpec((rows, block), lambda i, core: (0, column(i, core) + shift))
    rhs = pl.BlockSpec((rows, local), lambda i, core: (0, 0))
    out = jax.ShapeDtypeStruct((width // 2, 2 * local), bf16)
    first = pl.BlockSpec((block, 2 * local), lambda i, core: (jnp.minimum(i, half - 1), 0))
    second = pl.BlockSpec((block, 2 * local), lambda i, core: (jnp.maximum(i - half, 0), 0))
    grid_spec = pltpu.PrefetchScalarGridSpec(
        num_scalar_prefetch=1,
        grid=(steps,),
        in_specs=[lhs(0), lhs(0), lhs(steps), lhs(0)] + [rhs] * 4,
        out_specs=[first, second, first, second],
    )
    return pl.pallas_call(
        functools.partial(weight_grad_kernel, half),
        grid_spec=grid_spec,
        out_shape=(out, out, out, out),
        compiler_params=params(48),
        cost_estimate=small_cost,
        name="weight_grads",
    )(core, nq, nkv, nkv, cot, gq, gk, gv, att)


def assemble_kernel(half, local, a_slot, b_slot, a_lo, a_hi, b_lo, b_hi, gwq, gwk, gwv, gwo):
    r = pl.program_id(0)

    @pl.when(a_slot[r] < half)
    def _():
        gwq[...] = a_lo[:, 0:local].astype(f32)
        gwk[...] = a_lo[:, local : 2 * local].astype(f32)

    @pl.when(a_slot[r] >= half)
    def _():
        gwq[...] = a_hi[:, 0:local].astype(f32)
        gwk[...] = a_hi[:, local : 2 * local].astype(f32)

    @pl.when(b_slot[r] < half)
    def _():
        gwv[...] = b_lo[:, 0:local].astype(f32)
        gwo[...] = jnp.transpose(b_lo[:, local : 2 * local].astype(f32))

    @pl.when(b_slot[r] >= half)
    def _():
        gwv[...] = b_hi[:, 0:local].astype(f32)
        gwo[...] = jnp.transpose(b_hi[:, local : 2 * local].astype(f32))


def assemble(a_slot, b_slot, a_lo, a_hi, b_lo, b_hi, pieces):
    half = pieces // 2
    piece = a_lo.shape[0] // half
    local = a_lo.shape[1] // 2
    width = pieces * piece
    low = lambda pick: pl.BlockSpec(
        (piece, 2 * local), lambda i, a, b: (jnp.minimum((a, b)[pick][i], half - 1), 0)
    )
    high = lambda pick: pl.BlockSpec(
        (piece, 2 * local), lambda i, a, b: (jnp.maximum((a, b)[pick][i] - half, 0), 0)
    )
    rowed = pl.BlockSpec((piece, local), lambda i, a, b: (i, 0))
    tall = jax.ShapeDtypeStruct((width, local), f32)
    grid_spec = pltpu.PrefetchScalarGridSpec(
        num_scalar_prefetch=2,
        grid=(pieces,),
        in_specs=[low(0), high(0), low(1), high(1)],
        out_specs=[rowed, rowed, rowed, pl.BlockSpec((local, piece), lambda i, a, b: (0, i))],
    )
    return pl.pallas_call(
        functools.partial(assemble_kernel, half, local),
        grid_spec=grid_spec,
        out_shape=(tall, tall, tall, jax.ShapeDtypeStruct((local, width), f32)),
        compiler_params=params(32),
        name="assemble",
    )(a_slot, b_slot, a_lo, a_hi, b_lo, b_hi)


def flipped(x, axis, bit, sender=None):
    count = lax.axis_size(axis)
    sends = [i for i in range(count) if sender is None or bool(i & bit) == sender]
    return lax.ppermute(x, axis, [(i, i ^ bit) for i in sends])


def top(bit):
    return 2 * bit == lax.axis_size("seq")


def bits_of(count):
    bits = []
    while (1 << len(bits)) < count:
        bits.append(1 << len(bits))
    return bits


def slot_order(bits):
    order = [0]
    for bit in bits:
        order = order + [m | bit for m in order]
    return order


def collect(block, bits):
    held = {0: block}
    for bit in bits:
        sender = False if top(bit) else None
        held.update({m | bit: flipped(x, "seq", bit, sender) for m, x in held.items()})
    return held


def summed(a, b):
    return (a.astype(f32) + b.astype(f32)).astype(bf16)


def disperse(low, high, bits):
    terms = [low, flipped(high, "seq", bits[-1], True if top(bits[-1]) else None)]
    half = low.shape[0] // 2
    for bit in reversed(bits[:-1]):
        total = functools.reduce(lambda a, b: a + b, [t[half : 2 * half].astype(f32) for t in terms])
        terms.append(flipped(total.astype(bf16), "seq", bit, True if top(bit) else None))
        half = half // 2
    return terms


def merge_kernel(count, blocks, sides, *refs):
    step = pl.program_id(0)
    ins, outs = refs[: 2 * count], refs[2 * count :]

    @pl.when(step < blocks)
    def _():
        for i in range(count):
            outs[2 * i][...] = summed(ins[2 * i][...], ins[2 * i + 1][...])

    @pl.when(step >= blocks)
    def _():
        for i in range(count):
            outs[2 * i + 1][...] = summed(ins[2 * i][...], ins[2 * i + 1][...])


def reduce_level(pairs, bits, rank, midway=None):
    sides = jnp.stack([(rank & bit) // bit for bit in bits]).astype(jnp.int32)
    blocks = 2
    in_specs, out_specs, out_shape = [], [], []
    for at, (own, _) in enumerate(pairs):
        half, cols = own.shape[0] // 2, own.shape[1]
        block = half // blocks

        def pick(i, sides, at=at):
            side = sides[at]
            return (jnp.where(i < blocks, (1 - side) * blocks + i, side * blocks + i - blocks), 0)

        in_specs += [pl.BlockSpec((block, cols), pick)] * 2
        out_specs.append(pl.BlockSpec((block, cols), lambda i, sides: (jnp.minimum(i, blocks - 1), 0)))
        out_specs.append(pl.BlockSpec((block, cols), lambda i, sides: (jnp.maximum(i - blocks, 0), 0)))
        out_shape += [jax.ShapeDtypeStruct((half, cols), bf16)] * 2
    outs = pl.pallas_call(
        functools.partial(merge_kernel, len(pairs), blocks),
        grid_spec=pltpu.PrefetchScalarGridSpec(
            num_scalar_prefetch=1, grid=(2 * blocks,), in_specs=in_specs, out_specs=out_specs
        ),
        out_shape=out_shape,
        compiler_params=params(32),
        cost_estimate=small_cost,
        name="merge",
    )(sides, *[x for pair in pairs for x in pair])
    pairs = []
    for i, bit in enumerate(bits):
        send = outs[2 * i] if midway is None else after(outs[2 * i], midway)
        pairs.append((outs[2 * i + 1], flipped(send, "seq", bit)))
    return pairs


def widen_kernel(x, out):
    out[...] = x[...].astype(f32)


def widened(x):
    rows, cols = x.shape
    spec = pl.BlockSpec((min(512, rows), cols), lambda i: (i, 0))
    return pl.pallas_call(
        widen_kernel,
        grid=(rows // min(512, rows),),
        out_shape=jax.ShapeDtypeStruct(x.shape, f32),
        in_specs=[spec],
        out_specs=spec,
        compiler_params=params(48),
        name="widen",
    )(x)


def spread(piece, bits):
    held = piece
    for bit in bits[:-1]:
        held = jnp.concatenate([held, flipped(held, "seq", bit)], axis=0)
    return held, flipped(held, "seq", bits[-1])


def piece_slots(bits, rank, count):
    order = slot_order(bits[::-1])
    table = [0] * count
    for slot, m in enumerate(order):
        table[m] = slot
    owners = []
    for r in range(count):
        owner = 0
        for at, bit in enumerate(bits):
            if (r >> (len(bits) - 1 - at)) & 1:
                owner |= bit
        owners.append(owner)
    return jnp.take(jnp.array(table, jnp.int32), jnp.array(owners, jnp.int32) ^ rank)


def ring(x, axis):
    count = lax.axis_size(axis)
    from_below, from_above = [], []
    up = down = x
    for k in range(1, count):
        up = lax.ppermute(up, axis, [(i, i + 1) for i in range(k - 1, count - 1)])
        down = lax.ppermute(down, axis, [(i, i - 1) for i in range(1, count - k + 1)])
        from_below.append(up)
        from_above.append(down)
    return from_below + from_above


def after(x, *earlier):
    anywhere = pl.BlockSpec(memory_space=pl.ANY)
    return pl.pallas_call(
        lambda *refs: None,
        out_shape=jax.ShapeDtypeStruct(x.shape, x.dtype),
        in_specs=[anywhere] * (1 + len(earlier)),
        out_specs=anywhere,
        input_output_aliases={0: 0},
        name="after",
    )(x, *earlier)


def small_sum(x, midway):
    x = x.astype(bf16)
    for axis in ("seq", "head"):
        if axis == "head":
            x = after(x, midway)
        bits = bits_of(lax.axis_size(axis))
        for bit in bits[1:] + bits[:1]:
            x = summed(x, flipped(x, axis, bit))
    return x.astype(f32)


def body(
    histories,
    norm_gains,
    mix_in,
    mix_out,
    mix_bias,
    w_query,
    w_key,
    w_value,
    w_out,
    w_up,
    w_down,
    cotangent,
    doc_ids,
    positions,
):
    seq_count = lax.axis_size("seq")
    rank = lax.axis_index("seq")
    block_rows = positions.shape[0]
    hist_count, tok_rows, width = histories.shape
    count = norm_gains.shape[0]
    units = mix_in.shape[1]
    mixes = mix_out.shape[1]

    def gather(x):
        return lax.all_gather(x, "head", axis=0, tiled=True)

    def scatter(x):
        return lax.psum_scatter(x, "head", scatter_dimension=0, tiled=True)

    tables = rope_lanes(positions)
    place = rank * block_rows + jnp.arange(block_rows, dtype=jnp.int32)
    first = place - positions
    span = jnp.concatenate([first[None], place[None], jnp.zeros((6, block_rows), jnp.int32)], axis=0)
    info = jnp.stack([rank.astype(jnp.int32), jnp.max(first)])
    bits = bits_of(seq_count)
    key_bits = bits[1:] + bits[:1]
    value_bits = bits[1:][::-1] + bits[:1]
    key_order = slot_order(key_bits)
    value_order = slot_order(value_bits)
    half = seq_count // 2
    order = key_order[half:] + key_order[:half]
    offsets = jnp.array(order, jnp.int32) ^ rank
    key_at = jnp.array([key_order.index(m) for m in order], jnp.int32)
    value_at = jnp.array([value_order.index(m) for m in order], jnp.int32)
    same, down, up = tables
    core = (rank & 1)[None].astype(jnp.int32)
    cot_pieces = [cotangent] + ring(cotangent, "head")
    n3, nkv, nq, streams, coef, mix_pre = mix_forward(
        histories, norm_gains, mix_in, mix_out, mix_bias[None, :]
    )
    n3_pieces = [n3] + ring(n3, "head")
    nkv_full = gather(after(nkv, *n3_pieces[1:], *cot_pieces[1:]))
    nq_full = gather(nq)
    act, ff_grad, gw_up, gw_down, cot_full = feed_forward(
        lax.axis_index("head")[None], n3_pieces, cot_pieces, w_up, w_down
    )
    gw_up, gw_down = lax.psum((gw_up, gw_down), "seq")
    key, value = project(
        key_value_kernel, nkv_full, (w_key, w_value), (after(same, act), down, up), 2, "project_kv"
    )
    (query,) = project(query_kernel, nq_full, (w_query,), tables, 1, "project_q")
    keys = collect(key, key_bits)
    values = collect(value, value_bits)
    keys, values = [keys[m] for m in order], [values[m] for m in order]
    do = dot_nt(cot_full, w_out).astype(bf16)
    attended, lse = attend(query, keys, values, info, offsets, after(span, do))
    gq, gk_hi, gk_lo, gv_hi, gv_lo = attend_back(
        query,
        keys,
        values,
        do,
        attended,
        lse,
        info,
        offsets,
        key_at,
        value_at,
        span,
        tables,
    )
    gnq = scatter(dot_nt(gq, w_query).astype(bf16))
    ff_out, gn3_part = feed_forward_sums(after(act, gq), ff_grad, w_up, w_down)
    gn3 = scatter(gn3_part)
    branch_part = (ff_out + dot(attended, w_out)).astype(bf16)
    branch = scatter(branch_part)
    layer_out = (streams[3] + branch.astype(f32)).astype(bf16)
    gk, gv, gnkv_part = key_value_back(
        disperse(gk_lo, gk_hi, key_bits),
        disperse(gv_lo, gv_hi, value_bits),
        w_key,
        w_value,
        (after(same, gn3_part, branch_part), down, up),
    )
    gnkv = scatter(gnkv_part)
    send_a, own_a, send_b, own_b = weight_grads(
        core, nq_full, nkv_full, cot_full, gq, gk, after(gv, gw_up, gw_down), attended
    )
    pairs = [(own_a, flipped(send_a, "seq", 1)), (own_b, flipped(send_b, "seq", 1))]
    a_bits = bits[1:]
    b_bits = bits[1:][::-1]
    gw_up, gw_down = widened(gw_up), widened(gw_down)
    for level in range(len(a_bits)):
        last = level == len(a_bits) - 1
        pairs = reduce_level(pairs, (a_bits[level], b_bits[level]), rank, gw_up if last else None)
    piece_a, piece_b = summed(*pairs[0]), summed(*pairs[1])
    a_lo, a_hi = spread(piece_a, a_bits[::-1] + bits[:1])
    b_lo, b_hi = spread(piece_b, b_bits[::-1] + bits[:1])
    gwq, gwk, gwv, gwo = assemble(
        piece_slots(bits[:1] + a_bits, rank, seq_count),
        piece_slots(bits[:1] + b_bits, rank, seq_count),
        a_lo,
        a_hi,
        b_lo,
        b_hi,
        seq_count,
    )
    ghist, pack = unmix(
        histories, streams, gn3, gnkv, gnq, cotangent, coef, mix_pre, norm_gains, mix_in, mix_out
    )
    pack = small_sum(pack, gw_down)
    return (
        layer_out,
        ghist,
        pack[units : units + count, :width],
        jnp.transpose(pack[:units, :width]),
        pack[:units, width : width + mixes],
        pack[units, width : width + mixes],
        gwq,
        gwk,
        gwv,
        gwo,
        gw_up,
        gw_down,
    )


def solution(mesh):
    return jax.shard_map(
        body,
        mesh=mesh,
        in_specs=(
            P(None, ("seq", "head"), None),
            P(),
            P(),
            P(),
            P(),
            P(None, "head"),
            P(None, "head"),
            P(None, "head"),
            P("head", None),
            P(None, "head"),
            P("head", None),
            P(("seq", "head"), None),
            P(),
            P("seq"),
        ),
        out_specs=(
            P(("seq", "head"), None),
            P(None, ("seq", "head"), None),
            P(),
            P(),
            P(),
            P(),
            P(None, "head"),
            P(None, "head"),
            P(None, "head"),
            P("head", None),
            P(None, "head"),
            P("head", None),
        ),
        check_vma=False,
    )
```
